32 devices in a mesh: track: 8 (over z, y), det: 4 (over x, core).
Axes of the slice: x: 2, y: 2, z: 4, core: 2. Of those that a mesh axis runs over, the one named last changes fastest.
Arguments:
- jac: float32 [4096, 12, 512], P('track', None, 'det'), may hold values from -1.75 to 1.75
- obs: float32 [4096, 512], P('track', 'det'), may hold values from -6 to 6
- match: int32 [4096], P('track'), may hold values from 0 to 4095, as said below
- tile_knot: int32 [4096], P('track'), may hold values from 0 to 127
- tile_frac: float32 [4096], P('track'), may hold values from 0 to 1
Outputs:
- knot_field: float32 [12, 1024], P(None, 'track')
- tie_residual: float32 [4096, 512], P('track', 'det')
The draws below stay inside these ranges and needn't reach their ends.
Inputs may be any that keep to these rules, and one draw needn't show every extreme that they name: match[match[i]] = i and match[i] != i; the tiles of each index of track cross exactly 64 tiles of every index of track, itself included.
All inputs are finite; a program needn't handle non-finite values.
Results may differ from the reference program's by a relative error of at most 0.0001.
Values sent between devices are 32-bit elements; how exact they have to be, the bound alone decides.
No kernel may reach another device: no remote copies, remote signals or barrier semaphores. Data moves between devices by JAX's collectives and lax.ppermute only.
A program may use at most 64 MiB of HBM per device.

```python
import jax
import jax.numpy as jnp
from jax import lax

W = 512
P_SIZE = 12
TILE_DEV = 512
KNOT_DEV = 128
ITERS = 4
TILES = 4096
KNOTS = 1024
PEER = 64
N_TRACK = 8


def draw_match(key, part):
    subkeys = jax.random.split(key, N_TRACK)
    shuffled = jax.vmap(lambda single: jax.random.permutation(single, TILE_DEV))(subkeys).astype(jnp.int32)
    slot_pos = jnp.arange(TILE_DEV, dtype=jnp.int32)
    device_col = jnp.arange(N_TRACK, dtype=jnp.int32)[:, None]
    peer_index = jnp.broadcast_to((slot_pos // PEER)[None, :], (N_TRACK, TILE_DEV))
    within = jnp.broadcast_to((slot_pos % PEER)[None, :], (N_TRACK, TILE_DEV))
    paired = jnp.where(peer_index == device_col, jnp.bitwise_xor(within, 1), within)
    partner_slot = shuffled[peer_index, device_col * PEER + paired]
    partner_value = peer_index * TILE_DEV + partner_slot
    rows_index = jnp.broadcast_to(device_col, (N_TRACK, TILE_DEV))
    table = jnp.zeros((N_TRACK, TILE_DEV), jnp.int32).at[rows_index, shuffled].set(partner_value)
    return table.reshape(-1)


def touch_ends(array, key, low, high):
    longest = array.shape.index(max(array.shape))
    spots = []
    for shift in (0, 1):
        where = [jax.random.randint(jax.random.fold_in(key, axis), (), 0, length) for axis, length in enumerate(array.shape)]
        where[longest] = (where[longest] + shift) % array.shape[longest]
        spots.append(tuple(where))
    return array.at[spots[0]].set(low).at[spots[1]].set(high)


def shard_levels(rng, shape, pieces, smallest, largest):
    def one(dim, shards_of):
        steps = jax.random.uniform(jax.random.fold_in(jax.random.fold_in(rng, 6), dim), (shards_of,), jnp.float32, smallest / len(pieces), largest / len(pieces))
        return jnp.repeat(jnp.exp(steps), shape[dim] // shards_of).reshape((-1,) + (1,) * (len(shape) - dim - 1))

    factor_of = one(*pieces[0])
    for cut in pieces[1:]:
        factor_of = factor_of * one(*cut)
    return factor_of


def scatter_about(key, extent, spread, bound, pieces=(), kind=jnp.bfloat16):
    loudness = shard_levels(key, extent, pieces, -0.22, 0.18) if pieces else 1.0
    array = jax.random.normal(key, extent, jnp.float32) * spread * loudness
    return jnp.minimum(jnp.maximum(array, -bound), bound).astype(kind)


def setup_inputs(seed: int = 0) -> dict:
    key_list = jax.random.split(jax.random.key(seed), 6)
    jac = scatter_about(key_list[0], (TILES, P_SIZE, W), P_SIZE ** -0.5, 1.75, ((0, 8), (2, 4)), jnp.float32)
    obs = scatter_about(key_list[1], (TILES, W), 1.0, 6.0, ((0, 8), (1, 4)), jnp.float32)
    match = draw_match(jax.random.fold_in(key_list[5], 71), 0)
    tile_knot = touch_ends(jax.random.randint(key_list[3], (TILES,), 0, KNOT_DEV), jax.random.fold_in(key_list[3], 1), 0, KNOT_DEV - 1).astype(jnp.int32)
    tile_frac = jnp.clip(1.0 * jax.random.uniform(key_list[4], (TILES,), jnp.float32) ** shard_levels(key_list[4], (TILES,), ((0, 8),), -0.2, 0.2), 0.0, 1.0)
    return {"jac": jac, "obs": obs, "match": match, "tile_knot": tile_knot, "tile_frac": tile_frac}


damping = 1.0


def reference(jac, obs, match, tile_knot, tile_frac):
    highest = lax.Precision.HIGHEST
    params = jac.shape[1]
    tile_count = jac.shape[0]
    owner_track = jnp.arange(tile_count, dtype=jnp.int32) // TILE_DEV
    knot_index = (owner_track * KNOT_DEV + tile_knot).astype(jnp.int32)
    weight_high = tile_frac
    weight_low = 1.0 - tile_frac

    def forward(knot_field):
        padded = jnp.concatenate([knot_field, jnp.zeros((params, 1), jnp.float32)], axis=1)
        interp = padded[:, knot_index] * weight_low + padded[:, knot_index + 1] * weight_high
        predicted = jnp.einsum("ipw,pi->iw", jac, interp, precision=highest)
        return predicted - predicted[match]

    def adjoint(residual_rows):
        partial_value = jnp.einsum("ipw,iw->pi", jac, residual_rows, precision=highest)
        totals = jnp.zeros((params, KNOTS + 1), jnp.float32)
        totals = totals.at[:, knot_index].add(partial_value * weight_low)
        totals = totals.at[:, knot_index + 1].add(partial_value * weight_high)
        return totals[:, :KNOTS]

    misfit = obs - obs[match]
    knot_field = jnp.zeros((params, KNOTS), jnp.float32)
    tie_residual = misfit
    gradient = adjoint(tie_residual)
    direction = gradient
    slope_norm = jnp.sum(gradient * gradient)
    for iteration in range(ITERS):
        change = forward(direction)
        curvature = 0.5 * jnp.sum(change * change) + damping * jnp.sum(direction * direction)
        step_length = slope_norm / curvature
        knot_field = knot_field + step_length * direction
        tie_residual = tie_residual - step_length * change
        gradient = adjoint(tie_residual) - damping * knot_field
        new_norm = jnp.sum(gradient * gradient)
        direction = gradient + (new_norm / slope_norm) * direction
        slope_norm = new_norm
    return knot_field, tie_residual
```

```python
import functools

import jax
import jax.numpy as jnp
from jax import lax
from jax.experimental import pallas as pl
from jax.experimental.pallas import tpu as pltpu
from jax.sharding import PartitionSpec as P

KNOT_DEV = 128
ITERS = 4
LANES = 128
SUB = 8
PAD = 16
VMEM_BYTES = 50 * 2**20


damping = 1.0

SMEM = pl.BlockSpec(memory_space=pltpu.SMEM)
VMEM = pl.BlockSpec(memory_space=pltpu.VMEM)
PARAMS = pltpu.CompilerParams(vmem_limit_bytes=VMEM_BYTES)
HIGHEST = lax.Precision.HIGHEST


def f32(*shape):
    return jax.ShapeDtypeStruct(shape, jnp.float32)


def dot(a, b, dims):
    return lax.dot_general(
        a, b, (dims, ((), ())), precision=HIGHEST, preferred_element_type=jnp.float32
    )


def split3(x):
    first = x.astype(jnp.bfloat16)
    rest = x - first.astype(jnp.float32)
    second = rest.astype(jnp.bfloat16)
    third = (rest - second.astype(jnp.float32)).astype(jnp.bfloat16)
    return first, second, third


def bf16_dot(a, b):
    return jnp.dot(a, b, preferred_element_type=jnp.float32)


def turn(x, shift):
    shift = shift % LANES
    return x if shift == 0 else pltpu.roll(x, shift, 1)


def lane_group(shape, q):
    return lax.broadcasted_iota(jnp.int32, shape, 1) // q


def to_crossing(x, perm, q, store):
    tiles = x.shape[0]
    groups = LANES // q
    across = jnp.concatenate(
        [x[c * LANES : (c + 1) * LANES].T for c in range(tiles // LANES)], axis=1
    )
    moved = sum(bf16_dot(part, perm) for part in reversed(split3(across)))
    group = lane_group((q, LANES), q)
    for c in range(tiles // LANES):
        for b in range(groups):
            block = None
            for h in range(groups):
                piece = turn(moved[h * q : (h + 1) * q, c * LANES : (c + 1) * LANES], (h - b) * q)
                block = piece if block is None else jnp.where(group == h, piece, block)
            store(c * groups + b, block)


def from_crossing(load, perm, q, tiles):
    groups = LANES // q
    group = lane_group((q, LANES), q)
    parts = []
    for c in range(tiles // LANES):
        rows = []
        for h in range(groups):
            block = None
            for b in range(groups):
                piece = turn(load(c * groups + b), (b - h) * q)
                block = piece if block is None else jnp.where(group == b, piece, block)
            rows.append(block)
        parts.append(jnp.concatenate(rows, axis=0).T)
    stacked = jnp.concatenate(parts, axis=0)
    return sum(bf16_dot(perm, part) for part in reversed(split3(stacked)))


def order_kernel(q, me_ref, match_ref, knot_ref, frac_ref, obs_ref, perm_ref, weight_ref, obs_out):
    tiles = obs_ref.shape[0]
    groups = LANES // q
    me = me_ref[0]
    match = match_ref[...]
    slot = lax.broadcasted_iota(jnp.int32, (1, tiles), 1)
    peer = match // tiles
    other = match - peer * tiles
    inner = jnp.where(
        peer == me,
        jnp.minimum(slot, other) + jnp.where(slot > other, tiles, 0),
        jnp.where(peer > me, slot, other),
    )
    key = (peer * (2 * tiles) + inner).astype(jnp.float32)
    key_cols = jnp.broadcast_to(key, (LANES, tiles)).T[:, :1]
    place = jnp.sum(jnp.where(key < key_cols, 1.0, 0.0), axis=1, keepdims=True)
    cols = lax.broadcasted_iota(jnp.int32, (tiles, tiles), 1).astype(jnp.float32)
    perm = jnp.where(place == cols, 1.0, 0.0).astype(jnp.bfloat16)
    perm_ref[...] = perm

    def put(index, block):
        obs_out[index * q : (index + 1) * q, :] = block

    to_crossing(obs_ref[...], perm, q, put)

    row = lax.broadcasted_iota(jnp.int32, (SUB, tiles), 0)
    facts = jnp.where(row == 0, knot_ref[...].astype(jnp.float32), frac_ref[...])
    moved = sum(bf16_dot(part, perm) for part in reversed(split3(facts)))
    group = lane_group((SUB, LANES), q)
    knots = lax.broadcasted_iota(jnp.int32, (KNOT_DEV, LANES), 0).astype(jnp.float32)
    first_row = lax.broadcasted_iota(jnp.int32, (SUB, LANES), 0) == 0
    for c in range(tiles // LANES):
        chunk = moved[:, c * LANES : (c + 1) * LANES]
        for b in range(groups):
            block = None
            for h in range(groups):
                piece = turn(chunk, (h - b) * q)
                block = piece if block is None else jnp.where(group == h, piece, block)
            knot = block[0:1]
            frac = block[1:2]
            lanes = slice((c * groups + b) * LANES, (c * groups + b + 1) * LANES)
            weight_ref[0:KNOT_DEV, lanes] = jnp.where(knots == knot, 1.0 - frac, 0.0) + jnp.where(
                knots == knot + 1.0, frac, 0.0
            )
            edge = jnp.where(knot == KNOT_DEV - 1.0, frac, 0.0)
            weight_ref[KNOT_DEV : KNOT_DEV + SUB, lanes] = jnp.where(first_row, edge, 0.0)


def jac_kernel(q, perm_ref, jac_ref, out_ref):
    def put(index, block):
        out_ref[0, index * q : (index + 1) * q, :] = block

    to_crossing(jac_ref[0], perm_ref[...], q, put)


def crossing_values(me, arrived_ref, out_ref, q):
    out_ref[...] = arrived_ref[...]
    own = arrived_ref[pl.ds(pl.multiple_of(me * q, SUB), q), :]
    lane = lax.broadcasted_iota(jnp.int32, (q, LANES), 1)
    swapped = jnp.where(lane % q < q // 2, turn(own, -(q // 2)), turn(own, q // 2))
    out_ref[pl.ds(pl.multiple_of(me * q, SUB), q), :] = swapped


def difference(me, sent_ref, arrived_ref, out_ref, q):
    crossing_values(me, arrived_ref, out_ref, q)
    out_ref[...] = sent_ref[...] - out_ref[...]


def adjoint_kernel(q, me_ref, sent_ref, arrived_ref, jac_ref, weight_ref, diff_ref, send_ref, parts_ref):
    params, tiles, _ = jac_ref.shape
    difference(me_ref[0], sent_ref, arrived_ref, diff_ref, q)

    def block_sums(b, carry):
        rows = pl.ds(pl.multiple_of(b * q, SUB), q)
        diff = diff_ref[rows, :]
        for p in range(params):
            product = jac_ref[p, rows, :] * diff
            folded = product[0:SUB]
            for step in range(1, q // SUB):
                folded = folded + product[step * SUB : (step + 1) * SUB]
            parts_ref[b, p * SUB : (p + 1) * SUB, :] = folded
        return carry

    blocks = tiles // q
    lax.fori_loop(0, blocks, block_sums, 0)
    spread = None
    for b in range(blocks):
        term = dot(parts_ref[b], weight_ref[:, b * LANES : (b + 1) * LANES], ((1,), (1,)))
        spread = term if spread is None else spread + term
    lane = lax.broadcasted_iota(jnp.int32, (1, LANES), 1)
    send_ref[...] = jnp.zeros(send_ref.shape, jnp.float32)
    spill_row = jnp.zeros((1, LANES), jnp.float32)
    rows = []
    for p in range(params):
        total = jnp.sum(spread[p * SUB : (p + 1) * SUB], axis=0, keepdims=True)
        rows.append(total[:, :KNOT_DEV])
        spill_row = jnp.where(lane == p, total[:, KNOT_DEV : KNOT_DEV + 1], spill_row)
    rows.append(spill_row)
    block = jnp.concatenate(rows, axis=0)
    for d in range(send_ref.shape[0]):
        send_ref[d, 0 : params + 1, :] = block


def field_sums(gathered_ref, n_track, n_det, params, store):
    lane = lax.broadcasted_iota(jnp.int32, (PAD, LANES), 1)
    row = lax.broadcasted_iota(jnp.int32, (PAD, LANES), 0)
    spill = jnp.zeros((PAD, 1), jnp.float32)
    for b in range(n_track):
        total = gathered_ref[b * n_det]
        for d in range(1, n_det):
            total = total + gathered_ref[b * n_det + d]
        field = jnp.where(row < params, total, 0.0)
        field = field + jnp.where(lane == 0, spill, 0.0)
        store(b, field)
        spill = jnp.sum(
            jnp.where((lane == row) & (row < params), total[params : params + 1], 0.0),
            axis=1,
            keepdims=True,
        )


def total_of(x):
    return jnp.sum(jnp.sum(x, axis=0), keepdims=True).reshape(1, 1)


def full_dot(a_ref, b_ref):
    total = a_ref[0] * b_ref[0]
    for b in range(1, a_ref.shape[0]):
        total = total + a_ref[b] * b_ref[b]
    return jnp.sum(total, keepdims=True)


def predict(me, q, direction_ref, jac_ref, weight_ref, interp_ref, sent_ref):
    params, tiles, _ = jac_ref.shape
    n_track = direction_ref.shape[0]
    following = direction_ref[jnp.minimum(me + 1, n_track - 1)][:, 0:1]
    following = jnp.where(me + 1 < n_track, following, 0.0)
    own = direction_ref[me]
    blocks = tiles // q
    for b in range(blocks):
        lanes = slice(b * LANES, (b + 1) * LANES)
        interp_ref[b] = (
            dot(own, weight_ref[0:KNOT_DEV, lanes], ((1,), (0,)))
            + following * weight_ref[KNOT_DEV : KNOT_DEV + 1, lanes]
        )

    def block_values(b, carry):
        rows = pl.ds(pl.multiple_of(b * q, SUB), q)
        interp = interp_ref[b]
        total = jac_ref[0, rows, :] * interp[0:1]
        for p in range(1, params):
            total = total + jac_ref[p, rows, :] * interp[p : p + 1]
        sent_ref[rows, :] = total
        return carry

    lax.fori_loop(0, blocks, block_values, 0)


def first_kernel(
    q, n_det, me_ref, gathered_ref, jac_ref, weight_ref, grad_ref, norm_ref, sent_ref, interp_ref
):
    n_track = grad_ref.shape[0]

    def put(b, field):
        grad_ref[b] = field

    field_sums(gathered_ref, n_track, n_det, jac_ref.shape[0], put)
    norm_ref[...] = jnp.broadcast_to(full_dot(grad_ref, grad_ref), norm_ref.shape)
    predict(me_ref[0], q, grad_ref, jac_ref, weight_ref, interp_ref, sent_ref)


def step_kernel(
    q,
    n_det,
    me_ref,
    gathered_ref,
    jac_ref,
    weight_ref,
    grad_ref,
    direction_ref,
    norm_ref,
    knot_ref,
    residual_ref,
    diff_ref,
    grad_out,
    direction_out,
    norm_out,
    knot_out,
    residual_out,
    sent_ref,
    image_ref,
    interp_ref,
):
    n_track = grad_ref.shape[0]
    me = me_ref[0]

    def put(b, field):
        image_ref[b] = field + damping * direction_ref[b]

    field_sums(gathered_ref, n_track, n_det, jac_ref.shape[0], put)
    norm = norm_ref[0:1, 0:1]
    length = norm / full_dot(direction_ref, image_ref)
    knot_out[...] = knot_ref[...] + length * direction_ref[me]
    residual_out[...] = residual_ref[...] - length * diff_ref[...]
    for b in range(n_track):
        grad_out[b] = grad_ref[b] - length * image_ref[b]
    new_norm = full_dot(grad_out, grad_out)
    norm_out[...] = jnp.broadcast_to(new_norm, norm_out.shape)
    ratio = new_norm / norm
    for b in range(n_track):
        direction_out[b] = grad_out[b] + ratio * direction_ref[b]
    predict(me, q, direction_out, jac_ref, weight_ref, interp_ref, sent_ref)


def last_kernel(q, me_ref, sent_ref, arrived_ref, diff_ref, send_ref):
    difference(me_ref[0], sent_ref, arrived_ref, diff_ref, q)
    diff = diff_ref[...]
    squares = jnp.sum(diff * diff, axis=0, keepdims=True)
    send_ref[...] = jnp.broadcast_to(squares[None], send_ref.shape)


def restore_kernel(q, perm_ref, residual_ref, diff_ref, residual_out, diff_out):
    tiles = residual_ref.shape[0]
    for source, target in ((residual_ref, residual_out), (diff_ref, diff_out)):
        target[...] = from_crossing(
            lambda index: source[index * q : (index + 1) * q, :], perm_ref[...], q, tiles
        )


def finish_kernel(
    me_ref, squares_ref, direction_ref, norm_ref, knot_ref, residual_ref, diff_ref, knot_out, residual_out
):
    params = knot_out.shape[0]
    squares = squares_ref[0, 0:1, :]
    for d in range(1, squares_ref.shape[0]):
        squares = squares + squares_ref[d, 0:1, :]
    curvature = 0.5 * jnp.sum(squares, keepdims=True) + damping * full_dot(
        direction_ref, direction_ref
    )
    length = norm_ref[0:1, 0:1] / curvature
    knot = knot_ref[...] + length * direction_ref[me_ref[0]]
    knot_out[...] = knot[0:params]
    residual_out[...] = residual_ref[...] - length * diff_ref[...]


def call(kernel, outs, ins, scratch=()):
    return pl.pallas_call(
        kernel,
        out_shape=outs,
        in_specs=ins,
        out_specs=jax.tree.map(lambda _: VMEM, outs),
        scratch_shapes=list(scratch),
        compiler_params=PARAMS,
    )


def local(jac, obs, match, tile_knot, tile_frac):
    tiles, params, columns = jac.shape
    n_track = lax.axis_size("track")
    n_det = lax.axis_size("det")
    n_all = n_track * n_det
    q = tiles // n_track
    me = lax.axis_index("track").astype(jnp.int32).reshape(1)

    perm, weights, sent = call(
        functools.partial(order_kernel, q),
        (
            jax.ShapeDtypeStruct((tiles, tiles), jnp.bfloat16),
            f32(KNOT_DEV + SUB, n_track * LANES),
            f32(tiles, columns),
        ),
        [SMEM, VMEM, VMEM, VMEM, VMEM],
    )(me, match[None], tile_knot[None], tile_frac[None], obs)

    def crossing(values):
        return lax.all_to_all(values, "track", split_axis=0, concat_axis=0, tiled=True)

    def everywhere(values):
        return lax.all_to_all(values, ("track", "det"), split_axis=0, concat_axis=0, tiled=True)

    arrived = crossing(sent)
    jac_rows = pl.pallas_call(
        functools.partial(jac_kernel, q),
        grid=(params,),
        out_shape=f32(params, tiles, columns),
        in_specs=[
            pl.BlockSpec((tiles, tiles), lambda p: (0, 0)),
            pl.BlockSpec((1, tiles, columns), lambda p: (p, 0, 0)),
        ],
        out_specs=pl.BlockSpec((1, tiles, columns), lambda p: (p, 0, 0)),
        compiler_params=PARAMS,
    )(perm, jnp.transpose(jac, (1, 0, 2)))

    def adjoint(sent, arrived):
        diff, payload = call(
            functools.partial(adjoint_kernel, q),
            (f32(tiles, columns), f32(n_all, PAD, LANES)),
            [SMEM] + [VMEM] * 4,
            [pltpu.VMEM((n_track, params * SUB, LANES), jnp.float32)],
        )(me, sent, arrived, jac_rows, weights)
        return diff, everywhere(payload)

    field = f32(n_track, PAD, LANES)
    interp = pltpu.VMEM((n_track, PAD, LANES), jnp.float32)
    residual, gathered = adjoint(sent, arrived)
    gradient, slope_norm, sent = call(
        functools.partial(first_kernel, q, n_det),
        (field, f32(SUB, LANES), f32(tiles, columns)),
        [SMEM] + [VMEM] * 3,
        [interp],
    )(me, gathered, jac_rows, weights)
    direction = gradient
    knot_field = jnp.zeros((PAD, KNOT_DEV), jnp.float32)
    for iteration in range(ITERS - 1):
        change, gathered = adjoint(sent, crossing(sent))
        gradient, direction, slope_norm, knot_field, residual, sent = call(
            functools.partial(step_kernel, q, n_det),
            (field, field, f32(SUB, LANES), f32(PAD, KNOT_DEV), f32(tiles, columns), f32(tiles, columns)),
            [SMEM] + [VMEM] * 9,
            [pltpu.VMEM((n_track, PAD, LANES), jnp.float32), interp],
        )(
            me, gathered, jac_rows, weights, gradient, direction, slope_norm, knot_field, residual, change
        )
    change, squares = call(
        functools.partial(last_kernel, q),
        (f32(tiles, columns), f32(n_all, SUB, LANES)),
        [SMEM] + [VMEM] * 2,
    )(me, sent, crossing(sent))
    squares = everywhere(squares)
    residual, change = call(
        functools.partial(restore_kernel, q),
        (f32(tiles, columns), f32(tiles, columns)),
        [VMEM] * 3,
    )(perm, residual, change)
    return call(
        finish_kernel,
        (f32(params, KNOT_DEV), f32(tiles, columns)),
        [SMEM] + [VMEM] * 6,
    )(me, squares, direction, slope_norm, knot_field, residual, change)


def solution(mesh):
    in_specs = (P("track", None, "det"), P("track", "det"), P("track"), P("track"), P("track"))
    out_specs = (P(None, "track"), P("track", "det"))
    return jax.shard_map(local, mesh=mesh, in_specs=in_specs, out_specs=out_specs, check_vma=False)
```

```python
import functools

import jax
import jax.numpy as jnp
from jax import lax
from jax.experimental import pallas as pl
from jax.experimental.pallas import tpu as pltpu
from jax.sharding import PartitionSpec as P

KNOT_DEV = 128
ITERS = 4
LANES = 128
SUB = 8
PAD = 16
VMEM_BYTES = 14 * 2**20


damping = 1.0

SMEM = pl.BlockSpec(memory_space=pltpu.SMEM)
VMEM = pl.BlockSpec(memory_space=pltpu.VMEM)
PARAMS = pltpu.CompilerParams(vmem_limit_bytes=VMEM_BYTES)
HIGHEST = lax.Precision.HIGHEST


def f32(*shape):
    return jax.ShapeDtypeStruct(shape, jnp.float32)


def dot(a, b, dims):
    return lax.dot_general(
        a, b, (dims, ((), ())), precision=HIGHEST, preferred_element_type=jnp.float32
    )


def split3(x):
    first = x.astype(jnp.bfloat16)
    rest = x - first.astype(jnp.float32)
    second = rest.astype(jnp.bfloat16)
    third = (rest - second.astype(jnp.float32)).astype(jnp.bfloat16)
    return first, second, third


def bf16_dot(a, b):
    return jnp.dot(a, b, preferred_element_type=jnp.float32)


def turn(x, shift):
    shift = shift % LANES
    return x if shift == 0 else pltpu.roll(x, shift, 1)


def lane_group(shape, q):
    return lax.broadcasted_iota(jnp.int32, shape, 1) // q


def to_crossing(x, perm, q, store):
    tiles = x.shape[0]
    groups = LANES // q
    across = jnp.concatenate(
        [x[c * LANES : (c + 1) * LANES].T for c in range(tiles // LANES)], axis=1
    )
    moved = sum(bf16_dot(part, perm) for part in reversed(split3(across)))
    group = lane_group((q, LANES), q)
    for c in range(tiles // LANES):
        for b in range(groups):
            block = None
            for h in range(groups):
                piece = turn(moved[h * q : (h + 1) * q, c * LANES : (c + 1) * LANES], (h - b) * q)
                block = piece if block is None else jnp.where(group == h, piece, block)
            store(c * groups + b, block)


def from_crossing(load, perm, q, tiles):
    groups = LANES // q
    group = lane_group((q, LANES), q)
    parts = []
    for c in range(tiles // LANES):
        rows = []
        for h in range(groups):
            block = None
            for b in range(groups):
                piece = turn(load(c * groups + b), (b - h) * q)
                block = piece if block is None else jnp.where(group == b, piece, block)
            rows.append(block)
        parts.append(jnp.concatenate(rows, axis=0).T)
    stacked = jnp.concatenate(parts, axis=0)
    return sum(bf16_dot(perm, part) for part in reversed(split3(stacked)))


def order_kernel(q, me_ref, match_ref, knot_ref, frac_ref, obs_ref, perm_ref, weight_ref, obs_out):
    tiles = obs_ref.shape[0]
    groups = LANES // q
    me = me_ref[0]
    match = match_ref[...]
    slot = lax.broadcasted_iota(jnp.int32, (1, tiles), 1)
    peer = match // tiles
    other = match - peer * tiles
    inner = jnp.where(
        peer == me,
        jnp.minimum(slot, other) + jnp.where(slot > other, tiles, 0),
        jnp.where(peer > me, slot, other),
    )
    key = (peer * (2 * tiles) + inner).astype(jnp.float32)
    key_cols = jnp.broadcast_to(key, (LANES, tiles)).T[:, :1]
    place = jnp.sum(jnp.where(key < key_cols, 1.0, 0.0), axis=1, keepdims=True)
    cols = lax.broadcasted_iota(jnp.int32, (tiles, tiles), 1).astype(jnp.float32)
    perm = jnp.where(place == cols, 1.0, 0.0).astype(jnp.bfloat16)
    perm_ref[...] = perm

    def put(index, block):
        obs_out[index * q : (index + 1) * q, :] = block

    to_crossing(obs_ref[...], perm, q, put)

    row = lax.broadcasted_iota(jnp.int32, (SUB, tiles), 0)
    facts = jnp.where(row == 0, knot_ref[...].astype(jnp.float32), frac_ref[...])
    moved = sum(bf16_dot(part, perm) for part in reversed(split3(facts)))
    group = lane_group((SUB, LANES), q)
    knots = lax.broadcasted_iota(jnp.int32, (KNOT_DEV, LANES), 0).astype(jnp.float32)
    first_row = lax.broadcasted_iota(jnp.int32, (SUB, LANES), 0) == 0
    for c in range(tiles // LANES):
        chunk = moved[:, c * LANES : (c + 1) * LANES]
        for b in range(groups):
            block = None
            for h in range(groups):
                piece = turn(chunk, (h - b) * q)
                block = piece if block is None else jnp.where(group == h, piece, block)
            knot = block[0:1]
            frac = block[1:2]
            lanes = slice((c * groups + b) * LANES, (c * groups + b + 1) * LANES)
            weight_ref[0:KNOT_DEV, lanes] = jnp.where(knots == knot, 1.0 - frac, 0.0) + jnp.where(
                knots == knot + 1.0, frac, 0.0
            )
            edge = jnp.where(knot == KNOT_DEV - 1.0, frac, 0.0)
            weight_ref[KNOT_DEV : KNOT_DEV + SUB, lanes] = jnp.where(first_row, edge, 0.0)


def jac_kernel(q, perm_ref, jac_ref, out_ref):
    def put(index, block):
        out_ref[0, index * q : (index + 1) * q, :] = block

    to_crossing(jac_ref[0], perm_ref[...], q, put)


def crossing_values(me, arrived_ref, out_ref, q):
    out_ref[...] = arrived_ref[...]
    own = arrived_ref[pl.ds(pl.multiple_of(me * q, SUB), q), :]
    lane = lax.broadcasted_iota(jnp.int32, (q, LANES), 1)
    swapped = jnp.where(lane % q < q // 2, turn(own, -(q // 2)), turn(own, q // 2))
    out_ref[pl.ds(pl.multiple_of(me * q, SUB), q), :] = swapped


def difference(me, sent_ref, arrived_ref, out_ref, q):
    crossing_values(me, arrived_ref, out_ref, q)
    out_ref[...] = sent_ref[...] - out_ref[...]


def adjoint_kernel(q, me_ref, sent_ref, arrived_ref, jac_ref, weight_ref, diff_ref, send_ref, parts_ref):
    params, tiles, _ = jac_ref.shape
    difference(me_ref[0], sent_ref, arrived_ref, diff_ref, q)

    def block_sums(b, carry):
        rows = pl.ds(pl.multiple_of(b * q, SUB), q)
        diff = diff_ref[rows, :]
        for p in range(params):
            product = jac_ref[p, rows, :] * diff
            folded = product[0:SUB]
            for step in range(1, q // SUB):
                folded = folded + product[step * SUB : (step + 1) * SUB]
            parts_ref[b, p * SUB : (p + 1) * SUB, :] = folded
        return carry

    blocks = tiles // q
    lax.fori_loop(0, blocks, block_sums, 0)
    spread = None
    for b in range(blocks):
        term = dot(parts_ref[b], weight_ref[:, b * LANES : (b + 1) * LANES], ((1,), (1,)))
        spread = term if spread is None else spread + term
    lane = lax.broadcasted_iota(jnp.int32, (1, LANES), 1)
    send_ref[...] = jnp.zeros(send_ref.shape, jnp.float32)
    spill_row = jnp.zeros((1, LANES), jnp.float32)
    rows = []
    for p in range(params):
        total = jnp.sum(spread[p * SUB : (p + 1) * SUB], axis=0, keepdims=True)
        rows.append(total[:, :KNOT_DEV])
        spill_row = jnp.where(lane == p, total[:, KNOT_DEV : KNOT_DEV + 1], spill_row)
    rows.append(spill_row)
    block = jnp.concatenate(rows, axis=0)
    for d in range(send_ref.shape[0]):
        send_ref[d, 0 : params + 1, :] = block


def field_sums(gathered_ref, n_track, n_det, params, store):
    lane = lax.broadcasted_iota(jnp.int32, (PAD, LANES), 1)
    row = lax.broadcasted_iota(jnp.int32, (PAD, LANES), 0)
    spill = jnp.zeros((PAD, 1), jnp.float32)
    for b in range(n_track):
        total = gathered_ref[b * n_det]
        for d in range(1, n_det):
            total = total + gathered_ref[b * n_det + d]
        field = jnp.where(row < params, total, 0.0)
        field = field + jnp.where(lane == 0, spill, 0.0)
        store(b, field)
        spill = jnp.sum(
            jnp.where((lane == row) & (row < params), total[params : params + 1], 0.0),
            axis=1,
            keepdims=True,
        )


def total_of(x):
    return jnp.sum(jnp.sum(x, axis=0), keepdims=True).reshape(1, 1)


def full_dot(a_ref, b_ref):
    total = a_ref[0] * b_ref[0]
    for b in range(1, a_ref.shape[0]):
        total = total + a_ref[b] * b_ref[b]
    return jnp.sum(total, keepdims=True)


def predict(me, q, direction_ref, jac_ref, weight_ref, interp_ref, sent_ref):
    params, tiles, _ = jac_ref.shape
    n_track = direction_ref.shape[0]
    following = direction_ref[jnp.minimum(me + 1, n_track - 1)][:, 0:1]
    following = jnp.where(me + 1 < n_track, following, 0.0)
    own = direction_ref[me]
    blocks = tiles // q
    for b in range(blocks):
        lanes = slice(b * LANES, (b + 1) * LANES)
        interp_ref[b] = (
            dot(own, weight_ref[0:KNOT_DEV, lanes], ((1,), (0,)))
            + following * weight_ref[KNOT_DEV : KNOT_DEV + 1, lanes]
        )

    def block_values(b, carry):
        rows = pl.ds(pl.multiple_of(b * q, SUB), q)
        interp = interp_ref[b]
        total = jac_ref[0, rows, :] * interp[0:1]
        for p in range(1, params):
            total = total + jac_ref[p, rows, :] * interp[p : p + 1]
        sent_ref[rows, :] = total
        return carry

    lax.fori_loop(0, blocks, block_values, 0)


def first_kernel(
    q, n_det, me_ref, gathered_ref, jac_ref, weight_ref, grad_ref, norm_ref, sent_ref, interp_ref
):
    n_track = grad_ref.shape[0]

    def put(b, field):
        grad_ref[b] = field

    field_sums(gathered_ref, n_track, n_det, jac_ref.shape[0], put)
    norm_ref[...] = jnp.broadcast_to(full_dot(grad_ref, grad_ref), norm_ref.shape)
    predict(me_ref[0], q, grad_ref, jac_ref, weight_ref, interp_ref, sent_ref)


def step_kernel(
    q,
    n_det,
    me_ref,
    gathered_ref,
    jac_ref,
    weight_ref,
    grad_ref,
    direction_ref,
    norm_ref,
    knot_ref,
    residual_ref,
    diff_ref,
    grad_out,
    direction_out,
    norm_out,
    knot_out,
    residual_out,
    sent_ref,
    image_ref,
    interp_ref,
):
    n_track = grad_ref.shape[0]
    me = me_ref[0]

    def put(b, field):
        image_ref[b] = field + damping * direction_ref[b]

    field_sums(gathered_ref, n_track, n_det, jac_ref.shape[0], put)
    norm = norm_ref[0:1, 0:1]
    length = norm / full_dot(direction_ref, image_ref)
    knot_out[...] = knot_ref[...] + length * direction_ref[me]
    residual_out[...] = residual_ref[...] - length * diff_ref[...]
    for b in range(n_track):
        grad_out[b] = grad_ref[b] - length * image_ref[b]
    new_norm = full_dot(grad_out, grad_out)
    norm_out[...] = jnp.broadcast_to(new_norm, norm_out.shape)
    ratio = new_norm / norm
    for b in range(n_track):
        direction_out[b] = grad_out[b] + ratio * direction_ref[b]
    predict(me, q, direction_out, jac_ref, weight_ref, interp_ref, sent_ref)


def last_kernel(q, me_ref, sent_ref, arrived_ref, diff_ref, send_ref):
    difference(me_ref[0], sent_ref, arrived_ref, diff_ref, q)
    diff = diff_ref[...]
    squares = jnp.sum(diff * diff, axis=0, keepdims=True)
    send_ref[...] = jnp.broadcast_to(squares[None], send_ref.shape)


def restore_kernel(q, perm_ref, residual_ref, diff_ref, residual_out, diff_out):
    tiles = residual_ref.shape[0]
    for source, target in ((residual_ref, residual_out), (diff_ref, diff_out)):
        target[...] = from_crossing(
            lambda index: source[index * q : (index + 1) * q, :], perm_ref[...], q, tiles
        )


def finish_kernel(
    me_ref, squares_ref, direction_ref, norm_ref, knot_ref, residual_ref, diff_ref, knot_out, residual_out
):
    params = knot_out.shape[0]
    squares = squares_ref[0, 0:1, :]
    for d in range(1, squares_ref.shape[0]):
        squares = squares + squares_ref[d, 0:1, :]
    curvature = 0.5 * jnp.sum(squares, keepdims=True) + damping * full_dot(
        direction_ref, direction_ref
    )
    length = norm_ref[0:1, 0:1] / curvature
    knot = knot_ref[...] + length * direction_ref[me_ref[0]]
    knot_out[...] = knot[0:params]
    residual_out[...] = residual_ref[...] - length * diff_ref[...]


def call(kernel, outs, ins, scratch=()):
    return pl.pallas_call(
        kernel,
        out_shape=outs,
        in_specs=ins,
        out_specs=jax.tree.map(lambda _: VMEM, outs),
        scratch_shapes=list(scratch),
        compiler_params=PARAMS,
    )


def local(jac, obs, match, tile_knot, tile_frac):
    tiles, params, columns = jac.shape
    n_track = lax.axis_size("track")
    n_det = lax.axis_size("det")
    n_all = n_track * n_det
    q = tiles // n_track
    me = lax.axis_index("track").astype(jnp.int32).reshape(1)

    perm, weights, sent = call(
        functools.partial(order_kernel, q),
        (
            jax.ShapeDtypeStruct((tiles, tiles), jnp.bfloat16),
            f32(KNOT_DEV + SUB, n_track * LANES),
            f32(tiles, columns),
        ),
        [SMEM, VMEM, VMEM, VMEM, VMEM],
    )(me, match[None], tile_knot[None], tile_frac[None], obs)

    def crossing(values):
        return lax.all_to_all(values, "track", split_axis=0, concat_axis=0, tiled=True)

    def everywhere(values):
        return lax.all_to_all(values, ("track", "det"), split_axis=0, concat_axis=0, tiled=True)

    arrived = crossing(sent)
    jac_rows = pl.pallas_call(
        functools.partial(jac_kernel, q),
        grid=(params,),
        out_shape=f32(params, tiles, columns),
        in_specs=[
            pl.BlockSpec((tiles, tiles), lambda p: (0, 0)),
            pl.BlockSpec((1, tiles, columns), lambda p: (p, 0, 0)),
        ],
        out_specs=pl.BlockSpec((1, tiles, columns), lambda p: (p, 0, 0)),
        compiler_params=PARAMS,
    )(perm, jnp.transpose(jac, (1, 0, 2)))

    def adjoint(sent, arrived):
        diff, payload = call(
            functools.partial(adjoint_kernel, q),
            (f32(tiles, columns), f32(1, PAD, LANES)),
            [SMEM] + [VMEM] * 4,
            [pltpu.VMEM((n_track, params * SUB, LANES), jnp.float32)],
        )(me, sent, arrived, jac_rows, weights)
        return diff, lax.all_gather(payload, ("track", "det"), axis=0, tiled=True)

    field = f32(n_track, PAD, LANES)
    interp = pltpu.VMEM((n_track, PAD, LANES), jnp.float32)
    residual, gathered = adjoint(sent, arrived)
    gradient, slope_norm, sent = call(
        functools.partial(first_kernel, q, n_det),
        (field, f32(SUB, LANES), f32(tiles, columns)),
        [SMEM] + [VMEM] * 3,
        [interp],
    )(me, gathered, jac_rows, weights)
    direction = gradient
    knot_field = jnp.zeros((PAD, KNOT_DEV), jnp.float32)
    for iteration in range(ITERS - 1):
        change, gathered = adjoint(sent, crossing(sent))
        gradient, direction, slope_norm, knot_field, residual, sent = call(
            functools.partial(step_kernel, q, n_det),
            (field, field, f32(SUB, LANES), f32(PAD, KNOT_DEV), f32(tiles, columns), f32(tiles, columns)),
            [SMEM] + [VMEM] * 9,
            [pltpu.VMEM((n_track, PAD, LANES), jnp.float32), interp],
        )(
            me, gathered, jac_rows, weights, gradient, direction, slope_norm, knot_field, residual, change
        )
    change, squares = call(
        functools.partial(last_kernel, q),
        (f32(tiles, columns), f32(n_all, SUB, LANES)),
        [SMEM] + [VMEM] * 2,
    )(me, sent, crossing(sent))
    squares = everywhere(squares)
    residual, change = call(
        functools.partial(restore_kernel, q),
        (f32(tiles, columns), f32(tiles, columns)),
        [VMEM] * 3,
    )(perm, residual, change)
    return call(
        finish_kernel,
        (f32(params, KNOT_DEV), f32(tiles, columns)),
        [SMEM] + [VMEM] * 6,
    )(me, squares, direction, slope_norm, knot_field, residual, change)


def solution(mesh):
    in_specs = (P("track", None, "det"), P("track", "det"), P("track"), P("track"), P("track"))
    out_specs = (P(None, "track"), P("track", "det"))
    return jax.shard_map(local, mesh=mesh, in_specs=in_specs, out_specs=out_specs, check_vma=False)
```

```python
import functools
import math

import jax
import jax.numpy as jnp
from jax import lax
from jax.experimental import pallas as pl
from jax.experimental.pallas import tpu as pltpu
from jax.sharding import PartitionSpec as P

KNOT_DEV = 128
ITERS = 4
LANES = 128
SUB = 8
PAD = 16
VMEM_BYTES = 14 * 2**20


damping = 1.0

SMEM = pl.BlockSpec(memory_space=pltpu.SMEM)
VMEM = pl.BlockSpec(memory_space=pltpu.VMEM)
ANY = pl.BlockSpec(memory_space=pl.ANY)
PARAMS = pltpu.CompilerParams(vmem_limit_bytes=VMEM_BYTES)
HIGHEST = lax.Precision.HIGHEST


def f32(*shape):
    return jax.ShapeDtypeStruct(shape, jnp.float32)


def dot(a, b, dims):
    return lax.dot_general(
        a, b, (dims, ((), ())), precision=HIGHEST, preferred_element_type=jnp.float32
    )


def split3(x):
    first = x.astype(jnp.bfloat16)
    rest = x - first.astype(jnp.float32)
    second = rest.astype(jnp.bfloat16)
    third = (rest - second.astype(jnp.float32)).astype(jnp.bfloat16)
    return first, second, third


def bf16_dot(a, b):
    return jnp.dot(a, b, preferred_element_type=jnp.float32)


def turn(x, shift):
    shift = shift % LANES
    return x if shift == 0 else pltpu.roll(x, shift, 1)


def lane_group(shape, q):
    return lax.broadcasted_iota(jnp.int32, shape, 1) // q


def to_crossing(arrays, perm, q, store):
    tiles = arrays[0].shape[0]
    groups = LANES // q
    stacked = []
    for x in arrays:
        across = jnp.concatenate(
            [x[c * LANES : (c + 1) * LANES].T for c in range(tiles // LANES)], axis=1
        )
        stacked.extend(split3(across))
    moved = bf16_dot(jnp.concatenate(stacked, axis=0), perm)
    group = lane_group((q, LANES), q)
    for index in range(len(arrays)):
        third, second, first = (
            moved[(3 * index + part) * LANES : (3 * index + part + 1) * LANES] for part in (2, 1, 0)
        )
        whole = third + second + first
        for c in range(tiles // LANES):
            for b in range(groups):
                block = None
                for h in range(groups):
                    piece = turn(
                        whole[h * q : (h + 1) * q, c * LANES : (c + 1) * LANES], (h - b) * q
                    )
                    block = piece if block is None else jnp.where(group == h, piece, block)
                store(index, c * groups + b, block)


def from_crossing(load, perm, q, tiles):
    groups = LANES // q
    group = lane_group((q, LANES), q)
    parts = []
    for c in range(tiles // LANES):
        rows = []
        for h in range(groups):
            block = None
            for b in range(groups):
                piece = turn(load(c * groups + b), (b - h) * q)
                block = piece if block is None else jnp.where(group == b, piece, block)
            rows.append(block)
        parts.append(jnp.concatenate(rows, axis=0).T)
    stacked = jnp.concatenate(parts, axis=0)
    return sum(bf16_dot(perm, part) for part in reversed(split3(stacked)))


def order_kernel(
    q,
    me_ref,
    match_hbm,
    knot_hbm,
    frac_hbm,
    obs_hbm,
    perm_ref,
    weight_ref,
    obs_out,
    match_ref,
    knot_ref,
    frac_ref,
    obs_ref,
    sems,
):
    tiles = obs_ref.shape[0]
    pairs = ((match_hbm, match_ref), (knot_hbm, knot_ref), (frac_hbm, frac_ref), (obs_hbm, obs_ref))
    copies = [
        pltpu.make_async_copy(source, target, sems.at[index])
        for index, (source, target) in enumerate(pairs)
    ]
    for copy in copies:
        copy.start()
    copies[0].wait()
    groups = LANES // q
    me = me_ref[0]
    match = match_ref[...]
    slot = lax.broadcasted_iota(jnp.int32, (1, tiles), 1)
    peer = match // tiles
    other = match - peer * tiles
    inner = jnp.where(
        peer == me,
        jnp.minimum(slot, other) + jnp.where(slot > other, tiles, 0),
        jnp.where(peer > me, slot, other),
    )
    key = (peer * (2 * tiles) + inner).astype(jnp.float32)
    key_cols = jnp.broadcast_to(key, (LANES, tiles)).T[:, :1]
    place = jnp.sum(jnp.where(key < key_cols, 1.0, 0.0), axis=1, keepdims=True)
    cols = lax.broadcasted_iota(jnp.int32, (tiles, tiles), 1).astype(jnp.float32)
    perm = jnp.where(place == cols, 1.0, 0.0).astype(jnp.bfloat16)
    perm_ref[...] = perm

    def put(_, index, block):
        obs_out[index * q : (index + 1) * q, :] = block

    copies[3].wait()
    to_crossing([obs_ref[...]], perm, q, put)

    copies[1].wait()
    copies[2].wait()
    row = lax.broadcasted_iota(jnp.int32, (SUB, tiles), 0)
    facts = jnp.where(row == 0, knot_ref[...].astype(jnp.float32), frac_ref[...])
    moved = sum(bf16_dot(part, perm) for part in reversed(split3(facts)))
    group = lane_group((SUB, LANES), q)
    knots = lax.broadcasted_iota(jnp.int32, (KNOT_DEV, LANES), 0).astype(jnp.float32)
    first_row = lax.broadcasted_iota(jnp.int32, (SUB, LANES), 0) == 0
    for c in range(tiles // LANES):
        chunk = moved[:, c * LANES : (c + 1) * LANES]
        for b in range(groups):
            block = None
            for h in range(groups):
                piece = turn(chunk, (h - b) * q)
                block = piece if block is None else jnp.where(group == h, piece, block)
            knot = block[0:1]
            frac = block[1:2]
            lanes = slice((c * groups + b) * LANES, (c * groups + b + 1) * LANES)
            weight_ref[0:KNOT_DEV, lanes] = jnp.where(knots == knot, 1.0 - frac, 0.0) + jnp.where(
                knots == knot + 1.0, frac, 0.0
            )
            edge = jnp.where(knot == KNOT_DEV - 1.0, frac, 0.0)
            weight_ref[KNOT_DEV : KNOT_DEV + SUB, lanes] = jnp.where(first_row, edge, 0.0)


def jac_kernel(q, together, perm_ref, jac_hbm, out_ref, jac_ref, sems):
    params = jac_ref.shape[0]
    copies = [
        pltpu.make_async_copy(jac_hbm.at[p], jac_ref.at[p], sems.at[p]) for p in range(params)
    ]
    for copy in copies:
        copy.start()
    for first in range(0, params, together):
        for p in range(first, first + together):
            copies[p].wait()

        def put(index, block_index, block):
            out_ref[first + index, block_index * q : (block_index + 1) * q, :] = block

        to_crossing([jac_ref[p] for p in range(first, first + together)], perm_ref[...], q, put)


def crossing_values(me, arrived_ref, out_ref, q):
    out_ref[...] = arrived_ref[...]
    own = arrived_ref[pl.ds(pl.multiple_of(me * q, SUB), q), :]
    lane = lax.broadcasted_iota(jnp.int32, (q, LANES), 1)
    swapped = jnp.where(lane % q < q // 2, turn(own, -(q // 2)), turn(own, q // 2))
    out_ref[pl.ds(pl.multiple_of(me * q, SUB), q), :] = swapped


def difference(me, sent_ref, arrived_ref, out_ref, q):
    crossing_values(me, arrived_ref, out_ref, q)
    out_ref[...] = sent_ref[...] - out_ref[...]


def adjoint_kernel(q, me_ref, sent_ref, arrived_ref, jac_ref, weight_ref, diff_ref, send_ref, parts_ref):
    params, tiles, _ = jac_ref.shape
    difference(me_ref[0], sent_ref, arrived_ref, diff_ref, q)

    def block_sums(b, carry):
        rows = pl.ds(pl.multiple_of(b * q, SUB), q)
        diff = diff_ref[rows, :]
        for p in range(params):
            product = jac_ref[p, rows, :] * diff
            folded = product[0:SUB]
            for step in range(1, q // SUB):
                folded = folded + product[step * SUB : (step + 1) * SUB]
            parts_ref[b, p * SUB : (p + 1) * SUB, :] = folded
        return carry

    blocks = tiles // q
    lax.fori_loop(0, blocks, block_sums, 0)
    spread = None
    for b in range(blocks):
        term = dot(parts_ref[b], weight_ref[:, b * LANES : (b + 1) * LANES], ((1,), (1,)))
        spread = term if spread is None else spread + term
    lane = lax.broadcasted_iota(jnp.int32, (1, LANES), 1)
    send_ref[...] = jnp.zeros(send_ref.shape, jnp.float32)
    spill_row = jnp.zeros((1, LANES), jnp.float32)
    rows = []
    for p in range(params):
        total = jnp.sum(spread[p * SUB : (p + 1) * SUB], axis=0, keepdims=True)
        rows.append(total[:, :KNOT_DEV])
        spill_row = jnp.where(lane == p, total[:, KNOT_DEV : KNOT_DEV + 1], spill_row)
    rows.append(spill_row)
    block = jnp.concatenate(rows, axis=0)
    for d in range(send_ref.shape[0]):
        send_ref[d, 0 : params + 1, :] = block


def field_sums(gathered_ref, n_track, n_det, params, store):
    lane = lax.broadcasted_iota(jnp.int32, (PAD, LANES), 1)
    row = lax.broadcasted_iota(jnp.int32, (PAD, LANES), 0)
    spill = jnp.zeros((PAD, 1), jnp.float32)
    for b in range(n_track):
        total = gathered_ref[b * n_det]
        for d in range(1, n_det):
            total = total + gathered_ref[b * n_det + d]
        field = jnp.where(row < params, total, 0.0)
        field = field + jnp.where(lane == 0, spill, 0.0)
        store(b, field)
        spill = jnp.sum(
            jnp.where((lane == row) & (row < params), total[params : params + 1], 0.0),
            axis=1,
            keepdims=True,
        )


def total_of(x):
    return jnp.sum(jnp.sum(x, axis=0), keepdims=True).reshape(1, 1)


def full_dot(a_ref, b_ref):
    total = a_ref[0] * b_ref[0]
    for b in range(1, a_ref.shape[0]):
        total = total + a_ref[b] * b_ref[b]
    return jnp.sum(total, keepdims=True)


def predict(me, q, direction_ref, jac_ref, weight_ref, interp_ref, sent_ref):
    params, tiles, _ = jac_ref.shape
    n_track = direction_ref.shape[0]
    following = direction_ref[jnp.minimum(me + 1, n_track - 1)][:, 0:1]
    following = jnp.where(me + 1 < n_track, following, 0.0)
    own = direction_ref[me]
    blocks = tiles // q
    for b in range(blocks):
        lanes = slice(b * LANES, (b + 1) * LANES)
        interp_ref[b] = (
            dot(own, weight_ref[0:KNOT_DEV, lanes], ((1,), (0,)))
            + following * weight_ref[KNOT_DEV : KNOT_DEV + 1, lanes]
        )

    def block_values(b, carry):
        rows = pl.ds(pl.multiple_of(b * q, SUB), q)
        interp = interp_ref[b]
        total = jac_ref[0, rows, :] * interp[0:1]
        for p in range(1, params):
            total = total + jac_ref[p, rows, :] * interp[p : p + 1]
        sent_ref[rows, :] = total
        return carry

    lax.fori_loop(0, blocks, block_values, 0)


def first_kernel(
    q, n_det, me_ref, gathered_ref, jac_ref, weight_ref, grad_ref, norm_ref, sent_ref, interp_ref
):
    n_track = grad_ref.shape[0]

    def put(b, field):
        grad_ref[b] = field

    field_sums(gathered_ref, n_track, n_det, jac_ref.shape[0], put)
    norm_ref[...] = jnp.broadcast_to(full_dot(grad_ref, grad_ref), norm_ref.shape)
    predict(me_ref[0], q, grad_ref, jac_ref, weight_ref, interp_ref, sent_ref)


def step_kernel(
    q,
    n_det,
    me_ref,
    gathered_ref,
    jac_ref,
    weight_ref,
    grad_ref,
    direction_ref,
    norm_ref,
    knot_ref,
    residual_ref,
    diff_ref,
    grad_out,
    direction_out,
    norm_out,
    knot_out,
    residual_out,
    sent_ref,
    image_ref,
    interp_ref,
):
    n_track = grad_ref.shape[0]
    me = me_ref[0]

    def put(b, field):
        image_ref[b] = field + damping * direction_ref[b]

    field_sums(gathered_ref, n_track, n_det, jac_ref.shape[0], put)
    norm = norm_ref[0:1, 0:1]
    length = norm / full_dot(direction_ref, image_ref)
    knot_out[...] = knot_ref[...] + length * direction_ref[me]
    residual_out[...] = residual_ref[...] - length * diff_ref[...]
    for b in range(n_track):
        grad_out[b] = grad_ref[b] - length * image_ref[b]
    new_norm = full_dot(grad_out, grad_out)
    norm_out[...] = jnp.broadcast_to(new_norm, norm_out.shape)
    ratio = new_norm / norm
    for b in range(n_track):
        direction_out[b] = grad_out[b] + ratio * direction_ref[b]
    predict(me, q, direction_out, jac_ref, weight_ref, interp_ref, sent_ref)


def last_kernel(q, me_ref, sent_ref, arrived_ref, diff_ref, send_ref):
    difference(me_ref[0], sent_ref, arrived_ref, diff_ref, q)
    diff = diff_ref[...]
    squares = jnp.sum(diff * diff, axis=0, keepdims=True)
    send_ref[...] = jnp.broadcast_to(squares[None], send_ref.shape)


def restore_kernel(q, perm_ref, residual_ref, diff_ref, residual_out, diff_out):
    tiles = residual_ref.shape[0]
    for source, target in ((residual_ref, residual_out), (diff_ref, diff_out)):
        target[...] = from_crossing(
            lambda index: source[index * q : (index + 1) * q, :], perm_ref[...], q, tiles
        )


def finish_kernel(
    me_ref, squares_ref, direction_ref, norm_ref, knot_ref, residual_ref, diff_ref, knot_out, residual_out
):
    params = knot_out.shape[0]
    squares = squares_ref[0]
    for d in range(1, squares_ref.shape[0]):
        squares = squares + squares_ref[d]
    curvature = 0.5 * jnp.sum(squares, keepdims=True) + damping * full_dot(
        direction_ref, direction_ref
    )
    length = norm_ref[0:1, 0:1] / curvature
    knot = knot_ref[...] + length * direction_ref[me_ref[0]]
    knot_out[...] = knot[0:params]
    residual_out[...] = residual_ref[...] - length * diff_ref[...]


def call(kernel, outs, ins, scratch=()):
    return pl.pallas_call(
        kernel,
        out_shape=outs,
        in_specs=ins,
        out_specs=jax.tree.map(lambda _: VMEM, outs),
        scratch_shapes=list(scratch),
        compiler_params=PARAMS,
    )


def local(jac, obs, match, tile_knot, tile_frac):
    tiles, params, columns = jac.shape
    n_track = lax.axis_size("track")
    n_det = lax.axis_size("det")
    n_all = n_track * n_det
    q = tiles // n_track
    me = lax.axis_index("track").astype(jnp.int32).reshape(1)

    perm, weights, sent = call(
        functools.partial(order_kernel, q),
        (
            jax.ShapeDtypeStruct((tiles, tiles), jnp.bfloat16),
            f32(KNOT_DEV + SUB, n_track * LANES),
            f32(tiles, columns),
        ),
        [SMEM, ANY, ANY, ANY, ANY],
        [
            pltpu.VMEM((1, tiles), jnp.int32),
            pltpu.VMEM((1, tiles), jnp.int32),
            pltpu.VMEM((1, tiles), jnp.float32),
            pltpu.VMEM((tiles, columns), jnp.float32),
            pltpu.SemaphoreType.DMA((4,)),
        ],
    )(me, match[None], tile_knot[None], tile_frac[None], obs)

    def crossing(values):
        return lax.all_to_all(values, "track", split_axis=0, concat_axis=0, tiled=True)

    def everywhere(values):
        return lax.all_to_all(values, ("track", "det"), split_axis=0, concat_axis=0, tiled=True)

    arrived = crossing(sent)
    jac_rows = call(
        functools.partial(jac_kernel, q, math.gcd(params, 3)),
        f32(params, tiles, columns),
        [VMEM, ANY],
        [
            pltpu.VMEM((params, tiles, columns), jnp.float32),
            pltpu.SemaphoreType.DMA((params,)),
        ],
    )(perm, jnp.transpose(jac, (1, 0, 2)))

    def adjoint(sent, arrived):
        diff, payload = call(
            functools.partial(adjoint_kernel, q),
            (f32(tiles, columns), f32(n_all, PAD, LANES)),
            [SMEM] + [VMEM] * 4,
            [pltpu.VMEM((n_track, params * SUB, LANES), jnp.float32)],
        )(me, sent, arrived, jac_rows, weights)
        return diff, everywhere(payload)

    field = f32(n_track, PAD, LANES)
    interp = pltpu.VMEM((n_track, PAD, LANES), jnp.float32)
    residual, gathered = adjoint(sent, arrived)
    gradient, slope_norm, sent = call(
        functools.partial(first_kernel, q, n_det),
        (field, f32(SUB, LANES), f32(tiles, columns)),
        [SMEM] + [VMEM] * 3,
        [interp],
    )(me, gathered, jac_rows, weights)
    direction = gradient
    knot_field = jnp.zeros((PAD, KNOT_DEV), jnp.float32)
    for iteration in range(ITERS - 1):
        change, gathered = adjoint(sent, crossing(sent))
        gradient, direction, slope_norm, knot_field, residual, sent = call(
            functools.partial(step_kernel, q, n_det),
            (field, field, f32(SUB, LANES), f32(PAD, KNOT_DEV), f32(tiles, columns), f32(tiles, columns)),
            [SMEM] + [VMEM] * 9,
            [pltpu.VMEM((n_track, PAD, LANES), jnp.float32), interp],
        )(
            me, gathered, jac_rows, weights, gradient, direction, slope_norm, knot_field, residual, change
        )
    change, squares = call(
        functools.partial(last_kernel, q),
        (f32(tiles, columns), f32(n_all, 1, LANES)),
        [SMEM] + [VMEM] * 2,
    )(me, sent, crossing(sent))
    squares = everywhere(squares)
    residual, change = call(
        functools.partial(restore_kernel, q),
        (f32(tiles, columns), f32(tiles, columns)),
        [VMEM] * 3,
    )(perm, residual, change)
    return call(
        finish_kernel,
        (f32(params, KNOT_DEV), f32(tiles, columns)),
        [SMEM] + [VMEM] * 6,
    )(me, squares, direction, slope_norm, knot_field, residual, change)


def solution(mesh):
    in_specs = (P("track", None, "det"), P("track", "det"), P("track"), P("track"), P("track"))
    out_specs = (P(None, "track"), P("track", "det"))
    return jax.shard_map(local, mesh=mesh, in_specs=in_specs, out_specs=out_specs, check_vma=False)
```

```python
import functools
import math

import jax
import jax.numpy as jnp
from jax import lax
from jax.experimental import pallas as pl
from jax.experimental.pallas import tpu as pltpu
from jax.sharding import PartitionSpec as P

KNOT_DEV = 128
ITERS = 4
LANES = 128
SUB = 8
PAD = 16
VMEM_BYTES = 14 * 2**20


damping = 1.0

SMEM = pl.BlockSpec(memory_space=pltpu.SMEM)
VMEM = pl.BlockSpec(memory_space=pltpu.VMEM)
ANY = pl.BlockSpec(memory_space=pl.ANY)
PARAMS = pltpu.CompilerParams(vmem_limit_bytes=VMEM_BYTES)
HIGHEST = lax.Precision.HIGHEST


def kept(shape, dtype=jnp.float32):
    return pltpu.VMEM(shape, dtype)


def from_hbm(x):
    return pltpu.with_memory_space_constraint(x, pltpu.HBM)


def f32(*shape):
    return jax.ShapeDtypeStruct(shape, jnp.float32)


def dot(a, b, dims):
    return lax.dot_general(
        a, b, (dims, ((), ())), precision=HIGHEST, preferred_element_type=jnp.float32
    )


def split3(x):
    first = x.astype(jnp.bfloat16)
    rest = x - first.astype(jnp.float32)
    second = rest.astype(jnp.bfloat16)
    third = (rest - second.astype(jnp.float32)).astype(jnp.bfloat16)
    return first, second, third


def bf16_dot(a, b):
    return jnp.dot(a, b, preferred_element_type=jnp.float32)


def turn(x, shift):
    shift = shift % LANES
    return x if shift == 0 else pltpu.roll(x, shift, 1)


def lane_group(shape, q):
    return lax.broadcasted_iota(jnp.int32, shape, 1) // q


def to_crossing(arrays, perm, q, store):
    tiles = arrays[0].shape[0]
    groups = LANES // q
    stacked = []
    for x in arrays:
        across = jnp.concatenate(
            [x[c * LANES : (c + 1) * LANES].T for c in range(tiles // LANES)], axis=1
        )
        stacked.extend(split3(across))
    moved = bf16_dot(jnp.concatenate(stacked, axis=0), perm)
    group = lane_group((q, LANES), q)
    for index in range(len(arrays)):
        third, second, first = (
            moved[(3 * index + part) * LANES : (3 * index + part + 1) * LANES] for part in (2, 1, 0)
        )
        whole = third + second + first
        for c in range(tiles // LANES):
            for b in range(groups):
                block = None
                for h in range(groups):
                    piece = turn(
                        whole[h * q : (h + 1) * q, c * LANES : (c + 1) * LANES], (h - b) * q
                    )
                    block = piece if block is None else jnp.where(group == h, piece, block)
                store(index, c * groups + b, block)


def from_crossing(load, perm, q, tiles):
    groups = LANES // q
    group = lane_group((q, LANES), q)
    parts = []
    for c in range(tiles // LANES):
        rows = []
        for h in range(groups):
            block = None
            for b in range(groups):
                piece = turn(load(c * groups + b), (b - h) * q)
                block = piece if block is None else jnp.where(group == b, piece, block)
            rows.append(block)
        parts.append(jnp.concatenate(rows, axis=0).T)
    stacked = jnp.concatenate(parts, axis=0)
    return sum(bf16_dot(perm, part) for part in reversed(split3(stacked)))


def order_kernel(
    q,
    me_ref,
    match_hbm,
    knot_hbm,
    frac_hbm,
    obs_hbm,
    perm_ref,
    weight_ref,
    obs_out,
    match_ref,
    knot_ref,
    frac_ref,
    obs_ref,
    sems,
):
    tiles = obs_ref.shape[0]
    pairs = ((match_hbm, match_ref), (knot_hbm, knot_ref), (frac_hbm, frac_ref), (obs_hbm, obs_ref))
    copies = [
        pltpu.make_async_copy(source, target, sems.at[index])
        for index, (source, target) in enumerate(pairs)
    ]
    for copy in copies:
        copy.start()
    copies[0].wait()
    groups = LANES // q
    me = me_ref[0]
    match = match_ref[...]
    slot = lax.broadcasted_iota(jnp.int32, (1, tiles), 1)
    peer = match // tiles
    other = match - peer * tiles
    inner = jnp.where(
        peer == me,
        jnp.minimum(slot, other) + jnp.where(slot > other, tiles, 0),
        jnp.where(peer > me, slot, other),
    )
    key = (peer * (2 * tiles) + inner).astype(jnp.float32)
    key_cols = jnp.broadcast_to(key, (LANES, tiles)).T[:, :1]
    place = jnp.sum(jnp.where(key < key_cols, 1.0, 0.0), axis=1, keepdims=True)
    cols = lax.broadcasted_iota(jnp.int32, (tiles, tiles), 1).astype(jnp.float32)
    perm = jnp.where(place == cols, 1.0, 0.0).astype(jnp.bfloat16)
    perm_ref[...] = perm

    def put(_, index, block):
        obs_out[index * q : (index + 1) * q, :] = block

    copies[3].wait()
    to_crossing([obs_ref[...]], perm, q, put)

    copies[1].wait()
    copies[2].wait()
    row = lax.broadcasted_iota(jnp.int32, (SUB, tiles), 0)
    facts = jnp.where(row == 0, knot_ref[...].astype(jnp.float32), frac_ref[...])
    moved = sum(bf16_dot(part, perm) for part in reversed(split3(facts)))
    group = lane_group((SUB, LANES), q)
    knots = lax.broadcasted_iota(jnp.int32, (KNOT_DEV, LANES), 0).astype(jnp.float32)
    first_row = lax.broadcasted_iota(jnp.int32, (SUB, LANES), 0) == 0
    for c in range(tiles // LANES):
        chunk = moved[:, c * LANES : (c + 1) * LANES]
        for b in range(groups):
            block = None
            for h in range(groups):
                piece = turn(chunk, (h - b) * q)
                block = piece if block is None else jnp.where(group == h, piece, block)
            knot = block[0:1]
            frac = block[1:2]
            lanes = slice((c * groups + b) * LANES, (c * groups + b + 1) * LANES)
            weight_ref[0:KNOT_DEV, lanes] = jnp.where(knots == knot, 1.0 - frac, 0.0) + jnp.where(
                knots == knot + 1.0, frac, 0.0
            )
            edge = jnp.where(knot == KNOT_DEV - 1.0, frac, 0.0)
            weight_ref[KNOT_DEV : KNOT_DEV + SUB, lanes] = jnp.where(first_row, edge, 0.0)


def jac_kernel(q, together, perm_ref, jac_hbm, out_ref, jac_ref, sems):
    params = jac_ref.shape[0]
    copies = [
        pltpu.make_async_copy(jac_hbm.at[p], jac_ref.at[p], sems.at[p]) for p in range(params)
    ]
    for copy in copies:
        copy.start()
    for first in range(0, params, together):
        for p in range(first, first + together):
            copies[p].wait()

        def put(index, block_index, block):
            out_ref[first + index, block_index * q : (block_index + 1) * q, :] = block

        to_crossing([jac_ref[p] for p in range(first, first + together)], perm_ref[...], q, put)


def crossing_values(me, arrived_ref, out_ref, q):
    out_ref[...] = arrived_ref[...]
    own = arrived_ref[pl.ds(pl.multiple_of(me * q, SUB), q), :]
    lane = lax.broadcasted_iota(jnp.int32, (q, LANES), 1)
    swapped = jnp.where(lane % q < q // 2, turn(own, -(q // 2)), turn(own, q // 2))
    out_ref[pl.ds(pl.multiple_of(me * q, SUB), q), :] = swapped


def difference(me, sent_ref, arrived_ref, out_ref, q):
    crossing_values(me, arrived_ref, out_ref, q)
    out_ref[...] = sent_ref[...] - out_ref[...]


def adjoint_kernel(q, me_ref, sent_ref, arrived_ref, jac_ref, weight_ref, diff_ref, send_ref, parts_ref):
    params, tiles, _ = jac_ref.shape
    difference(me_ref[0], sent_ref, arrived_ref, diff_ref, q)

    def block_sums(b, carry):
        rows = pl.ds(pl.multiple_of(b * q, SUB), q)
        diff = diff_ref[rows, :]
        for p in range(params):
            product = jac_ref[p, rows, :] * diff
            folded = product[0:SUB]
            for step in range(1, q // SUB):
                folded = folded + product[step * SUB : (step + 1) * SUB]
            parts_ref[b, p * SUB : (p + 1) * SUB, :] = folded
        return carry

    blocks = tiles // q
    lax.fori_loop(0, blocks, block_sums, 0)
    spread = None
    for b in range(blocks):
        term = dot(parts_ref[b], weight_ref[:, b * LANES : (b + 1) * LANES], ((1,), (1,)))
        spread = term if spread is None else spread + term
    lane = lax.broadcasted_iota(jnp.int32, (1, LANES), 1)
    send_ref[...] = jnp.zeros(send_ref.shape, jnp.float32)
    spill_row = jnp.zeros((1, LANES), jnp.float32)
    rows = []
    for p in range(params):
        total = jnp.sum(spread[p * SUB : (p + 1) * SUB], axis=0, keepdims=True)
        rows.append(total[:, :KNOT_DEV])
        spill_row = jnp.where(lane == p, total[:, KNOT_DEV : KNOT_DEV + 1], spill_row)
    rows.append(spill_row)
    block = jnp.concatenate(rows, axis=0)
    for d in range(send_ref.shape[0]):
        send_ref[d, 0 : params + 1, :] = block


def field_sums(gathered_ref, n_track, n_det, params, store):
    lane = lax.broadcasted_iota(jnp.int32, (PAD, LANES), 1)
    row = lax.broadcasted_iota(jnp.int32, (PAD, LANES), 0)
    spill = jnp.zeros((PAD, 1), jnp.float32)
    for b in range(n_track):
        total = gathered_ref[b * n_det]
        for d in range(1, n_det):
            total = total + gathered_ref[b * n_det + d]
        field = jnp.where(row < params, total, 0.0)
        field = field + jnp.where(lane == 0, spill, 0.0)
        store(b, field)
        spill = jnp.sum(
            jnp.where((lane == row) & (row < params), total[params : params + 1], 0.0),
            axis=1,
            keepdims=True,
        )


def total_of(x):
    return jnp.sum(jnp.sum(x, axis=0), keepdims=True).reshape(1, 1)


def full_dot(a_ref, b_ref):
    total = a_ref[0] * b_ref[0]
    for b in range(1, a_ref.shape[0]):
        total = total + a_ref[b] * b_ref[b]
    return jnp.sum(total, keepdims=True)


def predict(me, q, direction_ref, jac_ref, weight_ref, interp_ref, sent_ref):
    params, tiles, _ = jac_ref.shape
    n_track = direction_ref.shape[0]
    following = direction_ref[jnp.minimum(me + 1, n_track - 1)][:, 0:1]
    following = jnp.where(me + 1 < n_track, following, 0.0)
    own = direction_ref[me]
    blocks = tiles // q
    for b in range(blocks):
        lanes = slice(b * LANES, (b + 1) * LANES)
        interp_ref[b] = (
            dot(own, weight_ref[0:KNOT_DEV, lanes], ((1,), (0,)))
            + following * weight_ref[KNOT_DEV : KNOT_DEV + 1, lanes]
        )

    def block_values(b, carry):
        rows = pl.ds(pl.multiple_of(b * q, SUB), q)
        interp = interp_ref[b]
        total = jac_ref[0, rows, :] * interp[0:1]
        for p in range(1, params):
            total = total + jac_ref[p, rows, :] * interp[p : p + 1]
        sent_ref[rows, :] = total
        return carry

    lax.fori_loop(0, blocks, block_values, 0)


def first_kernel(
    q, n_det, me_ref, gathered_ref, jac_ref, weight_ref, grad_ref, norm_ref, sent_ref, interp_ref
):
    n_track = grad_ref.shape[0]

    def put(b, field):
        grad_ref[b] = field

    field_sums(gathered_ref, n_track, n_det, jac_ref.shape[0], put)
    norm_ref[...] = jnp.broadcast_to(full_dot(grad_ref, grad_ref), norm_ref.shape)
    predict(me_ref[0], q, grad_ref, jac_ref, weight_ref, interp_ref, sent_ref)


def step_kernel(
    q,
    n_det,
    me_ref,
    gathered_ref,
    jac_ref,
    weight_ref,
    grad_ref,
    direction_ref,
    norm_ref,
    knot_ref,
    residual_ref,
    diff_ref,
    grad_out,
    direction_out,
    norm_out,
    knot_out,
    residual_out,
    sent_ref,
    image_ref,
    interp_ref,
):
    n_track = grad_ref.shape[0]
    me = me_ref[0]

    def put(b, field):
        image_ref[b] = field + damping * direction_ref[b]

    field_sums(gathered_ref, n_track, n_det, jac_ref.shape[0], put)
    norm = norm_ref[0:1, 0:1]
    length = norm / full_dot(direction_ref, image_ref)
    knot_out[...] = knot_ref[...] + length * direction_ref[me]
    residual_out[...] = residual_ref[...] - length * diff_ref[...]
    for b in range(n_track):
        grad_out[b] = grad_ref[b] - length * image_ref[b]
    new_norm = full_dot(grad_out, grad_out)
    norm_out[...] = jnp.broadcast_to(new_norm, norm_out.shape)
    ratio = new_norm / norm
    for b in range(n_track):
        direction_out[b] = grad_out[b] + ratio * direction_ref[b]
    predict(me, q, direction_out, jac_ref, weight_ref, interp_ref, sent_ref)


def last_kernel(q, me_ref, sent_ref, arrived_ref, diff_ref, send_ref):
    difference(me_ref[0], sent_ref, arrived_ref, diff_ref, q)
    diff = diff_ref[...]
    squares = jnp.sum(diff * diff, axis=0, keepdims=True)
    send_ref[...] = jnp.broadcast_to(squares[None], send_ref.shape)


def restore_kernel(q, perm_ref, residual_ref, diff_ref, residual_out, diff_out):
    tiles = residual_ref.shape[0]
    for source, target in ((residual_ref, residual_out), (diff_ref, diff_out)):
        target[...] = from_crossing(
            lambda index: source[index * q : (index + 1) * q, :], perm_ref[...], q, tiles
        )


def finish_kernel(
    me_ref, squares_ref, direction_ref, norm_ref, knot_ref, residual_ref, diff_ref, knot_out, residual_out
):
    params = knot_out.shape[0]
    squares = squares_ref[0]
    for d in range(1, squares_ref.shape[0]):
        squares = squares + squares_ref[d]
    curvature = 0.5 * jnp.sum(squares, keepdims=True) + damping * full_dot(
        direction_ref, direction_ref
    )
    length = norm_ref[0:1, 0:1] / curvature
    knot = knot_ref[...] + length * direction_ref[me_ref[0]]
    knot_out[...] = knot[0:params]
    residual_out[...] = residual_ref[...] - length * diff_ref[...]


def call(kernel, outs, ins, scratch=()):
    return pl.pallas_call(
        kernel,
        out_shape=outs,
        in_specs=ins,
        out_specs=jax.tree.map(lambda _: VMEM, outs),
        scratch_shapes=list(scratch),
        compiler_params=PARAMS,
    )


def local(jac, obs, match, tile_knot, tile_frac):
    tiles, params, columns = jac.shape
    n_track = lax.axis_size("track")
    n_det = lax.axis_size("det")
    n_all = n_track * n_det
    q = tiles // n_track
    me = lax.axis_index("track").astype(jnp.int32).reshape(1)

    perm, weights, sent = call(
        functools.partial(order_kernel, q),
        (
            kept((tiles, tiles), jnp.bfloat16),
            kept((KNOT_DEV + SUB, n_track * LANES)),
            f32(tiles, columns),
        ),
        [SMEM, ANY, ANY, ANY, ANY],
        [
            pltpu.VMEM((1, tiles), jnp.int32),
            pltpu.VMEM((1, tiles), jnp.int32),
            pltpu.VMEM((1, tiles), jnp.float32),
            pltpu.VMEM((tiles, columns), jnp.float32),
            pltpu.SemaphoreType.DMA((4,)),
        ],
    )(me, *map(from_hbm, (match[None], tile_knot[None], tile_frac[None], obs)))

    def crossing(values):
        return lax.all_to_all(values, "track", split_axis=0, concat_axis=0, tiled=True)

    def everywhere(values):
        return lax.all_to_all(values, ("track", "det"), split_axis=0, concat_axis=0, tiled=True)

    arrived = crossing(sent)
    jac_rows = call(
        functools.partial(jac_kernel, q, math.gcd(params, 3)),
        kept((params, tiles, columns)),
        [VMEM, ANY],
        [
            pltpu.VMEM((params, tiles, columns), jnp.float32),
            pltpu.SemaphoreType.DMA((params,)),
        ],
    )(perm, from_hbm(jnp.transpose(jac, (1, 0, 2))))

    def adjoint(sent, arrived):
        diff, payload = call(
            functools.partial(adjoint_kernel, q),
            (f32(tiles, columns), f32(n_all, PAD, LANES)),
            [SMEM] + [VMEM] * 4,
            [pltpu.VMEM((n_track, params * SUB, LANES), jnp.float32)],
        )(me, sent, arrived, jac_rows, weights)
        return diff, everywhere(payload)

    field = f32(n_track, PAD, LANES)
    interp = pltpu.VMEM((n_track, PAD, LANES), jnp.float32)
    residual, gathered = adjoint(sent, arrived)
    gradient, slope_norm, sent = call(
        functools.partial(first_kernel, q, n_det),
        (field, f32(SUB, LANES), f32(tiles, columns)),
        [SMEM] + [VMEM] * 3,
        [interp],
    )(me, gathered, jac_rows, weights)
    direction = gradient
    knot_field = jnp.zeros((PAD, KNOT_DEV), jnp.float32)
    for iteration in range(ITERS - 1):
        change, gathered = adjoint(sent, crossing(sent))
        gradient, direction, slope_norm, knot_field, residual, sent = call(
            functools.partial(step_kernel, q, n_det),
            (field, field, f32(SUB, LANES), f32(PAD, KNOT_DEV), f32(tiles, columns), f32(tiles, columns)),
            [SMEM] + [VMEM] * 9,
            [pltpu.VMEM((n_track, PAD, LANES), jnp.float32), interp],
        )(
            me, gathered, jac_rows, weights, gradient, direction, slope_norm, knot_field, residual, change
        )
    change, squares = call(
        functools.partial(last_kernel, q),
        (f32(tiles, columns), f32(n_all, 1, LANES)),
        [SMEM] + [VMEM] * 2,
    )(me, sent, crossing(sent))
    squares = everywhere(squares)
    residual, change = call(
        functools.partial(restore_kernel, q),
        (f32(tiles, columns), f32(tiles, columns)),
        [VMEM] * 3,
    )(perm, residual, change)
    return call(
        finish_kernel,
        (f32(params, KNOT_DEV), f32(tiles, columns)),
        [SMEM] + [VMEM] * 6,
    )(me, squares, direction, slope_norm, knot_field, residual, change)


def solution(mesh):
    in_specs = (P("track", None, "det"), P("track", "det"), P("track"), P("track"), P("track"))
    out_specs = (P(None, "track"), P("track", "det"))
    return jax.shard_map(local, mesh=mesh, in_specs=in_specs, out_specs=out_specs, check_vma=False)
```

```python
import functools
import math

import jax
import jax.numpy as jnp
from jax import lax
from jax.experimental import pallas as pl
from jax.experimental.pallas import tpu as pltpu
from jax.sharding import PartitionSpec as P

KNOT_DEV = 128
ITERS = 4
LANES = 128
SUB = 8
PAD = 16
VMEM_BYTES = 14 * 2**20


damping = 1.0

SMEM = pl.BlockSpec(memory_space=pltpu.SMEM)
VMEM = pl.BlockSpec(memory_space=pltpu.VMEM)
ANY = pl.BlockSpec(memory_space=pl.ANY)
PARAMS = pltpu.CompilerParams(vmem_limit_bytes=VMEM_BYTES)
HIGHEST = lax.Precision.HIGHEST


def kept(shape, dtype=jnp.float32):
    return pltpu.VMEM(shape, dtype)


def from_hbm(x):
    return pltpu.with_memory_space_constraint(x, pltpu.HBM)


def f32(*shape):
    return jax.ShapeDtypeStruct(shape, jnp.float32)


def dot(a, b, dims):
    return lax.dot_general(
        a, b, (dims, ((), ())), precision=HIGHEST, preferred_element_type=jnp.float32
    )


def split3(x):
    first = x.astype(jnp.bfloat16)
    rest = x - first.astype(jnp.float32)
    second = rest.astype(jnp.bfloat16)
    third = (rest - second.astype(jnp.float32)).astype(jnp.bfloat16)
    return first, second, third


def bf16_dot(a, b):
    return jnp.dot(a, b, preferred_element_type=jnp.float32)


def turn(x, shift):
    shift = shift % LANES
    return x if shift == 0 else pltpu.roll(x, shift, 1)


def lane_group(shape, q):
    return lax.broadcasted_iota(jnp.int32, shape, 1) // q


def to_crossing(arrays, perm, q, store):
    tiles = arrays[0].shape[0]
    groups = LANES // q
    stacked = []
    for x in arrays:
        across = jnp.concatenate(
            [x[c * LANES : (c + 1) * LANES].T for c in range(tiles // LANES)], axis=1
        )
        stacked.extend(split3(across))
    moved = bf16_dot(jnp.concatenate(stacked, axis=0), perm)
    group = lane_group((q, LANES), q)
    for index in range(len(arrays)):
        third, second, first = (
            moved[(3 * index + part) * LANES : (3 * index + part + 1) * LANES] for part in (2, 1, 0)
        )
        whole = third + second + first
        for c in range(tiles // LANES):
            for b in range(groups):
                block = None
                for h in range(groups):
                    piece = turn(
                        whole[h * q : (h + 1) * q, c * LANES : (c + 1) * LANES], (h - b) * q
                    )
                    block = piece if block is None else jnp.where(group == h, piece, block)
                store(index, c * groups + b, block)


def from_crossing(load, perm, q, tiles):
    groups = LANES // q
    group = lane_group((q, LANES), q)
    parts = []
    for c in range(tiles // LANES):
        rows = []
        for h in range(groups):
            block = None
            for b in range(groups):
                piece = turn(load(c * groups + b), (b - h) * q)
                block = piece if block is None else jnp.where(group == b, piece, block)
            rows.append(block)
        parts.append(jnp.concatenate(rows, axis=0).T)
    stacked = jnp.concatenate(parts, axis=0)
    return sum(bf16_dot(perm, part) for part in reversed(split3(stacked)))


def crossing_order(me, match):
    tiles = match.shape[1]
    slot = lax.broadcasted_iota(jnp.int32, (1, tiles), 1)
    peer = match // tiles
    other = match - peer * tiles
    inner = jnp.where(
        peer == me,
        jnp.minimum(slot, other) + jnp.where(slot > other, tiles, 0),
        jnp.where(peer > me, slot, other),
    )
    key = (peer * (2 * tiles) + inner).astype(jnp.float32)
    key_cols = jnp.broadcast_to(key, (LANES, tiles)).T[:, :1]
    place = jnp.sum(jnp.where(key < key_cols, 1.0, 0.0), axis=1, keepdims=True)
    cols = lax.broadcasted_iota(jnp.int32, (tiles, tiles), 1).astype(jnp.float32)
    return jnp.where(place == cols, 1.0, 0.0).astype(jnp.bfloat16)


def order_kernel(
    q,
    me_ref,
    match_hbm,
    knot_hbm,
    frac_hbm,
    obs_hbm,
    perm_ref,
    weight_ref,
    obs_out,
    match_ref,
    knot_ref,
    frac_ref,
    obs_ref,
    sems,
):
    tiles = obs_ref.shape[0]
    pairs = ((match_hbm, match_ref), (knot_hbm, knot_ref), (frac_hbm, frac_ref), (obs_hbm, obs_ref))
    copies = [
        pltpu.make_async_copy(source, target, sems.at[index])
        for index, (source, target) in enumerate(pairs)
    ]
    for copy in copies:
        copy.start()
    copies[0].wait()
    groups = LANES // q
    me = me_ref[0]
    perm = crossing_order(me, match_ref[...])
    perm_ref[...] = perm

    def put(_, index, block):
        obs_out[index * q : (index + 1) * q, :] = block

    copies[3].wait()
    to_crossing([obs_ref[...]], perm, q, put)

    copies[1].wait()
    copies[2].wait()
    row = lax.broadcasted_iota(jnp.int32, (SUB, tiles), 0)
    facts = jnp.where(row == 0, knot_ref[...].astype(jnp.float32), frac_ref[...])
    moved = sum(bf16_dot(part, perm) for part in reversed(split3(facts)))
    group = lane_group((SUB, LANES), q)
    knots = lax.broadcasted_iota(jnp.int32, (KNOT_DEV, LANES), 0).astype(jnp.float32)
    first_row = lax.broadcasted_iota(jnp.int32, (SUB, LANES), 0) == 0
    for c in range(tiles // LANES):
        chunk = moved[:, c * LANES : (c + 1) * LANES]
        for b in range(groups):
            block = None
            for h in range(groups):
                piece = turn(chunk, (h - b) * q)
                block = piece if block is None else jnp.where(group == h, piece, block)
            knot = block[0:1]
            frac = block[1:2]
            lanes = slice((c * groups + b) * LANES, (c * groups + b + 1) * LANES)
            weight_ref[0:KNOT_DEV, lanes] = jnp.where(knots == knot, 1.0 - frac, 0.0) + jnp.where(
                knots == knot + 1.0, frac, 0.0
            )
            edge = jnp.where(knot == KNOT_DEV - 1.0, frac, 0.0)
            weight_ref[KNOT_DEV : KNOT_DEV + SUB, lanes] = jnp.where(first_row, edge, 0.0)


def jac_kernel(q, together, perm_ref, jac_hbm, out_ref, jac_ref, sems):
    params = jac_ref.shape[0]
    copies = [
        pltpu.make_async_copy(jac_hbm.at[p], jac_ref.at[p], sems.at[p]) for p in range(params)
    ]
    for copy in copies:
        copy.start()
    for first in range(0, params, together):
        for p in range(first, first + together):
            copies[p].wait()

        def put(index, block_index, block):
            out_ref[first + index, block_index * q : (block_index + 1) * q, :] = block

        to_crossing([jac_ref[p] for p in range(first, first + together)], perm_ref[...], q, put)


def crossing_values(me, arrived_ref, out_ref, q):
    out_ref[...] = arrived_ref[...]
    own = arrived_ref[pl.ds(pl.multiple_of(me * q, SUB), q), :]
    lane = lax.broadcasted_iota(jnp.int32, (q, LANES), 1)
    swapped = jnp.where(lane % q < q // 2, turn(own, -(q // 2)), turn(own, q // 2))
    out_ref[pl.ds(pl.multiple_of(me * q, SUB), q), :] = swapped


def difference(me, sent_ref, arrived_ref, out_ref, q):
    crossing_values(me, arrived_ref, out_ref, q)
    out_ref[...] = sent_ref[...] - out_ref[...]


def adjoint_kernel(q, me_ref, sent_ref, arrived_ref, jac_ref, weight_ref, diff_ref, send_ref, parts_ref):
    params, tiles, _ = jac_ref.shape
    difference(me_ref[0], sent_ref, arrived_ref, diff_ref, q)

    def block_sums(b, carry):
        rows = pl.ds(pl.multiple_of(b * q, SUB), q)
        diff = diff_ref[rows, :]
        for p in range(params):
            product = jac_ref[p, rows, :] * diff
            folded = product[0:SUB]
            for step in range(1, q // SUB):
                folded = folded + product[step * SUB : (step + 1) * SUB]
            parts_ref[b, p * SUB : (p + 1) * SUB, :] = folded
        return carry

    blocks = tiles // q
    lax.fori_loop(0, blocks, block_sums, 0)
    spread = None
    for b in range(blocks):
        term = dot(parts_ref[b], weight_ref[:, b * LANES : (b + 1) * LANES], ((1,), (1,)))
        spread = term if spread is None else spread + term
    lane = lax.broadcasted_iota(jnp.int32, (1, LANES), 1)
    send_ref[...] = jnp.zeros(send_ref.shape, jnp.float32)
    spill_row = jnp.zeros((1, LANES), jnp.float32)
    rows = []
    for p in range(params):
        total = jnp.sum(spread[p * SUB : (p + 1) * SUB], axis=0, keepdims=True)
        rows.append(total[:, :KNOT_DEV])
        spill_row = jnp.where(lane == p, total[:, KNOT_DEV : KNOT_DEV + 1], spill_row)
    rows.append(spill_row)
    block = jnp.concatenate(rows, axis=0)
    for d in range(send_ref.shape[0]):
        send_ref[d, 0 : params + 1, :] = block


def field_sums(gathered_ref, n_track, n_det, params, store, base=0):
    lane = lax.broadcasted_iota(jnp.int32, (PAD, LANES), 1)
    row = lax.broadcasted_iota(jnp.int32, (PAD, LANES), 0)
    spill = jnp.zeros((PAD, 1), jnp.float32)
    for b in range(n_track):
        total = gathered_ref[b * n_det, base : base + PAD, :]
        for d in range(1, n_det):
            total = total + gathered_ref[b * n_det + d, base : base + PAD, :]
        field = jnp.where(row < params, total, 0.0)
        field = field + jnp.where(lane == 0, spill, 0.0)
        store(b, field)
        spill = jnp.sum(
            jnp.where((lane == row) & (row < params), total[params : params + 1], 0.0),
            axis=1,
            keepdims=True,
        )


def total_of(x):
    return jnp.sum(jnp.sum(x, axis=0), keepdims=True).reshape(1, 1)


def full_dot(a_ref, b_ref):
    total = a_ref[0] * b_ref[0]
    for b in range(1, a_ref.shape[0]):
        total = total + a_ref[b] * b_ref[b]
    return jnp.sum(total, keepdims=True)


def predict(me, q, direction_ref, jac_ref, weight_ref, interp_ref, sent_ref):
    params, tiles, _ = jac_ref.shape
    n_track = direction_ref.shape[0]
    following = direction_ref[jnp.minimum(me + 1, n_track - 1)][:, 0:1]
    following = jnp.where(me + 1 < n_track, following, 0.0)
    own = direction_ref[me]
    blocks = tiles // q
    for b in range(blocks):
        lanes = slice(b * LANES, (b + 1) * LANES)
        interp_ref[b] = (
            dot(own, weight_ref[0:KNOT_DEV, lanes], ((1,), (0,)))
            + following * weight_ref[KNOT_DEV : KNOT_DEV + 1, lanes]
        )

    def block_values(b, carry):
        rows = pl.ds(pl.multiple_of(b * q, SUB), q)
        interp = interp_ref[b]
        total = jac_ref[0, rows, :] * interp[0:1]
        for p in range(1, params):
            total = total + jac_ref[p, rows, :] * interp[p : p + 1]
        sent_ref[rows, :] = total
        return carry

    lax.fori_loop(0, blocks, block_values, 0)


def first_kernel(
    q, n_det, me_ref, gathered_ref, jac_ref, weight_ref, grad_ref, norm_ref, sent_ref, interp_ref
):
    n_track = grad_ref.shape[0]

    def put(b, field):
        grad_ref[b] = field

    field_sums(gathered_ref, n_track, n_det, jac_ref.shape[0], put)
    norm_ref[...] = jnp.broadcast_to(full_dot(grad_ref, grad_ref), norm_ref.shape)
    predict(me_ref[0], q, grad_ref, jac_ref, weight_ref, interp_ref, sent_ref)


def step_kernel(
    q,
    n_det,
    me_ref,
    gathered_ref,
    jac_ref,
    weight_ref,
    grad_ref,
    direction_ref,
    norm_ref,
    knot_ref,
    residual_ref,
    diff_ref,
    grad_out,
    direction_out,
    norm_out,
    knot_out,
    residual_out,
    sent_ref,
    image_ref,
    interp_ref,
):
    n_track = grad_ref.shape[0]
    me = me_ref[0]

    def put(b, field):
        image_ref[b] = field + damping * direction_ref[b]

    field_sums(gathered_ref, n_track, n_det, jac_ref.shape[0], put)
    norm = norm_ref[0:1, 0:1]
    length = norm / full_dot(direction_ref, image_ref)
    knot_out[...] = knot_ref[...] + length * direction_ref[me]
    residual_out[...] = residual_ref[...] - length * diff_ref[...]
    for b in range(n_track):
        grad_out[b] = grad_ref[b] - length * image_ref[b]
    new_norm = full_dot(grad_out, grad_out)
    norm_out[...] = jnp.broadcast_to(new_norm, norm_out.shape)
    ratio = new_norm / norm
    for b in range(n_track):
        direction_out[b] = grad_out[b] + ratio * direction_ref[b]
    predict(me, q, direction_out, jac_ref, weight_ref, interp_ref, sent_ref)


def last_kernel(q, me_ref, sent_ref, arrived_ref, diff_ref, send_ref):
    difference(me_ref[0], sent_ref, arrived_ref, diff_ref, q)
    diff = diff_ref[...]
    squares = jnp.sum(diff * diff, axis=0, keepdims=True)
    send_ref[...] = jnp.broadcast_to(squares[None], send_ref.shape)


def restore_kernel(q, perm_ref, residual_ref, diff_ref, residual_out, diff_out):
    tiles = residual_ref.shape[0]
    for source, target in ((residual_ref, residual_out), (diff_ref, diff_out)):
        target[...] = from_crossing(
            lambda index: source[index * q : (index + 1) * q, :], perm_ref[...], q, tiles
        )


def finish_kernel(
    me_ref, squares_ref, direction_ref, norm_ref, knot_ref, residual_ref, diff_ref, knot_out, residual_out
):
    params = knot_out.shape[0]
    squares = squares_ref[0]
    for d in range(1, squares_ref.shape[0]):
        squares = squares + squares_ref[d]
    curvature = 0.5 * jnp.sum(squares, keepdims=True) + damping * full_dot(
        direction_ref, direction_ref
    )
    length = norm_ref[0:1, 0:1] / curvature
    knot = knot_ref[...] + length * direction_ref[me_ref[0]]
    knot_out[...] = knot[0:params]
    residual_out[...] = residual_ref[...] - length * diff_ref[...]


def call(kernel, outs, ins, scratch=()):
    return pl.pallas_call(
        kernel,
        out_shape=outs,
        in_specs=ins,
        out_specs=jax.tree.map(lambda _: VMEM, outs),
        scratch_shapes=list(scratch),
        compiler_params=PARAMS,
    )


def row_sums(parts):
    row = lax.broadcasted_iota(jnp.int32, (SUB, LANES), 0)
    level = list(parts)
    zero = jnp.zeros((SUB, LANES), jnp.float32)
    while len(level) % SUB:
        level.append(zero)
    for distance in (1, 2, 4):
        first = (row // distance) % 2 == 0
        level = [
            jnp.where(first, a, b) + pltpu.roll(jnp.where(first, b, a), distance, 0)
            for a, b in zip(level[::2], level[1::2])
        ]
    return level[0] if len(level) == 1 else jnp.concatenate(level, axis=0)


def fold_rows(x):
    total = x[0:SUB]
    for step in range(1, x.shape[0] // SUB):
        total = total + x[step * SUB : (step + 1) * SUB]
    return total


def fold_lanes(x, half):
    shift = half
    while shift < LANES:
        x = x + pltpu.roll(x, shift, 1)
        shift *= 2
    return x


def pair_index(p, other):
    low, high = min(p, other), max(p, other)
    return high * (high + 1) // 2 + low


def pad_to(x, unit):
    return -(-x // unit) * unit


def weight_rows(knot, frac):
    knots = lax.broadcasted_iota(jnp.int32, (KNOT_DEV, knot.shape[1]), 0).astype(jnp.float32)
    main = jnp.where(knots == knot, 1.0 - frac, 0.0) + jnp.where(knots == knot + 1.0, frac, 0.0)
    first = lax.broadcasted_iota(jnp.int32, (SUB, knot.shape[1]), 0) == 0
    edge = jnp.where(first, jnp.where(knot == KNOT_DEV - 1.0, frac, 0.0), 0.0)
    return main, edge


def setup_kernel(
    half,
    together,
    me_ref,
    match_hbm,
    knot_hbm,
    frac_hbm,
    obs_hbm,
    jac_hbm,
    perm_ref,
    weight_ref,
    rows_ref,
    message_ref,
    match_ref,
    knot_ref,
    frac_ref,
    obs_ref,
    jac_ref,
    sems,
):
    params, tiles, _ = jac_ref.shape
    n_track = message_ref.shape[0]
    q = 2 * half
    pairs = [(match_hbm, match_ref), (knot_hbm, knot_ref), (frac_hbm, frac_ref), (obs_hbm, obs_ref)]
    pairs += [(jac_hbm.at[p], jac_ref.at[p]) for p in range(params)]
    copies = [
        pltpu.make_async_copy(source, target, sems.at[index])
        for index, (source, target) in enumerate(pairs)
    ]
    for copy in copies:
        copy.start()
    copies[0].wait()
    me = me_ref[0]
    perm_ref[...] = crossing_order(me, match_ref[...])
    perm = perm_ref[...]
    for copy in copies[1:4]:
        copy.wait()

    row = lax.broadcasted_iota(jnp.int32, (SUB, tiles), 0)
    facts = jnp.where(row == 0, knot_ref[...].astype(jnp.float32), frac_ref[...])
    moved = sum(bf16_dot(part, perm) for part in reversed(split3(facts)))
    main, edge = weight_rows(moved[0:1], moved[1:2])
    weight_ref[0:KNOT_DEV, :] = main
    weight_ref[KNOT_DEV : KNOT_DEV + SUB, :] = edge

    obs_row = params * half
    per_chunk = LANES // q
    for b in range(n_track):
        chunk = moved[:, b // per_chunk * LANES : (b // per_chunk + 1) * LANES]
        message_ref[b, obs_row + q : obs_row + q + SUB, :] = turn(chunk, -(b % per_chunk) * q)

    def put_obs(_, s, block):
        first = obs_row + (s % 2) * half
        message_ref[s // 2, first : first + half, :] = block

    to_crossing([obs_ref[...]], perm, half, put_obs)

    for first in range(0, params, together):
        for p in range(first, first + together):
            copies[4 + p].wait()

        def put(index, s, block):
            rows_ref[first + index, s * half : (s + 1) * half, :] = block

        to_crossing([jac_ref[p] for p in range(first, first + together)], perm, half, put)
    for b in range(n_track):
        offset = pl.multiple_of(jnp.where(me <= b, 2 * b + 1, 2 * b) * half, SUB)
        for p in range(params):
            message_ref[b, p * half : (p + 1) * half, :] = rows_ref[p, pl.ds(offset, half), :]


def payload_rows(spread, params):
    lane = lax.broadcasted_iota(jnp.int32, (PAD, LANES), 1)
    row = lax.broadcasted_iota(jnp.int32, (PAD, LANES), 0)
    spill = jnp.sum(
        jnp.where(lane == row, spread[:, KNOT_DEV : KNOT_DEV + 1], 0.0), axis=0, keepdims=True
    )
    return jnp.where(row < params, spread[:, :KNOT_DEV], jnp.where(row == params, spill, 0.0))


def gram_kernel(half, me_ref, sent_ref, arrived_ref, rows_ref, weight_ref, misfit_ref, partner_ref, back_ref, diag_ref):
    params, tiles, _ = rows_ref.shape
    n_track = arrived_ref.shape[0]
    q = 2 * half
    me = me_ref[0]
    obs_row = params * half
    group = lax.broadcasted_iota(jnp.int32, (PAD, LANES), 1) // half
    lane8 = lax.broadcasted_iota(jnp.int32, (SUB, LANES), 1)
    subs = LANES // half

    per_chunk = LANES // q
    for c in range(tiles // LANES):
        facts = None
        for b in range(per_chunk):
            block = c * per_chunk + b
            piece = arrived_ref[block, obs_row + q : obs_row + q + SUB, :]
            swapped = jnp.where(lane8 < half, turn(piece, -half), turn(piece, half))
            piece = turn(jnp.where(me == block, swapped, piece), b * q)
            facts = piece if facts is None else jnp.where(lane8 // q == b, piece, facts)
        main, edge = weight_rows(facts[0:1], facts[1:2])
        lanes = slice(c * LANES, (c + 1) * LANES)
        partner_ref[0:KNOT_DEV, lanes] = main
        partner_ref[KNOT_DEV : KNOT_DEV + SUB, lanes] = edge

    for s in range(2 * n_track):
        b = s // 2
        own = sent_ref[b, obs_row + (s % 2) * half : obs_row + (s % 2 + 1) * half, :]
        first = pl.multiple_of(obs_row + jnp.where(me == b, 1 - s % 2, s % 2) * half, SUB)
        misfit_ref[s * half : (s + 1) * half, :] = own - arrived_ref[b, pl.ds(first, half), :]

    held = -(-params // subs)

    def cross(b, carry):
        offset = pl.multiple_of(jnp.where(me <= b, 2 * b, 2 * b + 1) * half, SUB)
        for slot in range(held):
            total = jnp.zeros((PAD, LANES), jnp.float32)
            for j in range(subs):
                p = j * held + slot
                if p >= params:
                    continue
                own = rows_ref[p, pl.ds(offset, half), :]
                parts = [
                    fold_rows(own * arrived_ref[b, other * half : (other + 1) * half, :])
                    for other in range(params)
                ]
                total = jnp.where(group == j, fold_lanes(row_sums(parts), half), total)
            back_ref[b, slot * PAD : (slot + 1) * PAD, :] = total
        return carry

    lax.fori_loop(0, n_track, cross, 0)

    n_pairs = params * (params + 1) // 2
    spread = None
    for c in range(tiles // LANES):
        lanes = slice(c * LANES, (c + 1) * LANES)

        def own_block(b, carry):
            totals, values = carry
            rows = pl.ds(pl.multiple_of((c * subs + b) * half, SUB), half)
            miss = misfit_ref[rows, :]
            parts = []
            for high in range(params):
                right = rows_ref[high, rows, :]
                for low in range(high + 1):
                    parts.append(fold_rows(rows_ref[low, rows, :] * right))
            sums = fold_lanes(row_sums(parts), half)
            wide = lax.broadcasted_iota(jnp.int32, sums.shape, 1) // half
            totals = jnp.where(wide == b, sums, totals)
            sums = fold_lanes(
                row_sums([fold_rows(rows_ref[p, rows, :] * miss) for p in range(params)]), half
            )
            return totals, jnp.where(group == b, sums, values)

        totals, values = lax.fori_loop(
            0,
            subs,
            own_block,
            (
                jnp.zeros((pad_to(n_pairs, SUB), LANES), jnp.float32),
                jnp.zeros((PAD, LANES), jnp.float32),
            ),
        )
        diag_ref[:, lanes] = totals
        term = dot(values, weight_ref[:, lanes], ((1,), (1,)))
        spread = term if spread is None else spread + term
    block = payload_rows(spread, params)
    for b in range(n_track):
        back_ref[b, held * PAD : (held + 1) * PAD, :] = block


def following_of(field_ref, index):
    n_track = field_ref.shape[0]
    if isinstance(index, int):
        if index + 1 == n_track:
            return jnp.zeros((PAD, 1), jnp.float32)
        return field_ref[index + 1][:, 0:1]
    values = field_ref[jnp.minimum(index + 1, n_track - 1)][:, 0:1]
    return jnp.where(index + 1 < n_track, values, 0.0)


def interp_own(me, field_ref, weight_ref):
    return (
        dot(field_ref[me], weight_ref[0:KNOT_DEV, :], ((1,), (0,)))
        + following_of(field_ref, me) * weight_ref[KNOT_DEV : KNOT_DEV + 1, :]
    )


def normal_rows(half, params, me, field_ref, cross_ref, diag_ref, weight_ref, partner_ref):
    tiles = weight_ref.shape[1]
    q = 2 * half
    own = interp_own(me, field_ref, weight_ref)
    lane = lax.broadcasted_iota(jnp.int32, (PAD, LANES), 1)
    per_chunk = LANES // q
    spread = None
    for c in range(tiles // LANES):
        lanes = slice(c * LANES, (c + 1) * LANES)
        other = None
        for b in range(per_chunk):
            block = c * per_chunk + b
            piece = (
                dot(field_ref[block], partner_ref[0:KNOT_DEV, lanes], ((1,), (0,)))
                + following_of(field_ref, block) * partner_ref[KNOT_DEV : KNOT_DEV + 1, lanes]
            )
            other = piece if other is None else jnp.where(lane // q == b, piece, other)
        total = None
        by_slot = None
        by_row = []
        for p in range(params):
            term = diag_ref[p, :, lanes] * own[p : p + 1, lanes]
            total = term if total is None else total + term
            matrix = cross_ref[p, :, lanes]
            term = matrix * other[p : p + 1]
            by_slot = term if by_slot is None else by_slot + term
            by_row.append(fold_rows(matrix * other))
        block = c * per_chunk + lane // q
        is_first = (lane // half) % 2 == 0
        is_owner = jnp.where(is_first, me, block) <= jnp.where(is_first, block, me - 1)
        total = total - jnp.where(is_owner, row_sums(by_row), by_slot)
        term = dot(total, weight_ref[:, lanes], ((1,), (1,)))
        spread = term if spread is None else spread + term
    return spread


def send_rows(send_ref, block):
    for b in range(send_ref.shape[0]):
        send_ref[b] = block


def start_kernel(
    half,
    me_ref,
    kept_ref,
    arrived_ref,
    pairs_ref,
    weight_ref,
    partner_ref,
    cross_ref,
    diag_ref,
    grad_ref,
    norm_ref,
    send_ref,
):
    params = cross_ref.shape[0]
    tiles = cross_ref.shape[2]
    n_track = grad_ref.shape[0]
    me = me_ref[0]
    subs = LANES // half
    held = -(-params // subs)
    group = lax.broadcasted_iota(jnp.int32, (PAD, LANES), 1) // half
    for s in range(tiles // half):
        b = s // 2
        is_owner = me <= b if s % 2 == 0 else me > b
        lanes = slice(s // subs * LANES, (s // subs + 1) * LANES)
        for p in range(params):
            rows = slice(p % held * PAD, (p % held + 1) * PAD)
            piece = jnp.where(is_owner, kept_ref[b, rows, :], arrived_ref[b, rows, :])
            piece = turn(piece, (s % subs - p // held) * half)
            if s % subs:
                piece = jnp.where(group == s % subs, piece, cross_ref[p, :, lanes])
            cross_ref[p, :, lanes] = piece
    diag_ref[...] = jnp.zeros(diag_ref.shape, jnp.float32)
    for p in range(params):
        for other in range(params):
            index = pair_index(p, other)
            diag_ref[p, other : other + 1, :] = pairs_ref[index : index + 1, :]

    def put(b, field):
        grad_ref[b] = field

    field_sums(arrived_ref, n_track, 1, params, put, held * PAD)
    norm_ref[...] = jnp.broadcast_to(full_dot(grad_ref, grad_ref), norm_ref.shape)
    spread = normal_rows(half, params, me, grad_ref, cross_ref, diag_ref, weight_ref, partner_ref)
    send_rows(send_ref, payload_rows(spread, params))


def advance(params, gathered_ref, grad_ref, direction_ref, norm_ref, knot_ref, grad_out, direction_out, norm_out, knot_out, image_ref):
    n_track = grad_ref.shape[0]

    def put(b, field):
        image_ref[b] = field + damping * direction_ref[b]

    field_sums(gathered_ref, n_track, 1, params, put)
    norm = norm_ref[0:1, 0:1]
    length = norm / full_dot(direction_ref, image_ref)
    for b in range(n_track):
        knot_out[b] = knot_ref[b] + length * direction_ref[b]
        grad_out[b] = grad_ref[b] - length * image_ref[b]
    new_norm = full_dot(grad_out, grad_out)
    norm_out[...] = jnp.broadcast_to(new_norm, norm_out.shape)
    ratio = new_norm / norm
    for b in range(n_track):
        direction_out[b] = grad_out[b] + ratio * direction_ref[b]


def next_kernel(
    half,
    me_ref,
    gathered_ref,
    grad_ref,
    direction_ref,
    norm_ref,
    knot_ref,
    cross_ref,
    diag_ref,
    weight_ref,
    partner_ref,
    grad_out,
    direction_out,
    norm_out,
    knot_out,
    send_ref,
    image_ref,
):
    params = cross_ref.shape[0]
    advance(
        params, gathered_ref, grad_ref, direction_ref, norm_ref, knot_ref, grad_out, direction_out, norm_out, knot_out, image_ref
    )
    spread = normal_rows(
        half, params, me_ref[0], direction_out, cross_ref, diag_ref, weight_ref, partner_ref
    )
    send_rows(send_ref, payload_rows(spread, params))


def final_kernel(
    half,
    me_ref,
    gathered_ref,
    grad_ref,
    direction_ref,
    norm_ref,
    knot_ref,
    cross_ref,
    diag_ref,
    weight_ref,
    partner_ref,
    rows_ref,
    direction_out,
    norm_out,
    knot_out,
    send_ref,
    image_ref,
    grad_out,
    interp_ref,
):
    params, tiles, _ = rows_ref.shape
    n_track = send_ref.shape[0]
    me = me_ref[0]
    q = 2 * half
    subs = LANES // half
    advance(
        params, gathered_ref, grad_ref, direction_ref, norm_ref, knot_ref, grad_out, direction_out, norm_out, knot_out, image_ref
    )
    spread = normal_rows(
        half, params, me, direction_out, cross_ref, diag_ref, weight_ref, partner_ref
    )
    block = spread[:, :KNOT_DEV] * direction_out[me]
    edge = spread[:, KNOT_DEV : KNOT_DEV + 1] * following_of(direction_out, me)
    share = jnp.sum(block, keepdims=True) + jnp.sum(edge, keepdims=True)
    group = lax.broadcasted_iota(jnp.int32, (PAD, LANES), 1) // half
    for index, field in enumerate((knot_out, direction_out)):
        interp = interp_own(me, field, weight_ref)
        for s in range(tiles // half):
            chunk = interp[:, s // subs * LANES : (s // subs + 1) * LANES]
            wide = None
            for h in range(subs):
                piece = turn(chunk, (h - s % subs) * half)
                wide = piece if wide is None else jnp.where(group == h, piece, wide)
            interp_ref[index, s] = wide

    def values(b, carry):
        for s in range(2):
            rows = pl.ds(pl.multiple_of((2 * b + s) * half, SUB), half)
            sums = [None, None]
            knot_interp = interp_ref[0, 2 * b + s]
            direction_interp = interp_ref[1, 2 * b + s]
            for p in range(params):
                jac = rows_ref[p, rows, :]
                for index, interp in enumerate((knot_interp, direction_interp)):
                    term = jac * interp[p : p + 1]
                    sums[index] = term if sums[index] is None else sums[index] + term
            for index in range(2):
                first = index * q + s * half
                send_ref[b, first : first + half, :] = sums[index]
        send_ref[b, 2 * q : 2 * q + SUB, :] = jnp.broadcast_to(share, (SUB, LANES))
        return carry

    lax.fori_loop(0, n_track, values, 0)


def close_kernel(
    half,
    me_ref,
    sent_ref,
    arrived_ref,
    direction_ref,
    norm_ref,
    knot_ref,
    misfit_ref,
    perm_ref,
    knot_out,
    residual_out,
    residual_ref,
):
    params = knot_out.shape[0]
    n_track = sent_ref.shape[0]
    tiles = misfit_ref.shape[0]
    me = me_ref[0]
    q = 2 * half
    share = arrived_ref[0, 2 * q : 2 * q + 1, :]
    for b in range(1, n_track):
        share = share + arrived_ref[b, 2 * q : 2 * q + 1, :]
    curvature = share[:, 0:1] + damping * full_dot(direction_ref, direction_ref)
    length = norm_ref[0:1, 0:1] / curvature
    knot = knot_ref[me] + length * direction_ref[me]
    knot_out[...] = knot[0:params]
    for s in range(2 * n_track):
        b = s // 2
        here = (s % 2) * half
        there = jnp.where(me == b, 1 - s % 2, s % 2) * half
        first = pl.ds(pl.multiple_of(there, SUB), half)
        second = pl.ds(pl.multiple_of(q + there, SUB), half)
        own = sent_ref[b, here : here + half, :] - arrived_ref[b, first, :]
        step = sent_ref[b, q + here : q + here + half, :] - arrived_ref[b, second, :]
        rows = slice(s * half, (s + 1) * half)
        residual_ref[rows, :] = misfit_ref[rows, :] - own - length * step
    residual_out[...] = from_crossing(
        lambda index: residual_ref[index * half : (index + 1) * half, :], perm_ref[...], half, tiles
    )


def local_blocks(jac, obs, match, tile_knot, tile_frac):
    tiles, params, columns = jac.shape
    n_track = lax.axis_size("track")
    half = tiles // n_track // 2
    q = 2 * half
    held = -(-params // (LANES // half))
    n_pairs = pad_to(params * (params + 1) // 2, SUB)
    me = lax.axis_index("track").astype(jnp.int32).reshape(1)

    def crossing(values):
        return lax.all_to_all(values, "track", split_axis=0, concat_axis=0, tiled=True)

    weight_shape = (KNOT_DEV + SUB, tiles)
    perm, weights, rows, message = call(
        functools.partial(setup_kernel, half, math.gcd(params, 3)),
        (
            kept((tiles, tiles), jnp.bfloat16),
            kept(weight_shape),
            kept((params, tiles, columns)),
            kept((n_track, params * half + q + SUB, LANES)),
        ),
        [SMEM] + [ANY] * 5,
        [
            pltpu.VMEM((1, tiles), jnp.int32),
            pltpu.VMEM((1, tiles), jnp.int32),
            pltpu.VMEM((1, tiles), jnp.float32),
            pltpu.VMEM((tiles, columns), jnp.float32),
            pltpu.VMEM((params, tiles, columns), jnp.float32),
            pltpu.SemaphoreType.DMA((4 + params,)),
        ],
    )(
        me,
        *map(
            from_hbm,
            (match[None], tile_knot[None], tile_frac[None], obs, jnp.transpose(jac, (1, 0, 2))),
        ),
    )
    misfit, partners, back, pairs = call(
        functools.partial(gram_kernel, half),
        (
            kept((tiles, columns)),
            kept(weight_shape),
            f32(n_track, (held + 1) * PAD, LANES),
            f32(n_pairs, tiles),
        ),
        [SMEM] + [VMEM] * 4,
    )(me, message, crossing(message), rows, weights)
    back, pairs = lax.psum((back, pairs), "det")
    field = f32(n_track, PAD, LANES)
    field_ref = pltpu.VMEM((n_track, PAD, LANES), jnp.float32)
    matrix = kept((params, PAD, tiles))
    norm_shape = f32(SUB, LANES)
    cross, diag, gradient, slope_norm, send = call(
        functools.partial(start_kernel, half),
        (matrix, matrix, field, norm_shape, field),
        [SMEM] + [VMEM] * 5,
    )(me, back, crossing(back), pairs, weights, partners)
    direction = gradient
    knot_field = jnp.zeros((n_track, PAD, LANES), jnp.float32)
    for iteration in range(ITERS - 2):
        gradient, direction, slope_norm, knot_field, send = call(
            functools.partial(next_kernel, half),
            (field, field, norm_shape, field, field),
            [SMEM] + [VMEM] * 9,
            [field_ref],
        )(
            me, crossing(send), gradient, direction, slope_norm, knot_field, cross, diag, weights, partners
        )
    direction, slope_norm, knot_field, send = call(
        functools.partial(final_kernel, half),
        (field, norm_shape, field, f32(n_track, 2 * q + SUB, LANES)),
        [SMEM] + [VMEM] * 10,
        [field_ref, field_ref, pltpu.VMEM((2, tiles // half, PAD, LANES), jnp.float32)],
    )(
        me, crossing(send), gradient, direction, slope_norm, knot_field, cross, diag, weights, partners, rows
    )
    return call(
        functools.partial(close_kernel, half),
        (f32(params, KNOT_DEV), f32(tiles, columns)),
        [SMEM] + [VMEM] * 7,
        [pltpu.VMEM((tiles, columns), jnp.float32)],
    )(me, send, crossing(send), direction, slope_norm, knot_field, misfit, perm)


def local(jac, obs, match, tile_knot, tile_frac):
    tiles, params, columns = jac.shape
    n_track = lax.axis_size("track")
    n_det = lax.axis_size("det")
    n_all = n_track * n_det
    q = tiles // n_track
    if (q // 2) % SUB == 0:
        return local_blocks(jac, obs, match, tile_knot, tile_frac)
    me = lax.axis_index("track").astype(jnp.int32).reshape(1)

    perm, weights, sent = call(
        functools.partial(order_kernel, q),
        (
            kept((tiles, tiles), jnp.bfloat16),
            kept((KNOT_DEV + SUB, n_track * LANES)),
            f32(tiles, columns),
        ),
        [SMEM, ANY, ANY, ANY, ANY],
        [
            pltpu.VMEM((1, tiles), jnp.int32),
            pltpu.VMEM((1, tiles), jnp.int32),
            pltpu.VMEM((1, tiles), jnp.float32),
            pltpu.VMEM((tiles, columns), jnp.float32),
            pltpu.SemaphoreType.DMA((4,)),
        ],
    )(me, *map(from_hbm, (match[None], tile_knot[None], tile_frac[None], obs)))

    def crossing(values):
        return lax.all_to_all(values, "track", split_axis=0, concat_axis=0, tiled=True)

    def everywhere(values):
        return lax.all_to_all(values, ("track", "det"), split_axis=0, concat_axis=0, tiled=True)

    arrived = crossing(sent)
    jac_rows = call(
        functools.partial(jac_kernel, q, math.gcd(params, 3)),
        kept((params, tiles, columns)),
        [VMEM, ANY],
        [
            pltpu.VMEM((params, tiles, columns), jnp.float32),
            pltpu.SemaphoreType.DMA((params,)),
        ],
    )(perm, from_hbm(jnp.transpose(jac, (1, 0, 2))))

    def adjoint(sent, arrived):
        diff, payload = call(
            functools.partial(adjoint_kernel, q),
            (f32(tiles, columns), f32(n_all, PAD, LANES)),
            [SMEM] + [VMEM] * 4,
            [pltpu.VMEM((n_track, params * SUB, LANES), jnp.float32)],
        )(me, sent, arrived, jac_rows, weights)
        return diff, everywhere(payload)

    field = f32(n_track, PAD, LANES)
    interp = pltpu.VMEM((n_track, PAD, LANES), jnp.float32)
    residual, gathered = adjoint(sent, arrived)
    gradient, slope_norm, sent = call(
        functools.partial(first_kernel, q, n_det),
        (field, f32(SUB, LANES), f32(tiles, columns)),
        [SMEM] + [VMEM] * 3,
        [interp],
    )(me, gathered, jac_rows, weights)
    direction = gradient
    knot_field = jnp.zeros((PAD, KNOT_DEV), jnp.float32)
    for iteration in range(ITERS - 1):
        change, gathered = adjoint(sent, crossing(sent))
        gradient, direction, slope_norm, knot_field, residual, sent = call(
            functools.partial(step_kernel, q, n_det),
            (field, field, f32(SUB, LANES), f32(PAD, KNOT_DEV), f32(tiles, columns), f32(tiles, columns)),
            [SMEM] + [VMEM] * 9,
            [pltpu.VMEM((n_track, PAD, LANES), jnp.float32), interp],
        )(
            me, gathered, jac_rows, weights, gradient, direction, slope_norm, knot_field, residual, change
        )
    change, squares = call(
        functools.partial(last_kernel, q),
        (f32(tiles, columns), f32(n_all, 1, LANES)),
        [SMEM] + [VMEM] * 2,
    )(me, sent, crossing(sent))
    squares = everywhere(squares)
    residual, change = call(
        functools.partial(restore_kernel, q),
        (f32(tiles, columns), f32(tiles, columns)),
        [VMEM] * 3,
    )(perm, residual, change)
    return call(
        finish_kernel,
        (f32(params, KNOT_DEV), f32(tiles, columns)),
        [SMEM] + [VMEM] * 6,
    )(me, squares, direction, slope_norm, knot_field, residual, change)


def solution(mesh):
    in_specs = (P("track", None, "det"), P("track", "det"), P("track"), P("track"), P("track"))
    out_specs = (P(None, "track"), P("track", "det"))
    return jax.shard_map(local, mesh=mesh, in_specs=in_specs, out_specs=out_specs, check_vma=False)
```

```python
import functools
import math

import jax
import jax.numpy as jnp
from jax import lax
from jax.experimental import pallas as pl
from jax.experimental.pallas import tpu as pltpu
from jax.sharding import PartitionSpec as P

KNOT_DEV = 128
ITERS = 4
LANES = 128
SUB = 8
PAD = 16
VMEM_BYTES = 14 * 2**20


damping = 1.0

SMEM = pl.BlockSpec(memory_space=pltpu.SMEM)
VMEM = pl.BlockSpec(memory_space=pltpu.VMEM)
ANY = pl.BlockSpec(memory_space=pl.ANY)
PARAMS = pltpu.CompilerParams(vmem_limit_bytes=VMEM_BYTES)
HIGHEST = lax.Precision.HIGHEST


def kept(shape, dtype=jnp.float32):
    return pltpu.VMEM(shape, dtype)


def from_hbm(x):
    return pltpu.with_memory_space_constraint(x, pltpu.HBM)


def f32(*shape):
    return jax.ShapeDtypeStruct(shape, jnp.float32)


def dot(a, b, dims):
    return lax.dot_general(
        a, b, (dims, ((), ())), precision=HIGHEST, preferred_element_type=jnp.float32
    )


def split3(x):
    first = x.astype(jnp.bfloat16)
    rest = x - first.astype(jnp.float32)
    second = rest.astype(jnp.bfloat16)
    third = (rest - second.astype(jnp.float32)).astype(jnp.bfloat16)
    return first, second, third


def bf16_dot(a, b):
    return jnp.dot(a, b, preferred_element_type=jnp.float32)


def turn(x, shift):
    shift = shift % LANES
    return x if shift == 0 else pltpu.roll(x, shift, 1)


def lane_group(shape, q):
    return lax.broadcasted_iota(jnp.int32, shape, 1) // q


def to_crossing(arrays, perm, q, store):
    tiles = arrays[0].shape[0]
    groups = LANES // q
    stacked = []
    for x in arrays:
        across = jnp.concatenate(
            [x[c * LANES : (c + 1) * LANES].T for c in range(tiles // LANES)], axis=1
        )
        stacked.extend(split3(across))
    moved = bf16_dot(jnp.concatenate(stacked, axis=0), perm)
    group = lane_group((q, LANES), q)
    for index in range(len(arrays)):
        third, second, first = (
            moved[(3 * index + part) * LANES : (3 * index + part + 1) * LANES] for part in (2, 1, 0)
        )
        whole = third + second + first
        for c in range(tiles // LANES):
            for b in range(groups):
                block = None
                for h in range(groups):
                    piece = turn(
                        whole[h * q : (h + 1) * q, c * LANES : (c + 1) * LANES], (h - b) * q
                    )
                    block = piece if block is None else jnp.where(group == h, piece, block)
                store(index, c * groups + b, block)


def from_crossing(load, perm, q, tiles):
    groups = LANES // q
    group = lane_group((q, LANES), q)
    parts = []
    for c in range(tiles // LANES):
        rows = []
        for h in range(groups):
            block = None
            for b in range(groups):
                piece = turn(load(c * groups + b), (b - h) * q)
                block = piece if block is None else jnp.where(group == b, piece, block)
            rows.append(block)
        parts.append(jnp.concatenate(rows, axis=0).T)
    stacked = jnp.concatenate(parts, axis=0)
    return sum(bf16_dot(perm, part) for part in reversed(split3(stacked)))


def crossing_order(me, match):
    tiles = match.shape[1]
    slot = lax.broadcasted_iota(jnp.int32, (1, tiles), 1)
    peer = match // tiles
    other = match - peer * tiles
    inner = jnp.where(
        peer == me,
        jnp.minimum(slot, other) + jnp.where(slot > other, tiles, 0),
        jnp.where(peer > me, slot, other),
    )
    key = (peer * (2 * tiles) + inner).astype(jnp.float32)
    key_cols = jnp.broadcast_to(key, (LANES, tiles)).T[:, :1]
    place = jnp.sum(jnp.where(key < key_cols, 1.0, 0.0), axis=1, keepdims=True)
    cols = lax.broadcasted_iota(jnp.int32, (tiles, tiles), 1).astype(jnp.float32)
    return jnp.where(place == cols, 1.0, 0.0).astype(jnp.bfloat16)


def order_kernel(q, me_ref, match_hbm, obs_hbm, obs_out, match_ref, obs_ref, sems):
    copies = [
        pltpu.make_async_copy(match_hbm, match_ref, sems.at[0]),
        pltpu.make_async_copy(obs_hbm, obs_ref, sems.at[1]),
    ]
    for copy in copies:
        copy.start()
    copies[0].wait()
    perm = crossing_order(me_ref[0], match_ref[...])
    copies[1].wait()

    def put(_, index, block):
        obs_out[index * q : (index + 1) * q, :] = block

    to_crossing([obs_ref[...]], perm, q, put)


def jac_kernel(
    q,
    together,
    me_ref,
    match_hbm,
    knot_hbm,
    frac_hbm,
    sent_hbm,
    jac_hbm,
    perm_ref,
    weight_ref,
    edge_ref,
    sent_ref,
    out_ref,
    match_ref,
    knot_ref,
    frac_ref,
    jac_ref,
    sems,
):
    params, tiles, _ = jac_ref.shape
    pairs = [(match_hbm, match_ref), (knot_hbm, knot_ref), (frac_hbm, frac_ref)]
    pairs += [(jac_hbm.at[p], jac_ref.at[p]) for p in range(params)]
    pairs += [(sent_hbm, sent_ref)]
    copies = [
        pltpu.make_async_copy(source, target, sems.at[index])
        for index, (source, target) in enumerate(pairs)
    ]
    for copy in copies:
        copy.start()
    for copy in copies[:3]:
        copy.wait()
    perm = crossing_order(me_ref[0], match_ref[...])
    perm_ref[...] = perm

    row = lax.broadcasted_iota(jnp.int32, (SUB, tiles), 0)
    facts = jnp.where(row == 0, knot_ref[...].astype(jnp.float32), frac_ref[...])
    moved = sum(bf16_dot(part, perm) for part in reversed(split3(facts)))
    knot, frac = moved[0:1], moved[1:2]
    knots = lax.broadcasted_iota(jnp.int32, (KNOT_DEV, tiles), 0).astype(jnp.float32)
    main = jnp.where(knots == knot, 1.0 - frac, 0.0) + jnp.where(knots == knot + 1.0, frac, 0.0)
    first_row = lax.broadcasted_iota(jnp.int32, (PAD, tiles), 0) == 0
    edge = jnp.where(first_row, jnp.where(knot == KNOT_DEV - 1.0, frac, 0.0), 0.0)
    edge_ref[...] = edge[0:SUB]
    for index, (upper, lower) in enumerate(zip(split3(main), split3(edge))):
        weight_ref[index, 0:KNOT_DEV, :] = upper
        weight_ref[index, KNOT_DEV : KNOT_DEV + PAD, :] = lower

    for first in range(0, params, together):
        for p in range(first, first + together):
            copies[3 + p].wait()

        def put(index, block_index, block):
            out_ref[first + index, block_index * q : (block_index + 1) * q, :] = block

        to_crossing([jac_ref[p] for p in range(first, first + together)], perm, q, put)
    copies[3 + params].wait()


def weight_dot(x, parts, over_tiles):
    dims = (((1,), (1 if over_tiles else 0,)), ((), ()))
    stacked = jnp.concatenate(split3(x), axis=0)
    first, second, third = (
        lax.dot_general(
            stacked[0 : (3 - index) * PAD], part, dims, preferred_element_type=jnp.float32
        )
        for index, part in enumerate(parts)
    )
    small = third + second[PAD : 2 * PAD] + first[2 * PAD : 3 * PAD]
    return (small + (second[0:PAD] + first[PAD : 2 * PAD])) + first[0:PAD]


def row_sums(parts):
    row = lax.broadcasted_iota(jnp.int32, (SUB, LANES), 0)
    level = list(parts)
    zero = jnp.zeros((SUB, LANES), jnp.float32)
    while len(level) % SUB:
        level.append(zero)
    for distance in (1, 2, 4):
        first = (row // distance) % 2 == 0
        level = [
            jnp.where(first, a, b) + pltpu.roll(jnp.where(first, b, a), distance, 0)
            for a, b in zip(level[::2], level[1::2])
        ]
    return level[0] if len(level) == 1 else jnp.concatenate(level, axis=0)


def fold_rows(x):
    total = x[0:SUB]
    for step in range(1, x.shape[0] // SUB):
        total = total + x[step * SUB : (step + 1) * SUB]
    return total


def fold_lanes(x, q):
    shift = q
    while shift < LANES:
        x = x + pltpu.roll(x, shift, 1)
        shift *= 2
    return x


def crossing_values(me, arrived_ref, out_ref, q):
    out_ref[...] = arrived_ref[...]
    own = arrived_ref[pl.ds(pl.multiple_of(me * q, SUB), q), :]
    lane = lax.broadcasted_iota(jnp.int32, (q, LANES), 1)
    swapped = jnp.where(lane % q < q // 2, turn(own, -(q // 2)), turn(own, q // 2))
    out_ref[pl.ds(pl.multiple_of(me * q, SUB), q), :] = swapped


def difference(me, sent_ref, arrived_ref, out_ref, q):
    crossing_values(me, arrived_ref, out_ref, q)
    out_ref[...] = sent_ref[...] - out_ref[...]


def adjoint_kernel(
    q, me_ref, sent_ref, arrived_ref, jac_ref, weight_ref, diff_ref, send_ref, values_ref
):
    params, tiles, _ = jac_ref.shape
    difference(me_ref[0], sent_ref, arrived_ref, diff_ref, q)
    groups = LANES // q
    group = lane_group((PAD, LANES), q)
    for c in range(tiles // LANES):
        values = None
        for i in range(groups):
            rows = slice((c * groups + i) * q, (c * groups + i + 1) * q)
            diff = diff_ref[rows, :]
            sums = fold_lanes(
                row_sums([fold_rows(jac_ref[p, rows, :] * diff) for p in range(params)]), q
            )
            values = sums if values is None else jnp.where(group == i, sums, values)
        values_ref[:, c * LANES : (c + 1) * LANES] = values
    spread = weight_dot(values_ref[...], [weight_ref[index] for index in range(3)], True)
    lane = lax.broadcasted_iota(jnp.int32, (PAD, LANES), 1)
    row = lax.broadcasted_iota(jnp.int32, (PAD, LANES), 0)
    spill = jnp.sum(
        jnp.where(lane == row, spread[:, KNOT_DEV : KNOT_DEV + 1], 0.0), axis=0, keepdims=True
    )
    block = jnp.where(row < params, spread[:, :KNOT_DEV], jnp.where(row == params, spill, 0.0))
    for d in range(send_ref.shape[0]):
        send_ref[d] = block


def field_sums(gathered_ref, n_track, n_det, params, store, base=0):
    lane = lax.broadcasted_iota(jnp.int32, (PAD, LANES), 1)
    row = lax.broadcasted_iota(jnp.int32, (PAD, LANES), 0)
    spill = jnp.zeros((PAD, 1), jnp.float32)
    for b in range(n_track):
        total = gathered_ref[b * n_det, base : base + PAD, :]
        for d in range(1, n_det):
            total = total + gathered_ref[b * n_det + d, base : base + PAD, :]
        field = jnp.where(row < params, total, 0.0)
        field = field + jnp.where(lane == 0, spill, 0.0)
        store(b, field)
        spill = jnp.sum(
            jnp.where((lane == row) & (row < params), total[params : params + 1], 0.0),
            axis=1,
            keepdims=True,
        )


def total_of(x):
    return jnp.sum(jnp.sum(x, axis=0), keepdims=True).reshape(1, 1)


def full_dot(a_ref, b_ref):
    total = a_ref[0] * b_ref[0]
    for b in range(1, a_ref.shape[0]):
        total = total + a_ref[b] * b_ref[b]
    return jnp.sum(total, keepdims=True)


def predict(me, q, direction_ref, jac_ref, weight_ref, edge_ref, interp_ref, sent_ref):
    params, tiles, _ = jac_ref.shape
    n_track = direction_ref.shape[0]
    following = direction_ref[jnp.minimum(me + 1, n_track - 1)][:, 0:1]
    following = jnp.where(me + 1 < n_track, following, 0.0)
    parts = [weight_ref[index, 0:KNOT_DEV, :] for index in range(3)]
    interp = weight_dot(direction_ref[me], parts, False) + following * edge_ref[0:1, :]
    groups = LANES // q
    group = lane_group((PAD, LANES), q)
    for c in range(tiles // LANES):
        chunk = interp[:, c * LANES : (c + 1) * LANES]
        for i in range(groups):
            wide = None
            for h in range(groups):
                piece = turn(chunk, (h - i) * q)
                wide = piece if wide is None else jnp.where(group == h, piece, wide)
            interp_ref[c * groups + i] = wide

    def block_values(b, carry):
        rows = pl.ds(pl.multiple_of(b * q, SUB), q)
        interp = interp_ref[b]
        total = jac_ref[0, rows, :] * interp[0:1]
        for p in range(1, params):
            total = total + jac_ref[p, rows, :] * interp[p : p + 1]
        sent_ref[rows, :] = total
        return carry

    lax.fori_loop(0, tiles // q, block_values, 0)


def first_kernel(
    q,
    n_det,
    me_ref,
    gathered_ref,
    jac_ref,
    weight_ref,
    edge_ref,
    grad_ref,
    norm_ref,
    sent_ref,
    interp_ref,
):
    n_track = grad_ref.shape[0]

    def put(b, field):
        grad_ref[b] = field

    field_sums(gathered_ref, n_track, n_det, jac_ref.shape[0], put)
    norm_ref[...] = jnp.broadcast_to(full_dot(grad_ref, grad_ref), norm_ref.shape)
    predict(me_ref[0], q, grad_ref, jac_ref, weight_ref, edge_ref, interp_ref, sent_ref)


def step_kernel(
    q,
    n_det,
    me_ref,
    gathered_ref,
    jac_ref,
    weight_ref,
    edge_ref,
    grad_ref,
    direction_ref,
    norm_ref,
    knot_ref,
    grad_out,
    direction_out,
    norm_out,
    knot_out,
    length_out,
    sent_ref,
    image_ref,
    interp_ref,
):
    n_track = grad_ref.shape[0]
    me = me_ref[0]

    def put(b, field):
        image_ref[b] = field + damping * direction_ref[b]

    field_sums(gathered_ref, n_track, n_det, jac_ref.shape[0], put)
    norm = norm_ref[0:1, 0:1]
    length = norm / full_dot(direction_ref, image_ref)
    length_out[...] = jnp.broadcast_to(length, length_out.shape)
    knot_out[...] = knot_ref[...] + length * direction_ref[me]
    for b in range(n_track):
        grad_out[b] = grad_ref[b] - length * image_ref[b]
    new_norm = full_dot(grad_out, grad_out)
    norm_out[...] = jnp.broadcast_to(new_norm, norm_out.shape)
    ratio = new_norm / norm
    for b in range(n_track):
        direction_out[b] = grad_out[b] + ratio * direction_ref[b]
    predict(me, q, direction_out, jac_ref, weight_ref, edge_ref, interp_ref, sent_ref)


def last_kernel(q, me_ref, sent_ref, arrived_ref, diff_ref, send_ref):
    difference(me_ref[0], sent_ref, arrived_ref, diff_ref, q)
    diff = diff_ref[...]
    squares = jnp.sum(diff * diff, axis=0, keepdims=True)
    send_ref[...] = jnp.broadcast_to(squares[None], send_ref.shape)


def restore_kernel(q, perm_ref, misfit_ref, diff_ref, *refs):
    steps = (len(refs) - 3) // 2
    residual_out, diff_out, residual_ref = refs[2 * steps :]
    tiles = misfit_ref.shape[0]
    residual = misfit_ref[...]
    for length_ref, change_ref in zip(refs[:steps], refs[steps : 2 * steps]):
        residual = residual - length_ref[0:1, 0:1] * change_ref[...]
    residual_ref[...] = residual
    for source, target in ((residual_ref, residual_out), (diff_ref, diff_out)):
        target[...] = from_crossing(
            lambda index: source[index * q : (index + 1) * q, :], perm_ref[...], q, tiles
        )


def finish_kernel(
    me_ref, squares_ref, direction_ref, norm_ref, knot_ref, residual_ref, diff_ref, knot_out, residual_out
):
    params = knot_out.shape[0]
    squares = squares_ref[0]
    for d in range(1, squares_ref.shape[0]):
        squares = squares + squares_ref[d]
    curvature = 0.5 * jnp.sum(squares, keepdims=True) + damping * full_dot(
        direction_ref, direction_ref
    )
    length = norm_ref[0:1, 0:1] / curvature
    knot = knot_ref[...] + length * direction_ref[me_ref[0]]
    knot_out[...] = knot[0:params]
    residual_out[...] = residual_ref[...] - length * diff_ref[...]


def call(kernel, outs, ins, scratch=()):
    return pl.pallas_call(
        kernel,
        out_shape=outs,
        in_specs=ins,
        out_specs=jax.tree.map(lambda _: VMEM, outs),
        scratch_shapes=list(scratch),
        compiler_params=PARAMS,
    )


def local(jac, obs, match, tile_knot, tile_frac):
    tiles, params, columns = jac.shape
    n_track = lax.axis_size("track")
    n_det = lax.axis_size("det")
    n_all = n_track * n_det
    q = tiles // n_track
    me = lax.axis_index("track").astype(jnp.int32).reshape(1)

    def crossing(values):
        return lax.all_to_all(values, "track", split_axis=0, concat_axis=0, tiled=True)

    def everywhere(values):
        return lax.all_to_all(values, ("track", "det"), split_axis=0, concat_axis=0, tiled=True)

    match_row = from_hbm(match[None])
    row_scratch = [pltpu.VMEM((1, tiles), jnp.int32)] * 2 + [pltpu.VMEM((1, tiles), jnp.float32)]
    sent = call(
        functools.partial(order_kernel, q),
        f32(tiles, columns),
        [SMEM, ANY, ANY],
        [
            row_scratch[0],
            pltpu.VMEM((tiles, columns), jnp.float32),
            pltpu.SemaphoreType.DMA((2,)),
        ],
    )(me, match_row, from_hbm(obs))
    arrived = crossing(sent)
    perm, weights, edge, sent, jac_rows = call(
        functools.partial(jac_kernel, q, math.gcd(params, 3)),
        (
            kept((tiles, tiles), jnp.bfloat16),
            kept((3, KNOT_DEV + PAD, tiles), jnp.bfloat16),
            kept((SUB, tiles)),
            kept((tiles, columns)),
            kept((params, tiles, columns)),
        ),
        [SMEM] + [ANY] * 5,
        row_scratch
        + [
            pltpu.VMEM((params, tiles, columns), jnp.float32),
            pltpu.SemaphoreType.DMA((4 + params,)),
        ],
    )(
        me,
        match_row,
        from_hbm(tile_knot[None]),
        from_hbm(tile_frac[None]),
        from_hbm(sent),
        from_hbm(jnp.transpose(jac, (1, 0, 2))),
    )

    def adjoint(sent, arrived):
        diff, payload = call(
            functools.partial(adjoint_kernel, q),
            (f32(tiles, columns), f32(n_all, PAD, LANES)),
            [SMEM] + [VMEM] * 4,
            [pltpu.VMEM((PAD, tiles), jnp.float32)],
        )(me, sent, arrived, jac_rows, weights)
        return diff, everywhere(payload)

    field = f32(n_track, PAD, LANES)
    scalar = f32(SUB, LANES)
    interp = pltpu.VMEM((n_track, PAD, LANES), jnp.float32)
    misfit, gathered = adjoint(sent, arrived)
    gradient, slope_norm, sent = call(
        functools.partial(first_kernel, q, n_det),
        (field, scalar, f32(tiles, columns)),
        [SMEM] + [VMEM] * 4,
        [interp],
    )(me, gathered, jac_rows, weights, edge)
    direction = gradient
    knot_field = jnp.zeros((PAD, KNOT_DEV), jnp.float32)
    lengths, changes = [], []
    for iteration in range(ITERS - 1):
        change, gathered = adjoint(sent, crossing(sent))
        gradient, direction, slope_norm, knot_field, length, sent = call(
            functools.partial(step_kernel, q, n_det),
            (field, field, scalar, f32(PAD, KNOT_DEV), scalar, f32(tiles, columns)),
            [SMEM] + [VMEM] * 8,
            [pltpu.VMEM((n_track, PAD, LANES), jnp.float32), interp],
        )(
            me, gathered, jac_rows, weights, edge, gradient, direction, slope_norm, knot_field
        )
        lengths.append(length)
        changes.append(change)
    change, squares = call(
        functools.partial(last_kernel, q),
        (f32(tiles, columns), f32(n_all, 1, LANES)),
        [SMEM] + [VMEM] * 2,
    )(me, sent, crossing(sent))
    squares = everywhere(squares)
    residual, change = call(
        functools.partial(restore_kernel, q),
        (f32(tiles, columns), f32(tiles, columns)),
        [VMEM] * (3 + 2 * len(changes)),
        [pltpu.VMEM((tiles, columns), jnp.float32)],
    )(perm, misfit, change, *lengths, *changes)
    return call(
        finish_kernel,
        (f32(params, KNOT_DEV), f32(tiles, columns)),
        [SMEM] + [VMEM] * 6,
    )(me, squares, direction, slope_norm, knot_field, residual, change)


def solution(mesh):
    in_specs = (P("track", None, "det"), P("track", "det"), P("track"), P("track"), P("track"))
    out_specs = (P(None, "track"), P("track", "det"))
    return jax.shard_map(local, mesh=mesh, in_specs=in_specs, out_specs=out_specs, check_vma=False)
```

```python
import functools
import math

import jax
import jax.numpy as jnp
from jax import lax
from jax.experimental import pallas as pl
from jax.experimental.pallas import tpu as pltpu
from jax.sharding import PartitionSpec as P

KNOT_DEV = 128
ITERS = 4
LANES = 128
SUB = 8
PAD = 16
VMEM_BYTES = 14 * 2**20


damping = 1.0

SMEM = pl.BlockSpec(memory_space=pltpu.SMEM)
VMEM = pl.BlockSpec(memory_space=pltpu.VMEM)
ANY = pl.BlockSpec(memory_space=pl.ANY)
PARAMS = pltpu.CompilerParams(vmem_limit_bytes=VMEM_BYTES)
HIGHEST = lax.Precision.HIGHEST


def kept(shape, dtype=jnp.float32):
    return pltpu.VMEM(shape, dtype)


def from_hbm(x):
    return pltpu.with_memory_space_constraint(x, pltpu.HBM)


def in_vmem(*arrays):
    return [pltpu.with_memory_space_constraint(x, pltpu.VMEM) for x in arrays]


def f32(*shape):
    return jax.ShapeDtypeStruct(shape, jnp.float32)


def dot(a, b, dims):
    return lax.dot_general(
        a, b, (dims, ((), ())), precision=HIGHEST, preferred_element_type=jnp.float32
    )


def split3(x):
    first = x.astype(jnp.bfloat16)
    rest = x - first.astype(jnp.float32)
    second = rest.astype(jnp.bfloat16)
    third = (rest - second.astype(jnp.float32)).astype(jnp.bfloat16)
    return first, second, third


def bf16_dot(a, b):
    return jnp.dot(a, b, preferred_element_type=jnp.float32)


def turn(x, shift):
    shift = shift % LANES
    return x if shift == 0 else pltpu.roll(x, shift, 1)


def lane_group(shape, q):
    return lax.broadcasted_iota(jnp.int32, shape, 1) // q


def to_crossing(arrays, perm, q, store):
    tiles = arrays[0].shape[0]
    groups = LANES // q
    stacked = []
    for x in arrays:
        across = jnp.concatenate(
            [x[c * LANES : (c + 1) * LANES].T for c in range(tiles // LANES)], axis=1
        )
        stacked.extend(split3(across))
    moved = bf16_dot(jnp.concatenate(stacked, axis=0), perm)
    group = lane_group((q, LANES), q)
    for index in range(len(arrays)):
        third, second, first = (
            moved[(3 * index + part) * LANES : (3 * index + part + 1) * LANES] for part in (2, 1, 0)
        )
        whole = third + second + first
        for c in range(tiles // LANES):
            for b in range(groups):
                block = None
                for h in range(groups):
                    piece = turn(
                        whole[h * q : (h + 1) * q, c * LANES : (c + 1) * LANES], (h - b) * q
                    )
                    block = piece if block is None else jnp.where(group == h, piece, block)
                store(index, c * groups + b, block)


def from_crossing(load, perm, q, tiles):
    groups = LANES // q
    group = lane_group((q, LANES), q)
    parts = []
    for c in range(tiles // LANES):
        rows = []
        for h in range(groups):
            block = None
            for b in range(groups):
                piece = turn(load(c * groups + b), (b - h) * q)
                block = piece if block is None else jnp.where(group == b, piece, block)
            rows.append(block)
        parts.append(jnp.concatenate(rows, axis=0).T)
    stacked = jnp.concatenate(parts, axis=0)
    return sum(bf16_dot(perm, part) for part in reversed(split3(stacked)))


def crossing_order(me, match):
    tiles = match.shape[1]
    slot = lax.broadcasted_iota(jnp.int32, (1, tiles), 1)
    peer = match // tiles
    other = match - peer * tiles
    inner = jnp.where(
        peer == me,
        jnp.minimum(slot, other) + jnp.where(slot > other, tiles, 0),
        jnp.where(peer > me, slot, other),
    )
    key = (peer * (2 * tiles) + inner).astype(jnp.float32)
    key_cols = jnp.broadcast_to(key, (LANES, tiles)).T[:, :1]
    place = jnp.sum(jnp.where(key < key_cols, 1.0, 0.0), axis=1, keepdims=True)
    cols = lax.broadcasted_iota(jnp.int32, (tiles, tiles), 1).astype(jnp.float32)
    return jnp.where(place == cols, 1.0, 0.0).astype(jnp.bfloat16)


def order_kernel(q, me_ref, match_hbm, obs_hbm, obs_out, match_ref, obs_ref, sems):
    copies = [
        pltpu.make_async_copy(match_hbm, match_ref, sems.at[0]),
        pltpu.make_async_copy(obs_hbm, obs_ref, sems.at[1]),
    ]
    for copy in copies:
        copy.start()
    copies[0].wait()
    perm = crossing_order(me_ref[0], match_ref[...])
    copies[1].wait()

    def put(_, index, block):
        obs_out[index * q : (index + 1) * q, :] = block

    to_crossing([obs_ref[...]], perm, q, put)


def jac_kernel(
    q,
    together,
    me_ref,
    match_hbm,
    knot_hbm,
    frac_hbm,
    sent_hbm,
    jac_hbm,
    perm_ref,
    weight_ref,
    edge_ref,
    sent_ref,
    out_ref,
    match_ref,
    knot_ref,
    frac_ref,
    jac_ref,
    sems,
):
    params, tiles, _ = jac_ref.shape
    pairs = [(match_hbm, match_ref), (knot_hbm, knot_ref), (frac_hbm, frac_ref)]
    pairs += [(jac_hbm.at[p], jac_ref.at[p]) for p in range(params)]
    pairs += [(sent_hbm, sent_ref)]
    copies = [
        pltpu.make_async_copy(source, target, sems.at[index])
        for index, (source, target) in enumerate(pairs)
    ]
    for copy in copies:
        copy.start()
    for copy in copies[:3]:
        copy.wait()
    perm = crossing_order(me_ref[0], match_ref[...])
    perm_ref[...] = perm

    row = lax.broadcasted_iota(jnp.int32, (SUB, tiles), 0)
    facts = jnp.where(row == 0, knot_ref[...].astype(jnp.float32), frac_ref[...])
    moved = sum(bf16_dot(part, perm) for part in reversed(split3(facts)))
    knot, frac = moved[0:1], moved[1:2]
    knots = lax.broadcasted_iota(jnp.int32, (KNOT_DEV, tiles), 0).astype(jnp.float32)
    main = jnp.where(knots == knot, 1.0 - frac, 0.0) + jnp.where(knots == knot + 1.0, frac, 0.0)
    first_row = lax.broadcasted_iota(jnp.int32, (PAD, tiles), 0) == 0
    edge = jnp.where(first_row, jnp.where(knot == KNOT_DEV - 1.0, frac, 0.0), 0.0)
    edge_ref[...] = edge[0:SUB]
    for index, (upper, lower) in enumerate(zip(split3(main), split3(edge))):
        weight_ref[index, 0:KNOT_DEV, :] = upper
        weight_ref[index, KNOT_DEV : KNOT_DEV + PAD, :] = lower

    for first in range(0, params, together):
        for p in range(first, first + together):
            copies[3 + p].wait()

        def put(index, block_index, block):
            out_ref[first + index, block_index * q : (block_index + 1) * q, :] = block

        to_crossing([jac_ref[p] for p in range(first, first + together)], perm, q, put)
    copies[3 + params].wait()


def weight_dot(x, parts, over_tiles):
    dims = (((1,), (1 if over_tiles else 0,)), ((), ()))
    stacked = jnp.concatenate(split3(x), axis=0)
    first, second, third = (
        lax.dot_general(
            stacked[0 : (3 - index) * PAD], part, dims, preferred_element_type=jnp.float32
        )
        for index, part in enumerate(parts)
    )
    small = third + second[PAD : 2 * PAD] + first[2 * PAD : 3 * PAD]
    return (small + (second[0:PAD] + first[PAD : 2 * PAD])) + first[0:PAD]


def row_sums(parts):
    row = lax.broadcasted_iota(jnp.int32, (SUB, LANES), 0)
    level = list(parts)
    zero = jnp.zeros((SUB, LANES), jnp.float32)
    while len(level) % SUB:
        level.append(zero)
    for distance in (1, 2, 4):
        first = (row // distance) % 2 == 0
        level = [
            jnp.where(first, a, b) + pltpu.roll(jnp.where(first, b, a), distance, 0)
            for a, b in zip(level[::2], level[1::2])
        ]
    return level[0] if len(level) == 1 else jnp.concatenate(level, axis=0)


def fold_rows(x):
    total = x[0:SUB]
    for step in range(1, x.shape[0] // SUB):
        total = total + x[step * SUB : (step + 1) * SUB]
    return total


def fold_lanes(x, q):
    shift = q
    while shift < LANES:
        x = x + pltpu.roll(x, shift, 1)
        shift *= 2
    return x


def crossing_values(me, arrived_ref, out_ref, q):
    out_ref[...] = arrived_ref[...]
    own = arrived_ref[pl.ds(pl.multiple_of(me * q, SUB), q), :]
    lane = lax.broadcasted_iota(jnp.int32, (q, LANES), 1)
    swapped = jnp.where(lane % q < q // 2, turn(own, -(q // 2)), turn(own, q // 2))
    out_ref[pl.ds(pl.multiple_of(me * q, SUB), q), :] = swapped


def difference(me, sent_ref, arrived_ref, out_ref, q):
    crossing_values(me, arrived_ref, out_ref, q)
    out_ref[...] = sent_ref[...] - out_ref[...]


def adjoint_kernel(
    q, me_ref, sent_ref, arrived_ref, jac_ref, weight_ref, diff_ref, send_ref, values_ref
):
    params, tiles, _ = jac_ref.shape
    difference(me_ref[0], sent_ref, arrived_ref, diff_ref, q)
    groups = LANES // q
    group = lane_group((PAD, LANES), q)
    for c in range(tiles // LANES):
        values = None
        for i in range(groups):
            rows = slice((c * groups + i) * q, (c * groups + i + 1) * q)
            diff = diff_ref[rows, :]
            sums = fold_lanes(
                row_sums([fold_rows(jac_ref[p, rows, :] * diff) for p in range(params)]), q
            )
            values = sums if values is None else jnp.where(group == i, sums, values)
        values_ref[:, c * LANES : (c + 1) * LANES] = values
    spread = weight_dot(values_ref[...], [weight_ref[index] for index in range(3)], True)
    lane = lax.broadcasted_iota(jnp.int32, (PAD, LANES), 1)
    row = lax.broadcasted_iota(jnp.int32, (PAD, LANES), 0)
    spill = jnp.sum(
        jnp.where(lane == row, spread[:, KNOT_DEV : KNOT_DEV + 1], 0.0), axis=0, keepdims=True
    )
    block = jnp.where(row < params, spread[:, :KNOT_DEV], jnp.where(row == params, spill, 0.0))
    for d in range(send_ref.shape[0]):
        send_ref[d] = block


def field_sums(gathered_ref, n_track, n_det, params, store, base=0):
    lane = lax.broadcasted_iota(jnp.int32, (PAD, LANES), 1)
    row = lax.broadcasted_iota(jnp.int32, (PAD, LANES), 0)
    spill = jnp.zeros((PAD, 1), jnp.float32)
    for b in range(n_track):
        total = gathered_ref[b * n_det, base : base + PAD, :]
        for d in range(1, n_det):
            total = total + gathered_ref[b * n_det + d, base : base + PAD, :]
        field = jnp.where(row < params, total, 0.0)
        field = field + jnp.where(lane == 0, spill, 0.0)
        store(b, field)
        spill = jnp.sum(
            jnp.where((lane == row) & (row < params), total[params : params + 1], 0.0),
            axis=1,
            keepdims=True,
        )


def total_of(x):
    return jnp.sum(jnp.sum(x, axis=0), keepdims=True).reshape(1, 1)


def full_dot(a_ref, b_ref):
    total = a_ref[0] * b_ref[0]
    for b in range(1, a_ref.shape[0]):
        total = total + a_ref[b] * b_ref[b]
    return jnp.sum(total, keepdims=True)


def predict(me, q, direction_ref, jac_ref, weight_ref, edge_ref, interp_ref, sent_ref):
    params, tiles, _ = jac_ref.shape
    n_track = direction_ref.shape[0]
    following = direction_ref[jnp.minimum(me + 1, n_track - 1)][:, 0:1]
    following = jnp.where(me + 1 < n_track, following, 0.0)
    parts = [weight_ref[index, 0:KNOT_DEV, :] for index in range(3)]
    interp = weight_dot(direction_ref[me], parts, False) + following * edge_ref[0:1, :]
    groups = LANES // q
    group = lane_group((PAD, LANES), q)
    for c in range(tiles // LANES):
        chunk = interp[:, c * LANES : (c + 1) * LANES]
        for i in range(groups):
            wide = None
            for h in range(groups):
                piece = turn(chunk, (h - i) * q)
                wide = piece if wide is None else jnp.where(group == h, piece, wide)
            interp_ref[c * groups + i] = wide

    def block_values(b, carry):
        rows = pl.ds(pl.multiple_of(b * q, SUB), q)
        interp = interp_ref[b]
        total = jac_ref[0, rows, :] * interp[0:1]
        for p in range(1, params):
            total = total + jac_ref[p, rows, :] * interp[p : p + 1]
        sent_ref[rows, :] = total
        return carry

    lax.fori_loop(0, tiles // q, block_values, 0)


def first_kernel(
    q,
    n_det,
    me_ref,
    gathered_ref,
    jac_ref,
    weight_ref,
    edge_ref,
    grad_ref,
    norm_ref,
    sent_ref,
    interp_ref,
):
    n_track = grad_ref.shape[0]

    def put(b, field):
        grad_ref[b] = field

    field_sums(gathered_ref, n_track, n_det, jac_ref.shape[0], put)
    norm_ref[...] = jnp.broadcast_to(full_dot(grad_ref, grad_ref), norm_ref.shape)
    predict(me_ref[0], q, grad_ref, jac_ref, weight_ref, edge_ref, interp_ref, sent_ref)


def step_kernel(
    q,
    n_det,
    me_ref,
    gathered_ref,
    jac_ref,
    weight_ref,
    edge_ref,
    grad_ref,
    direction_ref,
    norm_ref,
    knot_ref,
    grad_out,
    direction_out,
    norm_out,
    knot_out,
    length_out,
    sent_ref,
    image_ref,
    interp_ref,
):
    n_track = grad_ref.shape[0]
    me = me_ref[0]

    def put(b, field):
        image_ref[b] = field + damping * direction_ref[b]

    field_sums(gathered_ref, n_track, n_det, jac_ref.shape[0], put)
    norm = norm_ref[0:1, 0:1]
    length = norm / full_dot(direction_ref, image_ref)
    length_out[...] = jnp.broadcast_to(length, length_out.shape)
    knot_out[...] = knot_ref[...] + length * direction_ref[me]
    for b in range(n_track):
        grad_out[b] = grad_ref[b] - length * image_ref[b]
    new_norm = full_dot(grad_out, grad_out)
    norm_out[...] = jnp.broadcast_to(new_norm, norm_out.shape)
    ratio = new_norm / norm
    for b in range(n_track):
        direction_out[b] = grad_out[b] + ratio * direction_ref[b]
    predict(me, q, direction_out, jac_ref, weight_ref, edge_ref, interp_ref, sent_ref)


def last_kernel(q, me_ref, sent_ref, arrived_ref, diff_ref, send_ref):
    difference(me_ref[0], sent_ref, arrived_ref, diff_ref, q)
    diff = diff_ref[...]
    squares = jnp.sum(diff * diff, axis=0, keepdims=True)
    send_ref[...] = jnp.broadcast_to(squares[None], send_ref.shape)


def restore_kernel(q, perm_ref, misfit_ref, diff_ref, *refs):
    steps = (len(refs) - 3) // 2
    residual_out, diff_out, residual_ref = refs[2 * steps :]
    tiles = misfit_ref.shape[0]
    residual = misfit_ref[...]
    for length_ref, change_ref in zip(refs[:steps], refs[steps : 2 * steps]):
        residual = residual - length_ref[0:1, 0:1] * change_ref[...]
    residual_ref[...] = residual
    for source, target in ((residual_ref, residual_out), (diff_ref, diff_out)):
        target[...] = from_crossing(
            lambda index: source[index * q : (index + 1) * q, :], perm_ref[...], q, tiles
        )


def finish_kernel(
    me_ref, squares_ref, direction_ref, norm_ref, knot_ref, residual_ref, diff_ref, knot_out, residual_out
):
    params = knot_out.shape[0]
    squares = squares_ref[0]
    for d in range(1, squares_ref.shape[0]):
        squares = squares + squares_ref[d]
    curvature = 0.5 * jnp.sum(squares, keepdims=True) + damping * full_dot(
        direction_ref, direction_ref
    )
    length = norm_ref[0:1, 0:1] / curvature
    knot = knot_ref[...] + length * direction_ref[me_ref[0]]
    knot_out[...] = knot[0:params]
    residual_out[...] = residual_ref[...] - length * diff_ref[...]


def call(kernel, outs, ins, scratch=()):
    return pl.pallas_call(
        kernel,
        out_shape=outs,
        in_specs=ins,
        out_specs=jax.tree.map(lambda _: VMEM, outs),
        scratch_shapes=list(scratch),
        compiler_params=PARAMS,
    )


def local(jac, obs, match, tile_knot, tile_frac):
    tiles, params, columns = jac.shape
    n_track = lax.axis_size("track")
    n_det = lax.axis_size("det")
    n_all = n_track * n_det
    q = tiles // n_track
    me = lax.axis_index("track").astype(jnp.int32).reshape(1)

    def crossing(values):
        return lax.all_to_all(values, "track", split_axis=0, concat_axis=0, tiled=True)

    def everywhere(values):
        return lax.all_to_all(values, ("track", "det"), split_axis=0, concat_axis=0, tiled=True)

    match_row = from_hbm(match[None])
    row_scratch = [pltpu.VMEM((1, tiles), jnp.int32)] * 2 + [pltpu.VMEM((1, tiles), jnp.float32)]
    sent = call(
        functools.partial(order_kernel, q),
        f32(tiles, columns),
        [SMEM, ANY, ANY],
        [
            row_scratch[0],
            pltpu.VMEM((tiles, columns), jnp.float32),
            pltpu.SemaphoreType.DMA((2,)),
        ],
    )(me, match_row, from_hbm(obs))
    arrived = crossing(sent)
    perm, weights, edge, sent, jac_rows = call(
        functools.partial(jac_kernel, q, math.gcd(params, 3)),
        (
            kept((tiles, tiles), jnp.bfloat16),
            kept((3, KNOT_DEV + PAD, tiles), jnp.bfloat16),
            kept((SUB, tiles)),
            kept((tiles, columns)),
            kept((params, tiles, columns)),
        ),
        [SMEM] + [ANY] * 5,
        row_scratch
        + [
            pltpu.VMEM((params, tiles, columns), jnp.float32),
            pltpu.SemaphoreType.DMA((4 + params,)),
        ],
    )(
        me,
        match_row,
        from_hbm(tile_knot[None]),
        from_hbm(tile_frac[None]),
        from_hbm(sent),
        from_hbm(jnp.transpose(jac, (1, 0, 2))),
    )

    def adjoint(sent, arrived):
        diff, payload = call(
            functools.partial(adjoint_kernel, q),
            (kept((tiles, columns)), f32(n_all, PAD, LANES)),
            [SMEM] + [VMEM] * 4,
            [pltpu.VMEM((PAD, tiles), jnp.float32)],
        )(me, *in_vmem(sent, arrived, jac_rows, weights))
        return diff, everywhere(payload)

    field = f32(n_track, PAD, LANES)
    scalar = f32(SUB, LANES)
    interp = pltpu.VMEM((n_track, PAD, LANES), jnp.float32)
    misfit, gathered = adjoint(sent, arrived)
    gradient, slope_norm, sent = call(
        functools.partial(first_kernel, q, n_det),
        (field, scalar, f32(tiles, columns)),
        [SMEM] + [VMEM] * 4,
        [interp],
    )(me, *in_vmem(gathered, jac_rows, weights, edge))
    direction = gradient
    knot_field = jnp.zeros((PAD, KNOT_DEV), jnp.float32)
    lengths, changes = [], []
    for iteration in range(ITERS - 1):
        change, gathered = adjoint(sent, crossing(sent))
        gradient, direction, slope_norm, knot_field, length, sent = call(
            functools.partial(step_kernel, q, n_det),
            (field, field, scalar, f32(PAD, KNOT_DEV), scalar, f32(tiles, columns)),
            [SMEM] + [VMEM] * 8,
            [pltpu.VMEM((n_track, PAD, LANES), jnp.float32), interp],
        )(
            me,
            *in_vmem(
                gathered, jac_rows, weights, edge, gradient, direction, slope_norm, knot_field
            ),
        )
        lengths.append(length)
        changes.append(change)
    change, squares = call(
        functools.partial(last_kernel, q),
        (kept((tiles, columns)), f32(n_all, 1, LANES)),
        [SMEM] + [VMEM] * 2,
    )(me, *in_vmem(sent, crossing(sent)))
    squares = everywhere(squares)
    residual, change = call(
        functools.partial(restore_kernel, q),
        (f32(tiles, columns), f32(tiles, columns)),
        [VMEM] * (3 + 2 * len(changes)),
        [pltpu.VMEM((tiles, columns), jnp.float32)],
    )(*in_vmem(perm, misfit, change, *lengths, *changes))
    return call(
        finish_kernel,
        (f32(params, KNOT_DEV), f32(tiles, columns)),
        [SMEM] + [VMEM] * 6,
    )(me, *in_vmem(squares, direction, slope_norm, knot_field, residual, change))


def solution(mesh):
    in_specs = (P("track", None, "det"), P("track", "det"), P("track"), P("track"), P("track"))
    out_specs = (P(None, "track"), P("track", "det"))
    return jax.shard_map(local, mesh=mesh, in_specs=in_specs, out_specs=out_specs, check_vma=False)
```

```python
import functools
import math

import jax
import jax.numpy as jnp
from jax import lax
from jax.experimental import pallas as pl
from jax.experimental.pallas import tpu as pltpu
from jax.sharding import PartitionSpec as P

KNOT_DEV = 128
ITERS = 4
LANES = 128
SUB = 8
PAD = 16
VMEM_BYTES = 14 * 2**20


damping = 1.0

SMEM = pl.BlockSpec(memory_space=pltpu.SMEM)
VMEM = pl.BlockSpec(memory_space=pltpu.VMEM)
ANY = pl.BlockSpec(memory_space=pl.ANY)
PARAMS = pltpu.CompilerParams(vmem_limit_bytes=VMEM_BYTES)
HIGHEST = lax.Precision.HIGHEST


def kept(shape, dtype=jnp.float32):
    return pltpu.VMEM(shape, dtype)


def from_hbm(x):
    return pltpu.with_memory_space_constraint(x, pltpu.HBM)


def f32(*shape):
    return jax.ShapeDtypeStruct(shape, jnp.float32)


def dot(a, b, dims):
    return lax.dot_general(
        a, b, (dims, ((), ())), precision=HIGHEST, preferred_element_type=jnp.float32
    )


def split3(x):
    first = x.astype(jnp.bfloat16)
    rest = x - first.astype(jnp.float32)
    second = rest.astype(jnp.bfloat16)
    third = (rest - second.astype(jnp.float32)).astype(jnp.bfloat16)
    return first, second, third


def bf16_dot(a, b):
    return jnp.dot(a, b, preferred_element_type=jnp.float32)


def turn(x, shift):
    shift = shift % LANES
    return x if shift == 0 else pltpu.roll(x, shift, 1)


def lane_group(shape, q):
    return lax.broadcasted_iota(jnp.int32, shape, 1) // q


def to_crossing(arrays, perm, q, store):
    tiles = arrays[0].shape[0]
    groups = LANES // q
    stacked = []
    for x in arrays:
        across = jnp.concatenate(
            [x[c * LANES : (c + 1) * LANES].T for c in range(tiles // LANES)], axis=1
        )
        stacked.extend(split3(across))
    moved = bf16_dot(jnp.concatenate(stacked, axis=0), perm)
    group = lane_group((q, LANES), q)
    for index in range(len(arrays)):
        third, second, first = (
            moved[(3 * index + part) * LANES : (3 * index + part + 1) * LANES] for part in (2, 1, 0)
        )
        whole = third + second + first
        for c in range(tiles // LANES):
            for b in range(groups):
                block = None
                for h in range(groups):
                    piece = turn(
                        whole[h * q : (h + 1) * q, c * LANES : (c + 1) * LANES], (h - b) * q
                    )
                    block = piece if block is None else jnp.where(group == h, piece, block)
                store(index, c * groups + b, block)


def from_crossing(load, perm, q, tiles):
    groups = LANES // q
    group = lane_group((q, LANES), q)
    parts = []
    for c in range(tiles // LANES):
        rows = []
        for h in range(groups):
            block = None
            for b in range(groups):
                piece = turn(load(c * groups + b), (b - h) * q)
                block = piece if block is None else jnp.where(group == b, piece, block)
            rows.append(block)
        parts.append(jnp.concatenate(rows, axis=0).T)
    stacked = jnp.concatenate(parts, axis=0)
    return sum(bf16_dot(perm, part) for part in reversed(split3(stacked)))


def crossing_order(me, match):
    tiles = match.shape[1]
    slot = lax.broadcasted_iota(jnp.int32, (1, tiles), 1)
    peer = match // tiles
    other = match - peer * tiles
    inner = jnp.where(
        peer == me,
        jnp.minimum(slot, other) + jnp.where(slot > other, tiles, 0),
        jnp.where(peer > me, slot, other),
    )
    key = (peer * (2 * tiles) + inner).astype(jnp.float32)
    key_cols = jnp.broadcast_to(key, (LANES, tiles)).T[:, :1]
    place = jnp.sum(jnp.where(key < key_cols, 1.0, 0.0), axis=1, keepdims=True)
    cols = lax.broadcasted_iota(jnp.int32, (tiles, tiles), 1).astype(jnp.float32)
    return jnp.where(place == cols, 1.0, 0.0).astype(jnp.bfloat16)


def setup_kernel(
    q,
    together,
    me_ref,
    match_hbm,
    knot_hbm,
    frac_hbm,
    obs_hbm,
    jac_hbm,
    perm_ref,
    weight_ref,
    edge_ref,
    sent_ref,
    out_ref,
    match_ref,
    knot_ref,
    frac_ref,
    obs_ref,
    jac_ref,
    sems,
):
    params, tiles, _ = jac_ref.shape
    pairs = [(match_hbm, match_ref), (knot_hbm, knot_ref), (frac_hbm, frac_ref), (obs_hbm, obs_ref)]
    pairs += [(jac_hbm.at[p], jac_ref.at[p]) for p in range(params)]
    copies = [
        pltpu.make_async_copy(source, target, sems.at[index])
        for index, (source, target) in enumerate(pairs)
    ]
    for copy in copies:
        copy.start()
    copies[0].wait()
    perm = crossing_order(me_ref[0], match_ref[...])
    perm_ref[...] = perm
    for copy in copies[1:4]:
        copy.wait()

    row = lax.broadcasted_iota(jnp.int32, (SUB, tiles), 0)
    facts = jnp.where(row == 0, knot_ref[...].astype(jnp.float32), frac_ref[...])
    moved = sum(bf16_dot(part, perm) for part in reversed(split3(facts)))
    knot, frac = moved[0:1], moved[1:2]
    knots = lax.broadcasted_iota(jnp.int32, (KNOT_DEV, tiles), 0).astype(jnp.float32)
    main = jnp.where(knots == knot, 1.0 - frac, 0.0) + jnp.where(knots == knot + 1.0, frac, 0.0)
    first_row = lax.broadcasted_iota(jnp.int32, (PAD, tiles), 0) == 0
    edge = jnp.where(first_row, jnp.where(knot == KNOT_DEV - 1.0, frac, 0.0), 0.0)
    edge_ref[...] = edge[0:SUB]
    for index, (upper, lower) in enumerate(zip(split3(main), split3(edge))):
        weight_ref[index, 0:KNOT_DEV, :] = upper
        weight_ref[index, KNOT_DEV : KNOT_DEV + PAD, :] = lower

    def put_obs(_, index, block):
        sent_ref[index * q : (index + 1) * q, :] = block

    to_crossing([obs_ref[...]], perm, q, put_obs)
    for first in range(0, params, together):
        for p in range(first, first + together):
            copies[4 + p].wait()

        def put(index, block_index, block):
            out_ref[first + index, block_index * q : (block_index + 1) * q, :] = block

        to_crossing([jac_ref[p] for p in range(first, first + together)], perm, q, put)


def weight_dot(x, parts, over_tiles):
    dims = (((1,), (1 if over_tiles else 0,)), ((), ()))
    stacked = jnp.concatenate(split3(x), axis=0)
    first, second, third = (
        lax.dot_general(
            stacked[0 : (3 - index) * PAD], part, dims, preferred_element_type=jnp.float32
        )
        for index, part in enumerate(parts)
    )
    small = third + second[PAD : 2 * PAD] + first[2 * PAD : 3 * PAD]
    return (small + (second[0:PAD] + first[PAD : 2 * PAD])) + first[0:PAD]


def row_sums(parts):
    row = lax.broadcasted_iota(jnp.int32, (SUB, LANES), 0)
    level = list(parts)
    zero = jnp.zeros((SUB, LANES), jnp.float32)
    while len(level) % SUB:
        level.append(zero)
    for distance in (1, 2, 4):
        first = (row // distance) % 2 == 0
        level = [
            jnp.where(first, a, b) + pltpu.roll(jnp.where(first, b, a), distance, 0)
            for a, b in zip(level[::2], level[1::2])
        ]
    return level[0] if len(level) == 1 else jnp.concatenate(level, axis=0)


def fold_rows(x):
    total = x[0:SUB]
    for step in range(1, x.shape[0] // SUB):
        total = total + x[step * SUB : (step + 1) * SUB]
    return total


def fold_lanes(x, q):
    shift = q
    while shift < LANES:
        x = x + pltpu.roll(x, shift, 1)
        shift *= 2
    return x


def crossing_values(me, arrived_ref, out_ref, q):
    out_ref[...] = arrived_ref[...]
    own = arrived_ref[pl.ds(pl.multiple_of(me * q, SUB), q), :]
    lane = lax.broadcasted_iota(jnp.int32, (q, LANES), 1)
    swapped = jnp.where(lane % q < q // 2, turn(own, -(q // 2)), turn(own, q // 2))
    out_ref[pl.ds(pl.multiple_of(me * q, SUB), q), :] = swapped


def difference(me, sent_ref, arrived_ref, out_ref, q):
    crossing_values(me, arrived_ref, out_ref, q)
    out_ref[...] = sent_ref[...] - out_ref[...]


def adjoint_kernel(
    q, me_ref, sent_ref, arrived_ref, jac_ref, weight_ref, diff_ref, send_ref, values_ref
):
    params, tiles, _ = jac_ref.shape
    difference(me_ref[0], sent_ref, arrived_ref, diff_ref, q)
    groups = LANES // q
    group = lane_group((PAD, LANES), q)
    for c in range(tiles // LANES):
        values = None
        for i in range(groups):
            rows = slice((c * groups + i) * q, (c * groups + i + 1) * q)
            diff = diff_ref[rows, :]
            sums = fold_lanes(
                row_sums([fold_rows(jac_ref[p, rows, :] * diff) for p in range(params)]), q
            )
            values = sums if values is None else jnp.where(group == i, sums, values)
        values_ref[:, c * LANES : (c + 1) * LANES] = values
    spread = weight_dot(values_ref[...], [weight_ref[index] for index in range(3)], True)
    lane = lax.broadcasted_iota(jnp.int32, (PAD, LANES), 1)
    row = lax.broadcasted_iota(jnp.int32, (PAD, LANES), 0)
    spill = jnp.sum(
        jnp.where(lane == row, spread[:, KNOT_DEV : KNOT_DEV + 1], 0.0), axis=0, keepdims=True
    )
    block = jnp.where(row < params, spread[:, :KNOT_DEV], jnp.where(row == params, spill, 0.0))
    for d in range(send_ref.shape[0]):
        send_ref[d] = block


def field_sums(gathered_ref, n_track, n_det, params, store, base=0):
    lane = lax.broadcasted_iota(jnp.int32, (PAD, LANES), 1)
    row = lax.broadcasted_iota(jnp.int32, (PAD, LANES), 0)
    spill = jnp.zeros((PAD, 1), jnp.float32)
    for b in range(n_track):
        total = gathered_ref[b * n_det, base : base + PAD, :]
        for d in range(1, n_det):
            total = total + gathered_ref[b * n_det + d, base : base + PAD, :]
        field = jnp.where(row < params, total, 0.0)
        field = field + jnp.where(lane == 0, spill, 0.0)
        store(b, field)
        spill = jnp.sum(
            jnp.where((lane == row) & (row < params), total[params : params + 1], 0.0),
            axis=1,
            keepdims=True,
        )


def total_of(x):
    return jnp.sum(jnp.sum(x, axis=0), keepdims=True).reshape(1, 1)


def full_dot(a_ref, b_ref):
    total = a_ref[0] * b_ref[0]
    for b in range(1, a_ref.shape[0]):
        total = total + a_ref[b] * b_ref[b]
    return jnp.sum(total, keepdims=True)


def predict(me, q, direction_ref, jac_ref, weight_ref, edge_ref, interp_ref, sent_ref):
    params, tiles, _ = jac_ref.shape
    n_track = direction_ref.shape[0]
    following = direction_ref[jnp.minimum(me + 1, n_track - 1)][:, 0:1]
    following = jnp.where(me + 1 < n_track, following, 0.0)
    parts = [weight_ref[index, 0:KNOT_DEV, :] for index in range(3)]
    interp = weight_dot(direction_ref[me], parts, False) + following * edge_ref[0:1, :]
    groups = LANES // q
    group = lane_group((PAD, LANES), q)
    for c in range(tiles // LANES):
        chunk = interp[:, c * LANES : (c + 1) * LANES]
        for i in range(groups):
            wide = None
            for h in range(groups):
                piece = turn(chunk, (h - i) * q)
                wide = piece if wide is None else jnp.where(group == h, piece, wide)
            interp_ref[c * groups + i] = wide

    def block_values(b, carry):
        rows = pl.ds(pl.multiple_of(b * q, SUB), q)
        interp = interp_ref[b]
        total = jac_ref[0, rows, :] * interp[0:1]
        for p in range(1, params):
            total = total + jac_ref[p, rows, :] * interp[p : p + 1]
        sent_ref[rows, :] = total
        return carry

    lax.fori_loop(0, tiles // q, block_values, 0)


def first_kernel(
    q,
    n_det,
    me_ref,
    gathered_ref,
    jac_ref,
    weight_ref,
    edge_ref,
    grad_ref,
    norm_ref,
    sent_ref,
    interp_ref,
):
    n_track = grad_ref.shape[0]

    def put(b, field):
        grad_ref[b] = field

    field_sums(gathered_ref, n_track, n_det, jac_ref.shape[0], put)
    norm_ref[...] = jnp.broadcast_to(full_dot(grad_ref, grad_ref), norm_ref.shape)
    predict(me_ref[0], q, grad_ref, jac_ref, weight_ref, edge_ref, interp_ref, sent_ref)


def step_kernel(
    q,
    n_det,
    me_ref,
    gathered_ref,
    jac_ref,
    weight_ref,
    edge_ref,
    grad_ref,
    direction_ref,
    norm_ref,
    knot_ref,
    direction_out,
    norm_out,
    knot_out,
    length_out,
    sent_ref,
    grad_out,
    image_ref,
    interp_ref,
):
    n_track = grad_ref.shape[0]
    me = me_ref[0]

    def put(b, field):
        image_ref[b] = field + damping * direction_ref[b]

    field_sums(gathered_ref, n_track, n_det, jac_ref.shape[0], put)
    norm = norm_ref[0:1, 0:1]
    length = norm / full_dot(direction_ref, image_ref)
    length_out[...] = jnp.broadcast_to(length, length_out.shape)
    knot_out[...] = knot_ref[...] + length * direction_ref[me]
    for b in range(n_track):
        grad_out[b] = grad_ref[b] - length * image_ref[b]
    new_norm = full_dot(grad_out, grad_out)
    norm_out[...] = jnp.broadcast_to(new_norm, norm_out.shape)
    ratio = new_norm / norm
    for b in range(n_track):
        direction_out[b] = grad_out[b] + ratio * direction_ref[b]
    predict(me, q, direction_out, jac_ref, weight_ref, edge_ref, interp_ref, sent_ref)


def last_kernel(q, me_ref, sent_ref, arrived_ref, diff_ref, send_ref):
    difference(me_ref[0], sent_ref, arrived_ref, diff_ref, q)
    diff = diff_ref[...]
    squares = jnp.sum(diff * diff, axis=0, keepdims=True)
    send_ref[...] = jnp.broadcast_to(squares[None], send_ref.shape)


def restore_kernel(q, perm_ref, misfit_ref, diff_ref, *refs):
    steps = (len(refs) - 3) // 2
    residual_out, diff_out, residual_ref = refs[2 * steps :]
    tiles = misfit_ref.shape[0]
    residual = misfit_ref[...]
    for length_ref, change_ref in zip(refs[:steps], refs[steps : 2 * steps]):
        residual = residual - length_ref[0:1, 0:1] * change_ref[...]
    residual_ref[...] = residual
    for source, target in ((residual_ref, residual_out), (diff_ref, diff_out)):
        target[...] = from_crossing(
            lambda index: source[index * q : (index + 1) * q, :], perm_ref[...], q, tiles
        )


def finish_kernel(
    me_ref, squares_ref, direction_ref, norm_ref, knot_ref, residual_ref, diff_ref, knot_out, residual_out
):
    params = knot_out.shape[0]
    squares = squares_ref[0]
    for d in range(1, squares_ref.shape[0]):
        squares = squares + squares_ref[d]
    curvature = 0.5 * jnp.sum(squares, keepdims=True) + damping * full_dot(
        direction_ref, direction_ref
    )
    length = norm_ref[0:1, 0:1] / curvature
    knot = knot_ref[...] + length * direction_ref[me_ref[0]]
    knot_out[...] = knot[0:params]
    residual_out[...] = residual_ref[...] - length * diff_ref[...]


def call(kernel, outs, ins, scratch=()):
    return pl.pallas_call(
        kernel,
        out_shape=outs,
        in_specs=ins,
        out_specs=jax.tree.map(lambda _: VMEM, outs),
        scratch_shapes=list(scratch),
        compiler_params=PARAMS,
    )


def local(jac, obs, match, tile_knot, tile_frac):
    tiles, params, columns = jac.shape
    n_track = lax.axis_size("track")
    n_det = lax.axis_size("det")
    n_all = n_track * n_det
    q = tiles // n_track
    me = lax.axis_index("track").astype(jnp.int32).reshape(1)

    def crossing(values):
        return lax.all_to_all(values, "track", split_axis=0, concat_axis=0, tiled=True)

    def everywhere(values):
        return lax.all_to_all(values, ("track", "det"), split_axis=0, concat_axis=0, tiled=True)

    perm, weights, edge, sent, jac_rows = call(
        functools.partial(setup_kernel, q, math.gcd(params, 3)),
        (
            jax.ShapeDtypeStruct((tiles, tiles), jnp.bfloat16),
            kept((3, KNOT_DEV + PAD, tiles), jnp.bfloat16),
            kept((SUB, tiles)),
            f32(tiles, columns),
            kept((params, tiles, columns)),
        ),
        [SMEM] + [ANY] * 5,
        [
            pltpu.VMEM((1, tiles), jnp.int32),
            pltpu.VMEM((1, tiles), jnp.int32),
            pltpu.VMEM((1, tiles), jnp.float32),
            pltpu.VMEM((tiles, columns), jnp.float32),
            pltpu.VMEM((params, tiles, columns), jnp.float32),
            pltpu.SemaphoreType.DMA((4 + params,)),
        ],
    )(
        me,
        *map(
            from_hbm,
            (match[None], tile_knot[None], tile_frac[None], obs, jnp.transpose(jac, (1, 0, 2))),
        ),
    )

    def adjoint(sent, arrived):
        diff, payload = call(
            functools.partial(adjoint_kernel, q),
            (f32(tiles, columns), f32(n_all, PAD, LANES)),
            [SMEM] + [VMEM] * 4,
            [pltpu.VMEM((PAD, tiles), jnp.float32)],
        )(me, sent, arrived, jac_rows, weights)
        return diff, everywhere(payload)

    field = f32(n_track, PAD, LANES)
    scalar = f32(SUB, LANES)
    interp = pltpu.VMEM((n_track, PAD, LANES), jnp.float32)
    misfit, gathered = adjoint(sent, crossing(sent))
    gradient, slope_norm, sent = call(
        functools.partial(first_kernel, q, n_det),
        (field, scalar, f32(tiles, columns)),
        [SMEM] + [VMEM] * 4,
        [interp],
    )(me, gathered, jac_rows, weights, edge)
    direction = gradient
    knot_field = jnp.zeros((PAD, KNOT_DEV), jnp.float32)
    lengths, changes = [], []
    for iteration in range(ITERS - 1):
        change, gathered = adjoint(sent, crossing(sent))
        last = iteration == ITERS - 2
        results = call(
            functools.partial(step_kernel, q, n_det),
            (field, scalar, f32(PAD, KNOT_DEV), scalar, f32(tiles, columns))
            + (() if last else (field,)),
            [SMEM] + [VMEM] * 8,
            [interp] * (3 if last else 2),
        )(
            me, gathered, jac_rows, weights, edge, gradient, direction, slope_norm, knot_field
        )
        direction, slope_norm, knot_field, length, sent = results[:5]
        gradient = None if last else results[5]
        lengths.append(length)
        changes.append(change)
    change, squares = call(
        functools.partial(last_kernel, q),
        (f32(tiles, columns), f32(n_all, 1, LANES)),
        [SMEM] + [VMEM] * 2,
    )(me, sent, crossing(sent))
    squares = everywhere(squares)
    residual, change = call(
        functools.partial(restore_kernel, q),
        (f32(tiles, columns), f32(tiles, columns)),
        [VMEM] * (3 + 2 * len(changes)),
        [pltpu.VMEM((tiles, columns), jnp.float32)],
    )(perm, misfit, change, *lengths, *changes)
    return call(
        finish_kernel,
        (f32(params, KNOT_DEV), f32(tiles, columns)),
        [SMEM] + [VMEM] * 6,
    )(me, squares, direction, slope_norm, knot_field, residual, change)


def solution(mesh):
    in_specs = (P("track", None, "det"), P("track", "det"), P("track"), P("track"), P("track"))
    out_specs = (P(None, "track"), P("track", "det"))
    return jax.shard_map(local, mesh=mesh, in_specs=in_specs, out_specs=out_specs, check_vma=False)
```

```python
import functools
import math

import jax
import jax.numpy as jnp
from jax import lax
from jax.experimental import pallas as pl
from jax.experimental.pallas import tpu as pltpu
from jax.sharding import PartitionSpec as P

KNOT_DEV = 128
ITERS = 4
LANES = 128
SUB = 8
PAD = 16
VMEM_BYTES = 14 * 2**20


damping = 1.0

SMEM = pl.BlockSpec(memory_space=pltpu.SMEM)
VMEM = pl.BlockSpec(memory_space=pltpu.VMEM)
ANY = pl.BlockSpec(memory_space=pl.ANY)
PARAMS = pltpu.CompilerParams(vmem_limit_bytes=VMEM_BYTES)
HIGHEST = lax.Precision.HIGHEST


def kept(shape, dtype=jnp.float32):
    return pltpu.VMEM(shape, dtype)


def from_hbm(x):
    return pltpu.with_memory_space_constraint(x, pltpu.HBM)


def f32(*shape):
    return jax.ShapeDtypeStruct(shape, jnp.float32)


def dot(a, b, dims):
    return lax.dot_general(
        a, b, (dims, ((), ())), precision=HIGHEST, preferred_element_type=jnp.float32
    )


def split3(x):
    first = x.astype(jnp.bfloat16)
    rest = x - first.astype(jnp.float32)
    second = rest.astype(jnp.bfloat16)
    third = (rest - second.astype(jnp.float32)).astype(jnp.bfloat16)
    return first, second, third


def bf16_dot(a, b):
    return jnp.dot(a, b, preferred_element_type=jnp.float32)


def turn(x, shift):
    shift = shift % LANES
    return x if shift == 0 else pltpu.roll(x, shift, 1)


def lane_group(shape, q):
    return lax.broadcasted_iota(jnp.int32, shape, 1) // q


def to_crossing(arrays, perm, q, store):
    tiles = arrays[0].shape[0]
    groups = LANES // q
    stacked = []
    for x in arrays:
        across = jnp.concatenate(
            [x[c * LANES : (c + 1) * LANES].T for c in range(tiles // LANES)], axis=1
        )
        stacked.extend(split3(across))
    moved = bf16_dot(jnp.concatenate(stacked, axis=0), perm)
    group = lane_group((q, LANES), q)
    for index in range(len(arrays)):
        third, second, first = (
            moved[(3 * index + part) * LANES : (3 * index + part + 1) * LANES] for part in (2, 1, 0)
        )
        whole = third + second + first
        for c in range(tiles // LANES):
            for b in range(groups):
                block = None
                for h in range(groups):
                    piece = turn(
                        whole[h * q : (h + 1) * q, c * LANES : (c + 1) * LANES], (h - b) * q
                    )
                    block = piece if block is None else jnp.where(group == h, piece, block)
                store(index, c * groups + b, block)


def from_crossing(load, perm, q, tiles):
    groups = LANES // q
    group = lane_group((q, LANES), q)
    parts = []
    for c in range(tiles // LANES):
        rows = []
        for h in range(groups):
            block = None
            for b in range(groups):
                piece = turn(load(c * groups + b), (b - h) * q)
                block = piece if block is None else jnp.where(group == b, piece, block)
            rows.append(block)
        parts.append(jnp.concatenate(rows, axis=0).T)
    stacked = jnp.concatenate(parts, axis=0)
    return sum(bf16_dot(perm, part) for part in reversed(split3(stacked)))


def crossing_order(me, start, n_track, match):
    tiles = match.shape[1]
    slot = lax.broadcasted_iota(jnp.int32, (1, tiles), 1)
    peer = match // tiles
    other = match - peer * tiles
    inner = jnp.where(
        peer == me,
        jnp.minimum(slot, other) + jnp.where(slot > other, tiles, 0),
        jnp.where(peer > me, slot, other),
    )
    place = jnp.where(peer >= start, peer - start, peer - start + n_track)
    key = (place * (2 * tiles) + inner).astype(jnp.float32)
    key_cols = jnp.broadcast_to(key, (LANES, tiles)).T[:, :1]
    place = jnp.sum(jnp.where(key < key_cols, 1.0, 0.0), axis=1, keepdims=True)
    cols = lax.broadcasted_iota(jnp.int32, (tiles, tiles), 1).astype(jnp.float32)
    return jnp.where(place == cols, 1.0, 0.0).astype(jnp.bfloat16)


def setup_kernel(
    q,
    together,
    me_ref,
    match_hbm,
    knot_hbm,
    frac_hbm,
    obs_hbm,
    jac_hbm,
    perm_ref,
    weight_ref,
    edge_ref,
    sent_ref,
    out_ref,
    match_ref,
    knot_ref,
    frac_ref,
    obs_ref,
    jac_ref,
    sems,
):
    params, tiles, _ = jac_ref.shape
    pairs = [(match_hbm, match_ref), (knot_hbm, knot_ref), (frac_hbm, frac_ref), (obs_hbm, obs_ref)]
    pairs += [(jac_hbm.at[p], jac_ref.at[p]) for p in range(params)]
    copies = [
        pltpu.make_async_copy(source, target, sems.at[index])
        for index, (source, target) in enumerate(pairs)
    ]
    for copy in copies:
        copy.start()
    copies[0].wait()
    perm = crossing_order(me_ref[0], me_ref[2], tiles // q, match_ref[...])
    perm_ref[...] = perm
    for copy in copies[1:4]:
        copy.wait()

    row = lax.broadcasted_iota(jnp.int32, (SUB, tiles), 0)
    facts = jnp.where(row == 0, knot_ref[...].astype(jnp.float32), frac_ref[...])
    moved = sum(bf16_dot(part, perm) for part in reversed(split3(facts)))
    knot, frac = moved[0:1], moved[1:2]
    knots = lax.broadcasted_iota(jnp.int32, (KNOT_DEV, tiles), 0).astype(jnp.float32)
    main = jnp.where(knots == knot, 1.0 - frac, 0.0) + jnp.where(knots == knot + 1.0, frac, 0.0)
    first_row = lax.broadcasted_iota(jnp.int32, (PAD, tiles), 0) == 0
    edge = jnp.where(first_row, jnp.where(knot == KNOT_DEV - 1.0, frac, 0.0), 0.0)
    edge_ref[...] = edge[0:SUB]
    for index, (upper, lower) in enumerate(zip(split3(main), split3(edge))):
        weight_ref[index, 0:KNOT_DEV, :] = upper
        weight_ref[index, KNOT_DEV : KNOT_DEV + PAD, :] = lower

    def put_obs(_, index, block):
        sent_ref[index * q : (index + 1) * q, :] = block

    to_crossing([obs_ref[...]], perm, q, put_obs)
    for first in range(0, params, together):
        for p in range(first, first + together):
            copies[4 + p].wait()

        def put(index, block_index, block):
            out_ref[first + index, block_index * q : (block_index + 1) * q, :] = block

        to_crossing([jac_ref[p] for p in range(first, first + together)], perm, q, put)


def weight_dot(x, parts, over_tiles):
    dims = (((1,), (1 if over_tiles else 0,)), ((), ()))
    stacked = jnp.concatenate(split3(x), axis=0)
    first, second, third = (
        lax.dot_general(
            stacked[0 : (3 - index) * PAD], part, dims, preferred_element_type=jnp.float32
        )
        for index, part in enumerate(parts)
    )
    small = third + second[PAD : 2 * PAD] + first[2 * PAD : 3 * PAD]
    return (small + (second[0:PAD] + first[PAD : 2 * PAD])) + first[0:PAD]


def row_sums(parts):
    row = lax.broadcasted_iota(jnp.int32, (SUB, LANES), 0)
    level = list(parts)
    zero = jnp.zeros((SUB, LANES), jnp.float32)
    while len(level) % SUB:
        level.append(zero)
    for distance in (1, 2, 4):
        first = (row // distance) % 2 == 0
        level = [
            jnp.where(first, a, b) + pltpu.roll(jnp.where(first, b, a), distance, 0)
            for a, b in zip(level[::2], level[1::2])
        ]
    return level[0] if len(level) == 1 else jnp.concatenate(level, axis=0)


def fold_rows(x):
    total = x[0:SUB]
    for step in range(1, x.shape[0] // SUB):
        total = total + x[step * SUB : (step + 1) * SUB]
    return total


def fold_lanes(x, q):
    shift = q
    while shift < LANES:
        x = x + pltpu.roll(x, shift, 1)
        shift *= 2
    return x


def crossing_values(me, arrived_ref, out_ref, q):
    out_ref[...] = arrived_ref[...]
    own = arrived_ref[pl.ds(pl.multiple_of(me * q, SUB), q), :]
    lane = lax.broadcasted_iota(jnp.int32, (q, LANES), 1)
    swapped = jnp.where(lane % q < q // 2, turn(own, -(q // 2)), turn(own, q // 2))
    out_ref[pl.ds(pl.multiple_of(me * q, SUB), q), :] = swapped


def difference(me, sent_ref, arrived_ref, out_ref, q):
    crossing_values(me, arrived_ref, out_ref, q)
    out_ref[...] = sent_ref[...] - out_ref[...]


def adjoint_kernel(
    q, me_ref, sent_ref, arrived_ref, jac_ref, weight_ref, diff_ref, send_ref, values_ref
):
    params, tiles, _ = jac_ref.shape
    difference(me_ref[1], sent_ref, arrived_ref, diff_ref, q)
    groups = LANES // q
    group = lane_group((PAD, LANES), q)
    for c in range(tiles // LANES):
        values = None
        for i in range(groups):
            rows = slice((c * groups + i) * q, (c * groups + i + 1) * q)
            diff = diff_ref[rows, :]
            sums = fold_lanes(
                row_sums([fold_rows(jac_ref[p, rows, :] * diff) for p in range(params)]), q
            )
            values = sums if values is None else jnp.where(group == i, sums, values)
        values_ref[:, c * LANES : (c + 1) * LANES] = values
    spread = weight_dot(values_ref[...], [weight_ref[index] for index in range(3)], True)
    lane = lax.broadcasted_iota(jnp.int32, (PAD, LANES), 1)
    row = lax.broadcasted_iota(jnp.int32, (PAD, LANES), 0)
    spill = jnp.sum(
        jnp.where(lane == row, spread[:, KNOT_DEV : KNOT_DEV + 1], 0.0), axis=0, keepdims=True
    )
    block = jnp.where(row < params, spread[:, :KNOT_DEV], jnp.where(row == params, spill, 0.0))
    for d in range(send_ref.shape[0]):
        send_ref[d] = block


def field_sums(gathered_ref, n_track, n_det, params, store):
    lane = lax.broadcasted_iota(jnp.int32, (PAD, LANES), 1)
    row = lax.broadcasted_iota(jnp.int32, (PAD, LANES), 0)
    spill = jnp.zeros((PAD, 1), jnp.float32)
    for b in range(n_track):
        total = gathered_ref[b]
        for d in range(1, n_det):
            total = total + gathered_ref[d * n_track + b]
        field = jnp.where(row < params, total, 0.0)
        field = field + jnp.where(lane == 0, spill, 0.0)
        store(b, field)
        spill = jnp.sum(
            jnp.where((lane == row) & (row < params), total[params : params + 1], 0.0),
            axis=1,
            keepdims=True,
        )


def total_of(x):
    return jnp.sum(jnp.sum(x, axis=0), keepdims=True).reshape(1, 1)


def full_dot(a_ref, b_ref):
    total = a_ref[0] * b_ref[0]
    for b in range(1, a_ref.shape[0]):
        total = total + a_ref[b] * b_ref[b]
    return jnp.sum(total, keepdims=True)


def predict(me, q, direction_ref, jac_ref, weight_ref, edge_ref, interp_ref, sent_ref):
    params, tiles, _ = jac_ref.shape
    n_track = direction_ref.shape[0]
    following = direction_ref[jnp.minimum(me + 1, n_track - 1)][:, 0:1]
    following = jnp.where(me + 1 < n_track, following, 0.0)
    parts = [weight_ref[index, 0:KNOT_DEV, :] for index in range(3)]
    interp = weight_dot(direction_ref[me], parts, False) + following * edge_ref[0:1, :]
    groups = LANES // q
    group = lane_group((PAD, LANES), q)
    for c in range(tiles // LANES):
        chunk = interp[:, c * LANES : (c + 1) * LANES]
        for i in range(groups):
            wide = None
            for h in range(groups):
                piece = turn(chunk, (h - i) * q)
                wide = piece if wide is None else jnp.where(group == h, piece, wide)
            interp_ref[c * groups + i] = wide

    def block_values(b, carry):
        rows = pl.ds(pl.multiple_of(b * q, SUB), q)
        interp = interp_ref[b]
        total = jac_ref[0, rows, :] * interp[0:1]
        for p in range(1, params):
            total = total + jac_ref[p, rows, :] * interp[p : p + 1]
        sent_ref[rows, :] = total
        return carry

    lax.fori_loop(0, tiles // q, block_values, 0)


def first_kernel(
    q,
    n_det,
    me_ref,
    gathered_ref,
    jac_ref,
    weight_ref,
    edge_ref,
    grad_ref,
    norm_ref,
    sent_ref,
    interp_ref,
):
    n_track = grad_ref.shape[0]

    def put(b, field):
        grad_ref[b] = field

    field_sums(gathered_ref, n_track, n_det, jac_ref.shape[0], put)
    norm_ref[...] = jnp.broadcast_to(full_dot(grad_ref, grad_ref), norm_ref.shape)
    predict(me_ref[0], q, grad_ref, jac_ref, weight_ref, edge_ref, interp_ref, sent_ref)


def step_kernel(
    q,
    n_det,
    me_ref,
    gathered_ref,
    jac_ref,
    weight_ref,
    edge_ref,
    grad_ref,
    direction_ref,
    norm_ref,
    knot_ref,
    direction_out,
    norm_out,
    knot_out,
    length_out,
    sent_ref,
    grad_out,
    image_ref,
    interp_ref,
):
    n_track = grad_ref.shape[0]
    me = me_ref[0]

    def put(b, field):
        image_ref[b] = field + damping * direction_ref[b]

    field_sums(gathered_ref, n_track, n_det, jac_ref.shape[0], put)
    norm = norm_ref[0:1, 0:1]
    length = norm / full_dot(direction_ref, image_ref)
    length_out[...] = jnp.broadcast_to(length, length_out.shape)
    knot_out[...] = knot_ref[...] + length * direction_ref[me]
    for b in range(n_track):
        grad_out[b] = grad_ref[b] - length * image_ref[b]
    new_norm = full_dot(grad_out, grad_out)
    norm_out[...] = jnp.broadcast_to(new_norm, norm_out.shape)
    ratio = new_norm / norm
    for b in range(n_track):
        direction_out[b] = grad_out[b] + ratio * direction_ref[b]
    predict(me, q, direction_out, jac_ref, weight_ref, edge_ref, interp_ref, sent_ref)


def last_kernel(q, me_ref, sent_ref, arrived_ref, diff_ref, send_ref):
    difference(me_ref[1], sent_ref, arrived_ref, diff_ref, q)
    diff = diff_ref[...]
    squares = jnp.sum(diff * diff, axis=0, keepdims=True)
    send_ref[...] = jnp.broadcast_to(squares[None], send_ref.shape)


def restore_kernel(q, perm_ref, misfit_ref, diff_ref, *refs):
    steps = (len(refs) - 3) // 2
    residual_out, diff_out, residual_ref = refs[2 * steps :]
    tiles = misfit_ref.shape[0]
    residual = misfit_ref[...]
    for length_ref, change_ref in zip(refs[:steps], refs[steps : 2 * steps]):
        residual = residual - length_ref[0:1, 0:1] * change_ref[...]
    residual_ref[...] = residual
    for source, target in ((residual_ref, residual_out), (diff_ref, diff_out)):
        target[...] = from_crossing(
            lambda index: source[index * q : (index + 1) * q, :], perm_ref[...], q, tiles
        )


def finish_kernel(
    me_ref, squares_ref, direction_ref, norm_ref, knot_ref, residual_ref, diff_ref, knot_out, residual_out
):
    params = knot_out.shape[0]
    squares = squares_ref[0]
    for d in range(1, squares_ref.shape[0]):
        squares = squares + squares_ref[d]
    curvature = 0.5 * jnp.sum(squares, keepdims=True) + damping * full_dot(
        direction_ref, direction_ref
    )
    length = norm_ref[0:1, 0:1] / curvature
    knot = knot_ref[...] + length * direction_ref[me_ref[0]]
    knot_out[...] = knot[0:params]
    residual_out[...] = residual_ref[...] - length * diff_ref[...]


def call(kernel, outs, ins, scratch=()):
    return pl.pallas_call(
        kernel,
        out_shape=outs,
        in_specs=ins,
        out_specs=jax.tree.map(lambda _: VMEM, outs),
        scratch_shapes=list(scratch),
        compiler_params=PARAMS,
    )


def rotation(det, n_track, n_det):
    return det * (n_track // n_det)


def local(jac, obs, match, tile_knot, tile_frac):
    tiles, params, columns = jac.shape
    n_track = lax.axis_size("track")
    n_det = lax.axis_size("det")
    n_all = n_track * n_det
    q = tiles // n_track
    me = lax.axis_index("track")
    start = rotation(lax.axis_index("det"), n_track, n_det)
    me = jnp.stack([me, lax.rem(me - start + n_track, n_track), start]).astype(jnp.int32)

    groups = [
        [(place + rotation(d, n_track, n_det)) % n_track * n_det + d for place in range(n_track)]
        for d in range(n_det)
    ]

    def crossing(values):
        return lax.all_to_all(
            values,
            ("track", "det"),
            split_axis=0,
            concat_axis=0,
            axis_index_groups=groups,
            tiled=True,
        )

    def everywhere(values):
        return lax.all_to_all(values, ("det", "track"), split_axis=0, concat_axis=0, tiled=True)

    perm, weights, edge, sent, jac_rows = call(
        functools.partial(setup_kernel, q, math.gcd(params, 3)),
        (
            jax.ShapeDtypeStruct((tiles, tiles), jnp.bfloat16),
            kept((3, KNOT_DEV + PAD, tiles), jnp.bfloat16),
            kept((SUB, tiles)),
            f32(tiles, columns),
            kept((params, tiles, columns)),
        ),
        [SMEM] + [ANY] * 5,
        [
            pltpu.VMEM((1, tiles), jnp.int32),
            pltpu.VMEM((1, tiles), jnp.int32),
            pltpu.VMEM((1, tiles), jnp.float32),
            pltpu.VMEM((tiles, columns), jnp.float32),
            pltpu.VMEM((params, tiles, columns), jnp.float32),
            pltpu.SemaphoreType.DMA((4 + params,)),
        ],
    )(
        me,
        *map(
            from_hbm,
            (match[None], tile_knot[None], tile_frac[None], obs, jnp.transpose(jac, (1, 0, 2))),
        ),
    )

    def adjoint(sent, arrived):
        diff, payload = call(
            functools.partial(adjoint_kernel, q),
            (f32(tiles, columns), f32(n_all, PAD, LANES)),
            [SMEM] + [VMEM] * 4,
            [pltpu.VMEM((PAD, tiles), jnp.float32)],
        )(me, sent, arrived, jac_rows, weights)
        return diff, everywhere(payload)

    field = f32(n_track, PAD, LANES)
    scalar = f32(SUB, LANES)
    interp = pltpu.VMEM((n_track, PAD, LANES), jnp.float32)
    misfit, gathered = adjoint(sent, crossing(sent))
    gradient, slope_norm, sent = call(
        functools.partial(first_kernel, q, n_det),
        (field, scalar, f32(tiles, columns)),
        [SMEM] + [VMEM] * 4,
        [interp],
    )(me, gathered, jac_rows, weights, edge)
    direction = gradient
    knot_field = jnp.zeros((PAD, KNOT_DEV), jnp.float32)
    lengths, changes = [], []
    for iteration in range(ITERS - 1):
        change, gathered = adjoint(sent, crossing(sent))
        last = iteration == ITERS - 2
        results = call(
            functools.partial(step_kernel, q, n_det),
            (field, scalar, f32(PAD, KNOT_DEV), scalar, f32(tiles, columns))
            + (() if last else (field,)),
            [SMEM] + [VMEM] * 8,
            [interp] * (3 if last else 2),
        )(
            me, gathered, jac_rows, weights, edge, gradient, direction, slope_norm, knot_field
        )
        direction, slope_norm, knot_field, length, sent = results[:5]
        gradient = None if last else results[5]
        lengths.append(length)
        changes.append(change)
    change, squares = call(
        functools.partial(last_kernel, q),
        (f32(tiles, columns), f32(n_all, 1, LANES)),
        [SMEM] + [VMEM] * 2,
    )(me, sent, crossing(sent))
    squares = everywhere(squares)
    residual, change = call(
        functools.partial(restore_kernel, q),
        (f32(tiles, columns), f32(tiles, columns)),
        [VMEM] * (3 + 2 * len(changes)),
        [pltpu.VMEM((tiles, columns), jnp.float32)],
    )(perm, misfit, change, *lengths, *changes)
    return call(
        finish_kernel,
        (f32(params, KNOT_DEV), f32(tiles, columns)),
        [SMEM] + [VMEM] * 6,
    )(me, squares, direction, slope_norm, knot_field, residual, change)


def solution(mesh):
    in_specs = (P("track", None, "det"), P("track", "det"), P("track"), P("track"), P("track"))
    out_specs = (P(None, "track"), P("track", "det"))
    return jax.shard_map(local, mesh=mesh, in_specs=in_specs, out_specs=out_specs, check_vma=False)
```

```python
import functools
import math

import jax
import jax.numpy as jnp
from jax import lax
from jax.experimental import pallas as pl
from jax.experimental.pallas import tpu as pltpu
from jax.sharding import PartitionSpec as P

KNOT_DEV = 128
ITERS = 4
LANES = 128
SUB = 8
PAD = 16
VMEM_BYTES = 14 * 2**20


damping = 1.0

SMEM = pl.BlockSpec(memory_space=pltpu.SMEM)
VMEM = pl.BlockSpec(memory_space=pltpu.VMEM)
ANY = pl.BlockSpec(memory_space=pl.ANY)
PARAMS = pltpu.CompilerParams(vmem_limit_bytes=VMEM_BYTES)
HIGHEST = lax.Precision.HIGHEST


def kept(shape, dtype=jnp.float32):
    return pltpu.VMEM(shape, dtype)


def from_hbm(x):
    return pltpu.with_memory_space_constraint(x, pltpu.HBM)


def f32(*shape):
    return jax.ShapeDtypeStruct(shape, jnp.float32)


def dot(a, b, dims):
    return lax.dot_general(
        a, b, (dims, ((), ())), precision=HIGHEST, preferred_element_type=jnp.float32
    )


def split3(x):
    first = x.astype(jnp.bfloat16)
    rest = x - first.astype(jnp.float32)
    second = rest.astype(jnp.bfloat16)
    third = (rest - second.astype(jnp.float32)).astype(jnp.bfloat16)
    return first, second, third


def bf16_dot(a, b):
    return jnp.dot(a, b, preferred_element_type=jnp.float32)


def turn(x, shift):
    shift = shift % LANES
    return x if shift == 0 else pltpu.roll(x, shift, 1)


def lane_group(shape, q):
    return lax.broadcasted_iota(jnp.int32, shape, 1) // q


def to_crossing(arrays, perm, q, store):
    tiles = arrays[0].shape[0]
    groups = LANES // q
    stacked = []
    for x in arrays:
        across = jnp.concatenate(
            [x[c * LANES : (c + 1) * LANES].T for c in range(tiles // LANES)], axis=1
        )
        stacked.extend(split3(across))
    moved = bf16_dot(jnp.concatenate(stacked, axis=0), perm)
    group = lane_group((q, LANES), q)
    for index in range(len(arrays)):
        third, second, first = (
            moved[(3 * index + part) * LANES : (3 * index + part + 1) * LANES] for part in (2, 1, 0)
        )
        whole = third + second + first
        for c in range(tiles // LANES):
            for b in range(groups):
                block = None
                for h in range(groups):
                    piece = turn(
                        whole[h * q : (h + 1) * q, c * LANES : (c + 1) * LANES], (h - b) * q
                    )
                    block = piece if block is None else jnp.where(group == h, piece, block)
                store(index, c * groups + b, block)


def from_crossing(load, perm, q, tiles):
    groups = LANES // q
    group = lane_group((q, LANES), q)
    parts = []
    for c in range(tiles // LANES):
        rows = []
        for h in range(groups):
            block = None
            for b in range(groups):
                piece = turn(load(c * groups + b), (b - h) * q)
                block = piece if block is None else jnp.where(group == b, piece, block)
            rows.append(block)
        parts.append(jnp.concatenate(rows, axis=0).T)
    stacked = jnp.concatenate(parts, axis=0)
    return sum(bf16_dot(perm, part) for part in reversed(split3(stacked)))


def crossing_order(me, match):
    tiles = match.shape[1]
    slot = lax.broadcasted_iota(jnp.int32, (1, tiles), 1)
    peer = match // tiles
    other = match - peer * tiles
    inner = jnp.where(
        peer == me,
        jnp.minimum(slot, other) + jnp.where(slot > other, tiles, 0),
        jnp.where(peer > me, slot, other),
    )
    key = (peer * (2 * tiles) + inner).astype(jnp.float32)
    key_cols = jnp.broadcast_to(key, (LANES, tiles)).T[:, :1]
    place = jnp.sum(jnp.where(key < key_cols, 1.0, 0.0), axis=1, keepdims=True)
    cols = lax.broadcasted_iota(jnp.int32, (tiles, tiles), 1).astype(jnp.float32)
    return jnp.where(place == cols, 1.0, 0.0).astype(jnp.bfloat16)


def order_kernel(q, me_ref, match_hbm, obs_hbm, obs_out, match_ref, obs_ref, sems):
    copies = [
        pltpu.make_async_copy(match_hbm, match_ref, sems.at[0]),
        pltpu.make_async_copy(obs_hbm, obs_ref, sems.at[1]),
    ]
    for copy in copies:
        copy.start()
    copies[0].wait()
    perm = crossing_order(me_ref[0], match_ref[...])
    copies[1].wait()

    def put(_, index, block):
        obs_out[index * q : (index + 1) * q, :] = block

    to_crossing([obs_ref[...]], perm, q, put)


def table_rows(params, tiles):
    return (params + 1) * tiles + 3 * (tiles // LANES) * (KNOT_DEV + PAD)


def table_views(table_ref, params, tiles):
    return [table_ref.at[p * tiles : (p + 1) * tiles] for p in range(params + 1)]


def table_weights(table_ref, params, tiles):
    height = KNOT_DEV + PAD
    chunks = tiles // LANES
    parts = []
    for index in range(3):
        first = (params + 1) * tiles + index * chunks * height
        parts.append(
            jnp.concatenate(
                [table_ref[first + c * height : first + (c + 1) * height, :] for c in range(chunks)],
                axis=1,
            )
        )
    return parts


def table_kernel(
    q,
    together,
    me_ref,
    match_hbm,
    knot_hbm,
    frac_hbm,
    sent_hbm,
    jac_hbm,
    table_ref,
    match_ref,
    knot_ref,
    frac_ref,
    jac_ref,
    sems,
):
    params, tiles, _ = jac_ref.shape
    views = table_views(table_ref, params, tiles)
    pairs = [(match_hbm, match_ref), (knot_hbm, knot_ref), (frac_hbm, frac_ref)]
    pairs += [(jac_hbm.at[p], jac_ref.at[p]) for p in range(params)]
    pairs += [(sent_hbm, views[params])]
    copies = [
        pltpu.make_async_copy(source, target, sems.at[index])
        for index, (source, target) in enumerate(pairs)
    ]
    for copy in copies:
        copy.start()
    for copy in copies[:3]:
        copy.wait()
    perm = crossing_order(me_ref[0], match_ref[...])
    row = lax.broadcasted_iota(jnp.int32, (SUB, tiles), 0)
    facts = jnp.where(row == 0, knot_ref[...].astype(jnp.float32), frac_ref[...])
    moved = sum(bf16_dot(part, perm) for part in reversed(split3(facts)))
    knot, frac = moved[0:1], moved[1:2]
    knots = lax.broadcasted_iota(jnp.int32, (KNOT_DEV, tiles), 0).astype(jnp.float32)
    main = jnp.where(knots == knot, 1.0 - frac, 0.0) + jnp.where(knots == knot + 1.0, frac, 0.0)
    first_row = lax.broadcasted_iota(jnp.int32, (PAD, tiles), 0) == 0
    edge = jnp.where(first_row, jnp.where(knot == KNOT_DEV - 1.0, frac, 0.0), 0.0)
    place = (params + 1) * tiles
    for upper, lower in zip(split3(main), split3(edge)):
        for c in range(tiles // LANES):
            lanes = slice(c * LANES, (c + 1) * LANES)
            table_ref[place : place + KNOT_DEV, :] = upper[:, lanes].astype(jnp.float32)
            place += KNOT_DEV
            table_ref[place : place + PAD, :] = lower[:, lanes].astype(jnp.float32)
            place += PAD

    for first in range(0, params, together):
        for p in range(first, first + together):
            copies[3 + p].wait()

        def put(index, block_index, block):
            views[first + index][block_index * q : (block_index + 1) * q, :] = block

        to_crossing([jac_ref[p] for p in range(first, first + together)], perm, q, put)
    copies[3 + params].wait()


def weight_dot(x, parts, over_tiles):
    dims = (((1,), (1 if over_tiles else 0,)), ((), ()))
    stacked = jnp.concatenate(split3(x), axis=0)
    first, second, third = (
        lax.dot_general(
            stacked[0 : (3 - index) * PAD], part, dims, preferred_element_type=jnp.float32
        )
        for index, part in enumerate(parts)
    )
    small = third + second[PAD : 2 * PAD] + first[2 * PAD : 3 * PAD]
    return (small + (second[0:PAD] + first[PAD : 2 * PAD])) + first[0:PAD]


def row_sums(parts):
    row = lax.broadcasted_iota(jnp.int32, (SUB, LANES), 0)
    level = list(parts)
    zero = jnp.zeros((SUB, LANES), jnp.float32)
    while len(level) % SUB:
        level.append(zero)
    for distance in (1, 2, 4):
        first = (row // distance) % 2 == 0
        level = [
            jnp.where(first, a, b) + pltpu.roll(jnp.where(first, b, a), distance, 0)
            for a, b in zip(level[::2], level[1::2])
        ]
    return level[0] if len(level) == 1 else jnp.concatenate(level, axis=0)


def fold_rows(x):
    total = x[0:SUB]
    for step in range(1, x.shape[0] // SUB):
        total = total + x[step * SUB : (step + 1) * SUB]
    return total


def fold_lanes(x, q):
    shift = q
    while shift < LANES:
        x = x + pltpu.roll(x, shift, 1)
        shift *= 2
    return x


def crossing_values(me, arrived_ref, out_ref, q):
    out_ref[...] = arrived_ref[...]
    own = arrived_ref[pl.ds(pl.multiple_of(me * q, SUB), q), :]
    lane = lax.broadcasted_iota(jnp.int32, (q, LANES), 1)
    swapped = jnp.where(lane % q < q // 2, turn(own, -(q // 2)), turn(own, q // 2))
    out_ref[pl.ds(pl.multiple_of(me * q, SUB), q), :] = swapped


def difference(me, sent_ref, arrived_ref, out_ref, q):
    crossing_values(me, arrived_ref, out_ref, q)
    out_ref[...] = sent_ref[...] - out_ref[...]


def first_adjoint_kernel(
    q, params, me_ref, arrived_ref, table_ref, diff_ref, send_ref, values_ref
):
    tiles = arrived_ref.shape[0]
    views = table_views(table_ref, params, tiles)
    parts = [part.astype(jnp.bfloat16) for part in table_weights(table_ref, params, tiles)]
    difference(me_ref[0], views[params], arrived_ref, diff_ref, q)
    adjoint_rows(q, params, diff_ref, views, parts, send_ref, values_ref)


def adjoint_kernel(
    q, params, me_ref, sent_ref, arrived_ref, table_ref, weight_ref, diff_ref, send_ref, values_ref
):
    views = table_views(table_ref, params, sent_ref.shape[0])
    difference(me_ref[0], sent_ref, arrived_ref, diff_ref, q)
    parts = [weight_ref[index] for index in range(3)]
    adjoint_rows(q, params, diff_ref, views, parts, send_ref, values_ref)


def adjoint_rows(q, params, diff_ref, views, parts, send_ref, values_ref):
    tiles = diff_ref.shape[0]
    groups = LANES // q
    group = lane_group((PAD, LANES), q)
    for c in range(tiles // LANES):
        values = None
        for i in range(groups):
            rows = slice((c * groups + i) * q, (c * groups + i + 1) * q)
            diff = diff_ref[rows, :]
            sums = fold_lanes(
                row_sums([fold_rows(views[p][rows, :] * diff) for p in range(params)]), q
            )
            values = sums if values is None else jnp.where(group == i, sums, values)
        values_ref[:, c * LANES : (c + 1) * LANES] = values
    spread = weight_dot(values_ref[...], parts, True)
    lane = lax.broadcasted_iota(jnp.int32, (PAD, LANES), 1)
    row = lax.broadcasted_iota(jnp.int32, (PAD, LANES), 0)
    spill = jnp.sum(
        jnp.where(lane == row, spread[:, KNOT_DEV : KNOT_DEV + 1], 0.0), axis=0, keepdims=True
    )
    block = jnp.where(row < params, spread[:, :KNOT_DEV], jnp.where(row == params, spill, 0.0))
    for d in range(send_ref.shape[0]):
        send_ref[d] = block


def field_sums(gathered_ref, n_track, n_det, params, store, base=0):
    lane = lax.broadcasted_iota(jnp.int32, (PAD, LANES), 1)
    row = lax.broadcasted_iota(jnp.int32, (PAD, LANES), 0)
    spill = jnp.zeros((PAD, 1), jnp.float32)
    for b in range(n_track):
        total = gathered_ref[b * n_det, base : base + PAD, :]
        for d in range(1, n_det):
            total = total + gathered_ref[b * n_det + d, base : base + PAD, :]
        field = jnp.where(row < params, total, 0.0)
        field = field + jnp.where(lane == 0, spill, 0.0)
        store(b, field)
        spill = jnp.sum(
            jnp.where((lane == row) & (row < params), total[params : params + 1], 0.0),
            axis=1,
            keepdims=True,
        )


def total_of(x):
    return jnp.sum(jnp.sum(x, axis=0), keepdims=True).reshape(1, 1)


def full_dot(a_ref, b_ref):
    total = a_ref[0] * b_ref[0]
    for b in range(1, a_ref.shape[0]):
        total = total + a_ref[b] * b_ref[b]
    return jnp.sum(total, keepdims=True)


def predict(me, q, direction_ref, views, parts, edge, interp_ref, sent_ref):
    params = len(views) - 1
    tiles = sent_ref.shape[0]
    n_track = direction_ref.shape[0]
    following = direction_ref[jnp.minimum(me + 1, n_track - 1)][:, 0:1]
    following = jnp.where(me + 1 < n_track, following, 0.0)
    interp = weight_dot(direction_ref[me], parts, False) + following * edge
    groups = LANES // q
    group = lane_group((PAD, LANES), q)
    for c in range(tiles // LANES):
        chunk = interp[:, c * LANES : (c + 1) * LANES]
        for i in range(groups):
            wide = None
            for h in range(groups):
                piece = turn(chunk, (h - i) * q)
                wide = piece if wide is None else jnp.where(group == h, piece, wide)
            interp_ref[c * groups + i] = wide

    def block_values(b, carry):
        rows = pl.ds(pl.multiple_of(b * q, SUB), q)
        interp = interp_ref[b]
        total = views[0][rows, :] * interp[0:1]
        for p in range(1, params):
            total = total + views[p][rows, :] * interp[p : p + 1]
        sent_ref[rows, :] = total
        return carry

    lax.fori_loop(0, tiles // q, block_values, 0)


def first_kernel(
    q,
    n_det,
    params,
    me_ref,
    gathered_ref,
    table_ref,
    grad_ref,
    norm_ref,
    sent_ref,
    weight_ref,
    edge_ref,
    interp_ref,
):
    n_track = grad_ref.shape[0]
    tiles = sent_ref.shape[0]

    def put(b, field):
        grad_ref[b] = field

    field_sums(gathered_ref, n_track, n_det, params, put)
    norm_ref[...] = jnp.broadcast_to(full_dot(grad_ref, grad_ref), norm_ref.shape)
    wide = table_weights(table_ref, params, tiles)
    edge = sum(part[KNOT_DEV : KNOT_DEV + SUB] for part in reversed(wide))
    edge_ref[...] = edge
    parts = [part.astype(jnp.bfloat16) for part in wide]
    for index, part in enumerate(parts):
        weight_ref[index] = part
    upper = [part[0:KNOT_DEV] for part in parts]
    views = table_views(table_ref, params, tiles)
    predict(me_ref[0], q, grad_ref, views, upper, edge[0:1], interp_ref, sent_ref)


def step_kernel(
    q,
    n_det,
    params,
    me_ref,
    gathered_ref,
    table_ref,
    weight_ref,
    edge_ref,
    grad_ref,
    direction_ref,
    norm_ref,
    knot_ref,
    direction_out,
    norm_out,
    knot_out,
    length_out,
    sent_ref,
    grad_out,
    image_ref,
    interp_ref,
):
    n_track = grad_ref.shape[0]
    me = me_ref[0]

    def put(b, field):
        image_ref[b] = field + damping * direction_ref[b]

    field_sums(gathered_ref, n_track, n_det, params, put)
    norm = norm_ref[0:1, 0:1]
    length = norm / full_dot(direction_ref, image_ref)
    length_out[...] = jnp.broadcast_to(length, length_out.shape)
    knot_out[...] = knot_ref[...] + length * direction_ref[me]
    for b in range(n_track):
        grad_out[b] = grad_ref[b] - length * image_ref[b]
    new_norm = full_dot(grad_out, grad_out)
    norm_out[...] = jnp.broadcast_to(new_norm, norm_out.shape)
    ratio = new_norm / norm
    for b in range(n_track):
        direction_out[b] = grad_out[b] + ratio * direction_ref[b]
    views = table_views(table_ref, params, sent_ref.shape[0])
    parts = [weight_ref[index, 0:KNOT_DEV, :] for index in range(3)]
    predict(me, q, direction_out, views, parts, edge_ref[0:1, :], interp_ref, sent_ref)


def last_kernel(q, me_ref, sent_ref, arrived_ref, diff_ref, send_ref):
    difference(me_ref[0], sent_ref, arrived_ref, diff_ref, q)
    diff = diff_ref[...]
    squares = jnp.sum(diff * diff, axis=0, keepdims=True)
    send_ref[...] = jnp.broadcast_to(squares[None], send_ref.shape)


def restore_kernel(q, me_ref, match_hbm, misfit_ref, diff_ref, *refs):
    steps = (len(refs) - 5) // 2
    residual_out, diff_out, residual_ref, match_ref, sem = refs[2 * steps :]
    tiles = misfit_ref.shape[0]
    copy = pltpu.make_async_copy(match_hbm, match_ref, sem)
    copy.start()
    copy.wait()
    perm = crossing_order(me_ref[0], match_ref[...])
    residual = misfit_ref[...]
    for length_ref, change_ref in zip(refs[:steps], refs[steps : 2 * steps]):
        residual = residual - length_ref[0:1, 0:1] * change_ref[...]
    residual_ref[...] = residual
    for source, target in ((residual_ref, residual_out), (diff_ref, diff_out)):
        target[...] = from_crossing(
            lambda index: source[index * q : (index + 1) * q, :], perm, q, tiles
        )


def finish_kernel(
    me_ref, squares_ref, direction_ref, norm_ref, knot_ref, residual_ref, diff_ref, knot_out, residual_out
):
    params = knot_out.shape[0]
    squares = squares_ref[0]
    for d in range(1, squares_ref.shape[0]):
        squares = squares + squares_ref[d]
    curvature = 0.5 * jnp.sum(squares, keepdims=True) + damping * full_dot(
        direction_ref, direction_ref
    )
    length = norm_ref[0:1, 0:1] / curvature
    knot = knot_ref[...] + length * direction_ref[me_ref[0]]
    knot_out[...] = knot[0:params]
    residual_out[...] = residual_ref[...] - length * diff_ref[...]


def call(kernel, outs, ins, scratch=()):
    return pl.pallas_call(
        kernel,
        out_shape=outs,
        in_specs=ins,
        out_specs=jax.tree.map(lambda _: VMEM, outs),
        scratch_shapes=list(scratch),
        compiler_params=PARAMS,
    )


def local(jac, obs, match, tile_knot, tile_frac):
    tiles, params, columns = jac.shape
    n_track = lax.axis_size("track")
    n_det = lax.axis_size("det")
    n_all = n_track * n_det
    q = tiles // n_track
    me = lax.axis_index("track").astype(jnp.int32).reshape(1)

    def crossing(values):
        return lax.all_to_all(values, "track", split_axis=0, concat_axis=0, tiled=True)

    def everywhere(values):
        return lax.all_to_all(values, ("track", "det"), split_axis=0, concat_axis=0, tiled=True)

    match_row = from_hbm(match[None])
    int_row = pltpu.VMEM((1, tiles), jnp.int32)
    sent = call(
        functools.partial(order_kernel, q),
        f32(tiles, columns),
        [SMEM, ANY, ANY],
        [int_row, pltpu.VMEM((tiles, columns), jnp.float32), pltpu.SemaphoreType.DMA((2,))],
    )(me, match_row, from_hbm(obs))
    arrived = crossing(sent)
    table = call(
        functools.partial(table_kernel, q, math.gcd(params, 3)),
        kept((table_rows(params, tiles), columns)),
        [SMEM] + [ANY] * 5,
        [
            int_row,
            int_row,
            pltpu.VMEM((1, tiles), jnp.float32),
            pltpu.VMEM((params, tiles, columns), jnp.float32),
            pltpu.SemaphoreType.DMA((4 + params,)),
        ],
    )(
        me,
        match_row,
        *map(from_hbm, (tile_knot[None], tile_frac[None], sent, jnp.transpose(jac, (1, 0, 2)))),
    )

    field = f32(n_track, PAD, LANES)
    scalar = f32(SUB, LANES)
    interp = pltpu.VMEM((n_track, PAD, LANES), jnp.float32)
    adjoint_out = (f32(tiles, columns), f32(n_all, PAD, LANES))
    values = [pltpu.VMEM((PAD, tiles), jnp.float32)]
    misfit, payload = call(
        functools.partial(first_adjoint_kernel, q, params), adjoint_out, [SMEM] + [VMEM] * 2, values
    )(me, arrived, table)
    gradient, slope_norm, sent, weights, edge = call(
        functools.partial(first_kernel, q, n_det, params),
        (
            field,
            scalar,
            f32(tiles, columns),
            jax.ShapeDtypeStruct((3, KNOT_DEV + PAD, tiles), jnp.bfloat16),
            f32(SUB, tiles),
        ),
        [SMEM] + [VMEM] * 2,
        [interp],
    )(me, everywhere(payload), table)
    direction = gradient
    knot_field = jnp.zeros((PAD, KNOT_DEV), jnp.float32)
    lengths, changes = [], []
    for iteration in range(ITERS - 1):
        change, payload = call(
            functools.partial(adjoint_kernel, q, params), adjoint_out, [SMEM] + [VMEM] * 4, values
        )(me, sent, crossing(sent), table, weights)
        gathered = everywhere(payload)
        last = iteration == ITERS - 2
        results = call(
            functools.partial(step_kernel, q, n_det, params),
            (field, scalar, f32(PAD, KNOT_DEV), scalar, f32(tiles, columns))
            + (() if last else (field,)),
            [SMEM] + [VMEM] * 8,
            [interp] * (3 if last else 2),
        )(
            me, gathered, table, weights, edge, gradient, direction, slope_norm, knot_field
        )
        direction, slope_norm, knot_field, length, sent = results[:5]
        gradient = None if last else results[5]
        lengths.append(length)
        changes.append(change)
    change, squares = call(
        functools.partial(last_kernel, q),
        (f32(tiles, columns), f32(n_all, 1, LANES)),
        [SMEM] + [VMEM] * 2,
    )(me, sent, crossing(sent))
    squares = everywhere(squares)
    residual, change = call(
        functools.partial(restore_kernel, q),
        (f32(tiles, columns), f32(tiles, columns)),
        [SMEM, ANY] + [VMEM] * (2 + 2 * len(changes)),
        [pltpu.VMEM((tiles, columns), jnp.float32), int_row, pltpu.SemaphoreType.DMA],
    )(me, match_row, misfit, change, *lengths, *changes)
    return call(
        finish_kernel,
        (f32(params, KNOT_DEV), f32(tiles, columns)),
        [SMEM] + [VMEM] * 6,
    )(me, squares, direction, slope_norm, knot_field, residual, change)


def solution(mesh):
    in_specs = (P("track", None, "det"), P("track", "det"), P("track"), P("track"), P("track"))
    out_specs = (P(None, "track"), P("track", "det"))
    return jax.shard_map(local, mesh=mesh, in_specs=in_specs, out_specs=out_specs, check_vma=False)
```

```python
import functools
import math

import jax
import jax.numpy as jnp
from jax import lax
from jax.experimental import pallas as pl
from jax.experimental.pallas import tpu as pltpu
from jax.sharding import PartitionSpec as P

KNOT_DEV = 128
ITERS = 4
LANES = 128
SUB = 8
PAD = 16
VMEM_BYTES = 6 * 2**20


damping = 1.0

SMEM = pl.BlockSpec(memory_space=pltpu.SMEM)
VMEM = pl.BlockSpec(memory_space=pltpu.VMEM)
ANY = pl.BlockSpec(memory_space=pl.ANY)
PARAMS = pltpu.CompilerParams(vmem_limit_bytes=VMEM_BYTES)
HIGHEST = lax.Precision.HIGHEST


def kept(shape, dtype=jnp.float32):
    return pltpu.VMEM(shape, dtype)


def from_hbm(x):
    return pltpu.with_memory_space_constraint(x, pltpu.HBM)


def f32(*shape):
    return jax.ShapeDtypeStruct(shape, jnp.float32)


def dot(a, b, dims):
    return lax.dot_general(
        a, b, (dims, ((), ())), precision=HIGHEST, preferred_element_type=jnp.float32
    )


def split3(x):
    first = x.astype(jnp.bfloat16)
    rest = x - first.astype(jnp.float32)
    second = rest.astype(jnp.bfloat16)
    third = (rest - second.astype(jnp.float32)).astype(jnp.bfloat16)
    return first, second, third


def bf16_dot(a, b):
    return jnp.dot(a, b, preferred_element_type=jnp.float32)


def turn(x, shift):
    shift = shift % LANES
    return x if shift == 0 else pltpu.roll(x, shift, 1)


def lane_group(shape, q):
    return lax.broadcasted_iota(jnp.int32, shape, 1) // q


def to_crossing(arrays, perm, q, store):
    tiles = arrays[0].shape[0]
    groups = LANES // q
    stacked = []
    for x in arrays:
        across = jnp.concatenate(
            [x[c * LANES : (c + 1) * LANES].T for c in range(tiles // LANES)], axis=1
        )
        stacked.extend(split3(across))
    moved = bf16_dot(jnp.concatenate(stacked, axis=0), perm)
    group = lane_group((q, LANES), q)
    for index in range(len(arrays)):
        third, second, first = (
            moved[(3 * index + part) * LANES : (3 * index + part + 1) * LANES] for part in (2, 1, 0)
        )
        whole = third + second + first
        for c in range(tiles // LANES):
            for b in range(groups):
                block = None
                for h in range(groups):
                    piece = turn(
                        whole[h * q : (h + 1) * q, c * LANES : (c + 1) * LANES], (h - b) * q
                    )
                    block = piece if block is None else jnp.where(group == h, piece, block)
                store(index, c * groups + b, block)


def from_crossing(load, perm, q, tiles):
    groups = LANES // q
    group = lane_group((q, LANES), q)
    parts = []
    for c in range(tiles // LANES):
        rows = []
        for h in range(groups):
            block = None
            for b in range(groups):
                piece = turn(load(c * groups + b), (b - h) * q)
                block = piece if block is None else jnp.where(group == b, piece, block)
            rows.append(block)
        parts.append(jnp.concatenate(rows, axis=0).T)
    stacked = jnp.concatenate(parts, axis=0)
    return sum(bf16_dot(perm, part) for part in reversed(split3(stacked)))


def crossing_order(me, match):
    tiles = match.shape[1]
    slot = lax.broadcasted_iota(jnp.int32, (1, tiles), 1)
    peer = match // tiles
    other = match - peer * tiles
    inner = jnp.where(
        peer == me,
        jnp.minimum(slot, other) + jnp.where(slot > other, tiles, 0),
        jnp.where(peer > me, slot, other),
    )
    key = (peer * (2 * tiles) + inner).astype(jnp.float32)
    key_cols = jnp.broadcast_to(key, (LANES, tiles)).T[:, :1]
    place = jnp.sum(jnp.where(key < key_cols, 1.0, 0.0), axis=1, keepdims=True)
    cols = lax.broadcasted_iota(jnp.int32, (tiles, tiles), 1).astype(jnp.float32)
    return jnp.where(place == cols, 1.0, 0.0).astype(jnp.bfloat16)


def order_kernel(q, me_ref, match_hbm, obs_hbm, obs_out, match_ref, obs_ref, sems):
    copies = [
        pltpu.make_async_copy(match_hbm, match_ref, sems.at[0]),
        pltpu.make_async_copy(obs_hbm, obs_ref, sems.at[1]),
    ]
    for copy in copies:
        copy.start()
    copies[0].wait()
    perm = crossing_order(me_ref[0], match_ref[...])
    copies[1].wait()

    def put(_, index, block):
        obs_out[index * q : (index + 1) * q, :] = block

    to_crossing([obs_ref[...]], perm, q, put)


def table_rows(params, tiles):
    return (params + 1) * tiles + 3 * (tiles // LANES) * (KNOT_DEV + PAD)


def table_views(table_ref, params, tiles):
    return [table_ref.at[p * tiles : (p + 1) * tiles] for p in range(params + 1)]


def table_weights(table_ref, params, tiles):
    height = KNOT_DEV + PAD
    chunks = tiles // LANES
    parts = []
    for index in range(3):
        first = (params + 1) * tiles + index * chunks * height
        parts.append(
            jnp.concatenate(
                [table_ref[first + c * height : first + (c + 1) * height, :] for c in range(chunks)],
                axis=1,
            )
        )
    return parts


def table_kernel(
    q,
    together,
    me_ref,
    match_hbm,
    knot_hbm,
    frac_hbm,
    sent_hbm,
    jac_hbm,
    table_ref,
    match_ref,
    knot_ref,
    frac_ref,
    sems,
):
    params, tiles, _ = jac_hbm.shape
    views = table_views(table_ref, params, tiles)
    pairs = [(match_hbm, match_ref), (knot_hbm, knot_ref), (frac_hbm, frac_ref)]
    pairs += [(jac_hbm.at[p], views[p]) for p in range(params)]
    pairs += [(sent_hbm, views[params])]
    copies = [
        pltpu.make_async_copy(source, target, sems.at[index])
        for index, (source, target) in enumerate(pairs)
    ]
    for copy in copies:
        copy.start()
    for copy in copies[:3]:
        copy.wait()
    perm = crossing_order(me_ref[0], match_ref[...])
    row = lax.broadcasted_iota(jnp.int32, (SUB, tiles), 0)
    facts = jnp.where(row == 0, knot_ref[...].astype(jnp.float32), frac_ref[...])
    moved = sum(bf16_dot(part, perm) for part in reversed(split3(facts)))
    knot, frac = moved[0:1], moved[1:2]
    knots = lax.broadcasted_iota(jnp.int32, (KNOT_DEV, tiles), 0).astype(jnp.float32)
    main = jnp.where(knots == knot, 1.0 - frac, 0.0) + jnp.where(knots == knot + 1.0, frac, 0.0)
    first_row = lax.broadcasted_iota(jnp.int32, (PAD, tiles), 0) == 0
    edge = jnp.where(first_row, jnp.where(knot == KNOT_DEV - 1.0, frac, 0.0), 0.0)
    place = (params + 1) * tiles
    for upper, lower in zip(split3(main), split3(edge)):
        for c in range(tiles // LANES):
            lanes = slice(c * LANES, (c + 1) * LANES)
            table_ref[place : place + KNOT_DEV, :] = upper[:, lanes].astype(jnp.float32)
            place += KNOT_DEV
            table_ref[place : place + PAD, :] = lower[:, lanes].astype(jnp.float32)
            place += PAD

    for first in range(0, params, together):
        for p in range(first, first + together):
            copies[3 + p].wait()

        def put(index, block_index, block):
            views[first + index][block_index * q : (block_index + 1) * q, :] = block

        to_crossing([views[p][...] for p in range(first, first + together)], perm, q, put)
    copies[3 + params].wait()


def weight_dot(x, parts, over_tiles):
    dims = (((1,), (1 if over_tiles else 0,)), ((), ()))
    stacked = jnp.concatenate(split3(x), axis=0)
    first, second, third = (
        lax.dot_general(
            stacked[0 : (3 - index) * PAD], part, dims, preferred_element_type=jnp.float32
        )
        for index, part in enumerate(parts)
    )
    small = third + second[PAD : 2 * PAD] + first[2 * PAD : 3 * PAD]
    return (small + (second[0:PAD] + first[PAD : 2 * PAD])) + first[0:PAD]


def row_sums(parts):
    row = lax.broadcasted_iota(jnp.int32, (SUB, LANES), 0)
    level = list(parts)
    zero = jnp.zeros((SUB, LANES), jnp.float32)
    while len(level) % SUB:
        level.append(zero)
    for distance in (1, 2, 4):
        first = (row // distance) % 2 == 0
        level = [
            jnp.where(first, a, b) + pltpu.roll(jnp.where(first, b, a), distance, 0)
            for a, b in zip(level[::2], level[1::2])
        ]
    return level[0] if len(level) == 1 else jnp.concatenate(level, axis=0)


def fold_rows(x):
    total = x[0:SUB]
    for step in range(1, x.shape[0] // SUB):
        total = total + x[step * SUB : (step + 1) * SUB]
    return total


def fold_lanes(x, q):
    shift = q
    while shift < LANES:
        x = x + pltpu.roll(x, shift, 1)
        shift *= 2
    return x


def crossing_values(me, arrived_ref, out_ref, q):
    out_ref[...] = arrived_ref[...]
    own = arrived_ref[pl.ds(pl.multiple_of(me * q, SUB), q), :]
    lane = lax.broadcasted_iota(jnp.int32, (q, LANES), 1)
    swapped = jnp.where(lane % q < q // 2, turn(own, -(q // 2)), turn(own, q // 2))
    out_ref[pl.ds(pl.multiple_of(me * q, SUB), q), :] = swapped


def difference(me, sent_ref, arrived_ref, out_ref, q):
    crossing_values(me, arrived_ref, out_ref, q)
    out_ref[...] = sent_ref[...] - out_ref[...]


def first_adjoint_kernel(
    q, params, me_ref, arrived_ref, table_ref, diff_ref, send_ref, values_ref
):
    tiles = arrived_ref.shape[0]
    views = table_views(table_ref, params, tiles)
    parts = [part.astype(jnp.bfloat16) for part in table_weights(table_ref, params, tiles)]
    difference(me_ref[0], views[params], arrived_ref, diff_ref, q)
    adjoint_rows(q, params, diff_ref, views, parts, send_ref, values_ref)


def adjoint_kernel(
    q, params, me_ref, sent_ref, arrived_ref, table_ref, weight_ref, diff_ref, send_ref, values_ref
):
    views = table_views(table_ref, params, sent_ref.shape[0])
    difference(me_ref[0], sent_ref, arrived_ref, diff_ref, q)
    parts = [weight_ref[index] for index in range(3)]
    adjoint_rows(q, params, diff_ref, views, parts, send_ref, values_ref)


def adjoint_rows(q, params, diff_ref, views, parts, send_ref, values_ref):
    tiles = diff_ref.shape[0]
    groups = LANES // q
    group = lane_group((PAD, LANES), q)
    for c in range(tiles // LANES):
        values = None
        for i in range(groups):
            rows = slice((c * groups + i) * q, (c * groups + i + 1) * q)
            diff = diff_ref[rows, :]
            sums = fold_lanes(
                row_sums([fold_rows(views[p][rows, :] * diff) for p in range(params)]), q
            )
            values = sums if values is None else jnp.where(group == i, sums, values)
        values_ref[:, c * LANES : (c + 1) * LANES] = values
    spread = weight_dot(values_ref[...], parts, True)
    lane = lax.broadcasted_iota(jnp.int32, (PAD, LANES), 1)
    row = lax.broadcasted_iota(jnp.int32, (PAD, LANES), 0)
    spill = jnp.sum(
        jnp.where(lane == row, spread[:, KNOT_DEV : KNOT_DEV + 1], 0.0), axis=0, keepdims=True
    )
    block = jnp.where(row < params, spread[:, :KNOT_DEV], jnp.where(row == params, spill, 0.0))
    for d in range(send_ref.shape[0]):
        send_ref[d] = block


def field_sums(gathered_ref, n_track, n_det, params, store, base=0):
    lane = lax.broadcasted_iota(jnp.int32, (PAD, LANES), 1)
    row = lax.broadcasted_iota(jnp.int32, (PAD, LANES), 0)
    spill = jnp.zeros((PAD, 1), jnp.float32)
    for b in range(n_track):
        total = gathered_ref[b * n_det, base : base + PAD, :]
        for d in range(1, n_det):
            total = total + gathered_ref[b * n_det + d, base : base + PAD, :]
        field = jnp.where(row < params, total, 0.0)
        field = field + jnp.where(lane == 0, spill, 0.0)
        store(b, field)
        spill = jnp.sum(
            jnp.where((lane == row) & (row < params), total[params : params + 1], 0.0),
            axis=1,
            keepdims=True,
        )


def total_of(x):
    return jnp.sum(jnp.sum(x, axis=0), keepdims=True).reshape(1, 1)


def full_dot(a_ref, b_ref):
    total = a_ref[0] * b_ref[0]
    for b in range(1, a_ref.shape[0]):
        total = total + a_ref[b] * b_ref[b]
    return jnp.sum(total, keepdims=True)


def predict(me, q, direction_ref, views, parts, edge, interp_ref, sent_ref):
    params = len(views) - 1
    tiles = sent_ref.shape[0]
    n_track = direction_ref.shape[0]
    following = direction_ref[jnp.minimum(me + 1, n_track - 1)][:, 0:1]
    following = jnp.where(me + 1 < n_track, following, 0.0)
    interp = weight_dot(direction_ref[me], parts, False) + following * edge
    groups = LANES // q
    group = lane_group((PAD, LANES), q)
    for c in range(tiles // LANES):
        chunk = interp[:, c * LANES : (c + 1) * LANES]
        for i in range(groups):
            wide = None
            for h in range(groups):
                piece = turn(chunk, (h - i) * q)
                wide = piece if wide is None else jnp.where(group == h, piece, wide)
            interp_ref[c * groups + i] = wide

    def block_values(b, carry):
        rows = pl.ds(pl.multiple_of(b * q, SUB), q)
        interp = interp_ref[b]
        total = views[0][rows, :] * interp[0:1]
        for p in range(1, params):
            total = total + views[p][rows, :] * interp[p : p + 1]
        sent_ref[rows, :] = total
        return carry

    lax.fori_loop(0, tiles // q, block_values, 0)


def first_kernel(
    q,
    n_det,
    params,
    me_ref,
    gathered_ref,
    table_ref,
    grad_ref,
    norm_ref,
    sent_ref,
    weight_ref,
    edge_ref,
    interp_ref,
):
    n_track = grad_ref.shape[0]
    tiles = sent_ref.shape[0]

    def put(b, field):
        grad_ref[b] = field

    field_sums(gathered_ref, n_track, n_det, params, put)
    norm_ref[...] = jnp.broadcast_to(full_dot(grad_ref, grad_ref), norm_ref.shape)
    wide = table_weights(table_ref, params, tiles)
    edge = sum(part[KNOT_DEV : KNOT_DEV + SUB] for part in reversed(wide))
    edge_ref[...] = edge
    parts = [part.astype(jnp.bfloat16) for part in wide]
    for index, part in enumerate(parts):
        weight_ref[index] = part
    upper = [part[0:KNOT_DEV] for part in parts]
    views = table_views(table_ref, params, tiles)
    predict(me_ref[0], q, grad_ref, views, upper, edge[0:1], interp_ref, sent_ref)


def step_kernel(
    q,
    n_det,
    params,
    me_ref,
    gathered_ref,
    table_ref,
    weight_ref,
    edge_ref,
    grad_ref,
    direction_ref,
    norm_ref,
    knot_ref,
    direction_out,
    norm_out,
    knot_out,
    length_out,
    sent_ref,
    grad_out,
    image_ref,
    interp_ref,
):
    n_track = grad_ref.shape[0]
    me = me_ref[0]

    def put(b, field):
        image_ref[b] = field + damping * direction_ref[b]

    field_sums(gathered_ref, n_track, n_det, params, put)
    norm = norm_ref[0:1, 0:1]
    length = norm / full_dot(direction_ref, image_ref)
    length_out[...] = jnp.broadcast_to(length, length_out.shape)
    knot_out[...] = knot_ref[...] + length * direction_ref[me]
    for b in range(n_track):
        grad_out[b] = grad_ref[b] - length * image_ref[b]
    new_norm = full_dot(grad_out, grad_out)
    norm_out[...] = jnp.broadcast_to(new_norm, norm_out.shape)
    ratio = new_norm / norm
    for b in range(n_track):
        direction_out[b] = grad_out[b] + ratio * direction_ref[b]
    views = table_views(table_ref, params, sent_ref.shape[0])
    parts = [weight_ref[index, 0:KNOT_DEV, :] for index in range(3)]
    predict(me, q, direction_out, views, parts, edge_ref[0:1, :], interp_ref, sent_ref)


def last_kernel(q, me_ref, sent_ref, arrived_ref, diff_ref, send_ref):
    difference(me_ref[0], sent_ref, arrived_ref, diff_ref, q)
    diff = diff_ref[...]
    squares = jnp.sum(diff * diff, axis=0, keepdims=True)
    send_ref[...] = jnp.broadcast_to(squares[None], send_ref.shape)


def restore_kernel(q, me_ref, match_hbm, misfit_ref, diff_ref, *refs):
    steps = (len(refs) - 5) // 2
    residual_out, diff_out, residual_ref, match_ref, sem = refs[2 * steps :]
    tiles = misfit_ref.shape[0]
    copy = pltpu.make_async_copy(match_hbm, match_ref, sem)
    copy.start()
    copy.wait()
    perm = crossing_order(me_ref[0], match_ref[...])
    residual = misfit_ref[...]
    for length_ref, change_ref in zip(refs[:steps], refs[steps : 2 * steps]):
        residual = residual - length_ref[0:1, 0:1] * change_ref[...]
    residual_ref[...] = residual
    for source, target in ((residual_ref, residual_out), (diff_ref, diff_out)):
        target[...] = from_crossing(
            lambda index: source[index * q : (index + 1) * q, :], perm, q, tiles
        )


def finish_kernel(
    me_ref, squares_ref, direction_ref, norm_ref, knot_ref, residual_ref, diff_ref, knot_out, residual_out
):
    params = knot_out.shape[0]
    squares = squares_ref[0]
    for d in range(1, squares_ref.shape[0]):
        squares = squares + squares_ref[d]
    curvature = 0.5 * jnp.sum(squares, keepdims=True) + damping * full_dot(
        direction_ref, direction_ref
    )
    length = norm_ref[0:1, 0:1] / curvature
    knot = knot_ref[...] + length * direction_ref[me_ref[0]]
    knot_out[...] = knot[0:params]
    residual_out[...] = residual_ref[...] - length * diff_ref[...]


def call(kernel, outs, ins, scratch=()):
    return pl.pallas_call(
        kernel,
        out_shape=outs,
        in_specs=ins,
        out_specs=jax.tree.map(lambda _: VMEM, outs),
        scratch_shapes=list(scratch),
        compiler_params=PARAMS,
    )


def local(jac, obs, match, tile_knot, tile_frac):
    tiles, params, columns = jac.shape
    n_track = lax.axis_size("track")
    n_det = lax.axis_size("det")
    n_all = n_track * n_det
    q = tiles // n_track
    me = lax.axis_index("track").astype(jnp.int32).reshape(1)

    def crossing(values):
        return lax.all_to_all(values, "track", split_axis=0, concat_axis=0, tiled=True)

    def everywhere(values):
        return lax.all_to_all(values, ("track", "det"), split_axis=0, concat_axis=0, tiled=True)

    match_row = from_hbm(match[None])
    int_row = pltpu.VMEM((1, tiles), jnp.int32)
    sent = call(
        functools.partial(order_kernel, q),
        f32(tiles, columns),
        [SMEM, ANY, ANY],
        [int_row, pltpu.VMEM((tiles, columns), jnp.float32), pltpu.SemaphoreType.DMA((2,))],
    )(me, match_row, from_hbm(obs))
    arrived = crossing(sent)
    table = call(
        functools.partial(table_kernel, q, math.gcd(params, 3)),
        kept((table_rows(params, tiles), columns)),
        [SMEM] + [ANY] * 5,
        [
            int_row,
            int_row,
            pltpu.VMEM((1, tiles), jnp.float32),
            pltpu.SemaphoreType.DMA((4 + params,)),
        ],
    )(
        me,
        match_row,
        *map(from_hbm, (tile_knot[None], tile_frac[None], sent, jnp.transpose(jac, (1, 0, 2)))),
    )

    field = f32(n_track, PAD, LANES)
    scalar = f32(SUB, LANES)
    interp = pltpu.VMEM((n_track, PAD, LANES), jnp.float32)
    adjoint_out = (f32(tiles, columns), f32(n_all, PAD, LANES))
    values = [pltpu.VMEM((PAD, tiles), jnp.float32)]
    misfit, payload = call(
        functools.partial(first_adjoint_kernel, q, params), adjoint_out, [SMEM] + [VMEM] * 2, values
    )(me, arrived, table)
    gradient, slope_norm, sent, weights, edge = call(
        functools.partial(first_kernel, q, n_det, params),
        (
            field,
            scalar,
            f32(tiles, columns),
            jax.ShapeDtypeStruct((3, KNOT_DEV + PAD, tiles), jnp.bfloat16),
            f32(SUB, tiles),
        ),
        [SMEM] + [VMEM] * 2,
        [interp],
    )(me, everywhere(payload), table)
    direction = gradient
    knot_field = jnp.zeros((PAD, KNOT_DEV), jnp.float32)
    lengths, changes = [], []
    for iteration in range(ITERS - 1):
        change, payload = call(
            functools.partial(adjoint_kernel, q, params), adjoint_out, [SMEM] + [VMEM] * 4, values
        )(me, sent, crossing(sent), table, weights)
        gathered = everywhere(payload)
        last = iteration == ITERS - 2
        results = call(
            functools.partial(step_kernel, q, n_det, params),
            (field, scalar, f32(PAD, KNOT_DEV), scalar, f32(tiles, columns))
            + (() if last else (field,)),
            [SMEM] + [VMEM] * 8,
            [interp] * (3 if last else 2),
        )(
            me, gathered, table, weights, edge, gradient, direction, slope_norm, knot_field
        )
        direction, slope_norm, knot_field, length, sent = results[:5]
        gradient = None if last else results[5]
        lengths.append(length)
        changes.append(change)
    change, squares = call(
        functools.partial(last_kernel, q),
        (f32(tiles, columns), f32(n_all, 1, LANES)),
        [SMEM] + [VMEM] * 2,
    )(me, sent, crossing(sent))
    squares = everywhere(squares)
    residual, change = call(
        functools.partial(restore_kernel, q),
        (f32(tiles, columns), f32(tiles, columns)),
        [SMEM, ANY] + [VMEM] * (2 + 2 * len(changes)),
        [pltpu.VMEM((tiles, columns), jnp.float32), int_row, pltpu.SemaphoreType.DMA],
    )(me, match_row, misfit, change, *lengths, *changes)
    return call(
        finish_kernel,
        (f32(params, KNOT_DEV), f32(tiles, columns)),
        [SMEM] + [VMEM] * 6,
    )(me, squares, direction, slope_norm, knot_field, residual, change)


def solution(mesh):
    in_specs = (P("track", None, "det"), P("track", "det"), P("track"), P("track"), P("track"))
    out_specs = (P(None, "track"), P("track", "det"))
    return jax.shard_map(local, mesh=mesh, in_specs=in_specs, out_specs=out_specs, check_vma=False)
```

```python
import functools
import math

import jax
import jax.numpy as jnp
from jax import lax
from jax.experimental import pallas as pl
from jax.experimental.pallas import tpu as pltpu
from jax.sharding import PartitionSpec as P

KNOT_DEV = 128
ITERS = 4
LANES = 128
SUB = 8
PAD = 16
VMEM_BYTES = 6 * 2**20


damping = 1.0

SMEM = pl.BlockSpec(memory_space=pltpu.SMEM)
VMEM = pl.BlockSpec(memory_space=pltpu.VMEM)
ANY = pl.BlockSpec(memory_space=pl.ANY)
PARAMS = pltpu.CompilerParams(vmem_limit_bytes=VMEM_BYTES)
HIGHEST = lax.Precision.HIGHEST


def kept(shape, dtype=jnp.float32):
    return pltpu.VMEM(shape, dtype)


def from_hbm(x):
    return pltpu.with_memory_space_constraint(x, pltpu.HBM)


def f32(*shape):
    return jax.ShapeDtypeStruct(shape, jnp.float32)


def dot(a, b, dims):
    return lax.dot_general(
        a, b, (dims, ((), ())), precision=HIGHEST, preferred_element_type=jnp.float32
    )


def split3(x):
    first = x.astype(jnp.bfloat16)
    rest = x - first.astype(jnp.float32)
    second = rest.astype(jnp.bfloat16)
    third = (rest - second.astype(jnp.float32)).astype(jnp.bfloat16)
    return first, second, third


def bf16_dot(a, b):
    return jnp.dot(a, b, preferred_element_type=jnp.float32)


def turn(x, shift):
    shift = shift % LANES
    return x if shift == 0 else pltpu.roll(x, shift, 1)


def lane_group(shape, q):
    return lax.broadcasted_iota(jnp.int32, shape, 1) // q


def to_crossing(arrays, perm, q, store):
    tiles = arrays[0].shape[0]
    groups = LANES // q
    stacked = []
    for x in arrays:
        across = jnp.concatenate(
            [x[c * LANES : (c + 1) * LANES].T for c in range(tiles // LANES)], axis=1
        )
        stacked.extend(split3(across))
    moved = bf16_dot(jnp.concatenate(stacked, axis=0), perm)
    group = lane_group((q, LANES), q)
    for index in range(len(arrays)):
        third, second, first = (
            moved[(3 * index + part) * LANES : (3 * index + part + 1) * LANES] for part in (2, 1, 0)
        )
        whole = third + second + first
        for c in range(tiles // LANES):
            for b in range(groups):
                block = None
                for h in range(groups):
                    piece = turn(
                        whole[h * q : (h + 1) * q, c * LANES : (c + 1) * LANES], (h - b) * q
                    )
                    block = piece if block is None else jnp.where(group == h, piece, block)
                store(index, c * groups + b, block)


def from_crossing(load, perm, q, tiles):
    groups = LANES // q
    group = lane_group((q, LANES), q)
    parts = []
    for c in range(tiles // LANES):
        rows = []
        for h in range(groups):
            block = None
            for b in range(groups):
                piece = turn(load(c * groups + b), (b - h) * q)
                block = piece if block is None else jnp.where(group == b, piece, block)
            rows.append(block)
        parts.append(jnp.concatenate(rows, axis=0).T)
    stacked = jnp.concatenate(parts, axis=0)
    return sum(bf16_dot(perm, part) for part in reversed(split3(stacked)))


def crossing_order(me, match):
    tiles = match.shape[1]
    slot = lax.broadcasted_iota(jnp.int32, (1, tiles), 1)
    peer = match // tiles
    other = match - peer * tiles
    inner = jnp.where(
        peer == me,
        jnp.minimum(slot, other) + jnp.where(slot > other, tiles, 0),
        jnp.where(peer > me, slot, other),
    )
    key = (peer * (2 * tiles) + inner).astype(jnp.float32)
    key_cols = jnp.broadcast_to(key, (LANES, tiles)).T[:, :1]
    place = jnp.sum(jnp.where(key < key_cols, 1.0, 0.0), axis=1, keepdims=True)
    cols = lax.broadcasted_iota(jnp.int32, (tiles, tiles), 1).astype(jnp.float32)
    return jnp.where(place == cols, 1.0, 0.0).astype(jnp.bfloat16)


def order_kernel(q, me_ref, match_hbm, obs_hbm, obs_out, match_ref, obs_ref, sems):
    copies = [
        pltpu.make_async_copy(match_hbm, match_ref, sems.at[0]),
        pltpu.make_async_copy(obs_hbm, obs_ref, sems.at[1]),
    ]
    for copy in copies:
        copy.start()
    copies[0].wait()
    perm = crossing_order(me_ref[0], match_ref[...])
    copies[1].wait()

    def put(_, index, block):
        obs_out[index * q : (index + 1) * q, :] = block

    to_crossing([obs_ref[...]], perm, q, put)


def rows_kernel(
    q,
    together,
    me_ref,
    match_hbm,
    knot_hbm,
    frac_hbm,
    _,
    jac_hbm,
    rows_ref,
    weight_ref,
    match_ref,
    knot_ref,
    frac_ref,
    sems,
):
    params, tiles = jac_hbm.shape[:2]
    pairs = [(match_hbm, match_ref), (knot_hbm, knot_ref), (frac_hbm, frac_ref)]
    pairs += [(jac_hbm.at[p], rows_ref.at[p]) for p in range(params)]
    copies = [
        pltpu.make_async_copy(source, target, sems.at[index])
        for index, (source, target) in enumerate(pairs)
    ]
    for copy in copies:
        copy.start()
    for copy in copies[:3]:
        copy.wait()
    perm = crossing_order(me_ref[0], match_ref[...])
    row = lax.broadcasted_iota(jnp.int32, (SUB, tiles), 0)
    facts = jnp.where(row == 0, knot_ref[...].astype(jnp.float32), frac_ref[...])
    moved = sum(bf16_dot(part, perm) for part in reversed(split3(facts)))
    knot, frac = moved[0:1], moved[1:2]
    knots = lax.broadcasted_iota(jnp.int32, (KNOT_DEV, tiles), 0).astype(jnp.float32)
    main = jnp.where(knots == knot, 1.0 - frac, 0.0) + jnp.where(knots == knot + 1.0, frac, 0.0)
    first_row = lax.broadcasted_iota(jnp.int32, (PAD, tiles), 0) == 0
    edge = jnp.where(first_row, jnp.where(knot == KNOT_DEV - 1.0, frac, 0.0), 0.0)
    for index, (upper, lower) in enumerate(zip(split3(main), split3(edge))):
        weight_ref[index, 0:KNOT_DEV, :] = upper
        weight_ref[index, KNOT_DEV : KNOT_DEV + PAD, :] = lower

    for first in range(0, params, together):
        for p in range(first, first + together):
            copies[3 + p].wait()

        def put(index, block_index, block):
            rows_ref[first + index, block_index * q : (block_index + 1) * q, :] = block

        to_crossing([rows_ref[p] for p in range(first, first + together)], perm, q, put)


def weight_dot(x, parts, over_tiles):
    dims = (((1,), (1 if over_tiles else 0,)), ((), ()))
    stacked = jnp.concatenate(split3(x), axis=0)
    first, second, third = (
        lax.dot_general(
            stacked[0 : (3 - index) * PAD], part, dims, preferred_element_type=jnp.float32
        )
        for index, part in enumerate(parts)
    )
    small = third + second[PAD : 2 * PAD] + first[2 * PAD : 3 * PAD]
    return (small + (second[0:PAD] + first[PAD : 2 * PAD])) + first[0:PAD]


def row_sums(parts):
    row = lax.broadcasted_iota(jnp.int32, (SUB, LANES), 0)
    level = list(parts)
    zero = jnp.zeros((SUB, LANES), jnp.float32)
    while len(level) % SUB:
        level.append(zero)
    for distance in (1, 2, 4):
        first = (row // distance) % 2 == 0
        level = [
            jnp.where(first, a, b) + pltpu.roll(jnp.where(first, b, a), distance, 0)
            for a, b in zip(level[::2], level[1::2])
        ]
    return level[0] if len(level) == 1 else jnp.concatenate(level, axis=0)


def fold_rows(x):
    total = x[0:SUB]
    for step in range(1, x.shape[0] // SUB):
        total = total + x[step * SUB : (step + 1) * SUB]
    return total


def fold_lanes(x, q):
    shift = q
    while shift < LANES:
        x = x + pltpu.roll(x, shift, 1)
        shift *= 2
    return x


def crossing_values(me, arrived_ref, out_ref, q):
    out_ref[...] = arrived_ref[...]
    own = arrived_ref[pl.ds(pl.multiple_of(me * q, SUB), q), :]
    lane = lax.broadcasted_iota(jnp.int32, (q, LANES), 1)
    swapped = jnp.where(lane % q < q // 2, turn(own, -(q // 2)), turn(own, q // 2))
    out_ref[pl.ds(pl.multiple_of(me * q, SUB), q), :] = swapped


def difference(me, sent_ref, arrived_ref, out_ref, q):
    crossing_values(me, arrived_ref, out_ref, q)
    out_ref[...] = sent_ref[...] - out_ref[...]


def first_adjoint_kernel(
    q,
    me_ref,
    arrived_ref,
    rows_ref,
    sent_hbm,
    weight_hbm,
    diff_ref,
    send_ref,
    weight_ref,
    values_ref,
    sent_ref,
    sems,
):
    copies = [
        pltpu.make_async_copy(sent_hbm, sent_ref, sems.at[0]),
        pltpu.make_async_copy(weight_hbm, weight_ref, sems.at[1]),
    ]
    for copy in copies:
        copy.start()
    copies[0].wait()
    difference(me_ref[0], sent_ref, arrived_ref, diff_ref, q)
    adjoint_values(q, diff_ref, rows_ref, values_ref)
    copies[1].wait()
    adjoint_rows(rows_ref.shape[0], values_ref, weight_ref, send_ref)


def adjoint_kernel(
    q, me_ref, sent_ref, arrived_ref, rows_ref, weight_ref, diff_ref, send_ref, values_ref
):
    difference(me_ref[0], sent_ref, arrived_ref, diff_ref, q)
    adjoint_values(q, diff_ref, rows_ref, values_ref)
    adjoint_rows(rows_ref.shape[0], values_ref, weight_ref, send_ref)


def adjoint_values(q, diff_ref, jac_ref, values_ref):
    params, tiles, _ = jac_ref.shape
    groups = LANES // q
    group = lane_group((PAD, LANES), q)
    for c in range(tiles // LANES):
        values = None
        for i in range(groups):
            rows = slice((c * groups + i) * q, (c * groups + i + 1) * q)
            diff = diff_ref[rows, :]
            sums = fold_lanes(
                row_sums([fold_rows(jac_ref[p, rows, :] * diff) for p in range(params)]), q
            )
            values = sums if values is None else jnp.where(group == i, sums, values)
        values_ref[:, c * LANES : (c + 1) * LANES] = values


def adjoint_rows(params, values_ref, weight_ref, send_ref):
    spread = weight_dot(values_ref[...], [weight_ref[index] for index in range(3)], True)
    lane = lax.broadcasted_iota(jnp.int32, (PAD, LANES), 1)
    row = lax.broadcasted_iota(jnp.int32, (PAD, LANES), 0)
    spill = jnp.sum(
        jnp.where(lane == row, spread[:, KNOT_DEV : KNOT_DEV + 1], 0.0), axis=0, keepdims=True
    )
    block = jnp.where(row < params, spread[:, :KNOT_DEV], jnp.where(row == params, spill, 0.0))
    for d in range(send_ref.shape[0]):
        send_ref[d] = block


def field_sums(gathered_ref, n_track, n_det, params, store, base=0):
    lane = lax.broadcasted_iota(jnp.int32, (PAD, LANES), 1)
    row = lax.broadcasted_iota(jnp.int32, (PAD, LANES), 0)
    spill = jnp.zeros((PAD, 1), jnp.float32)
    for b in range(n_track):
        total = gathered_ref[b * n_det, base : base + PAD, :]
        for d in range(1, n_det):
            total = total + gathered_ref[b * n_det + d, base : base + PAD, :]
        field = jnp.where(row < params, total, 0.0)
        field = field + jnp.where(lane == 0, spill, 0.0)
        store(b, field)
        spill = jnp.sum(
            jnp.where((lane == row) & (row < params), total[params : params + 1], 0.0),
            axis=1,
            keepdims=True,
        )


def total_of(x):
    return jnp.sum(jnp.sum(x, axis=0), keepdims=True).reshape(1, 1)


def full_dot(a_ref, b_ref):
    total = a_ref[0] * b_ref[0]
    for b in range(1, a_ref.shape[0]):
        total = total + a_ref[b] * b_ref[b]
    return jnp.sum(total, keepdims=True)


def predict(me, q, direction_ref, jac_ref, parts, edge, interp_ref, sent_ref):
    params, tiles, _ = jac_ref.shape
    n_track = direction_ref.shape[0]
    following = direction_ref[jnp.minimum(me + 1, n_track - 1)][:, 0:1]
    following = jnp.where(me + 1 < n_track, following, 0.0)
    interp = weight_dot(direction_ref[me], parts, False) + following * edge
    groups = LANES // q
    group = lane_group((PAD, LANES), q)
    for c in range(tiles // LANES):
        chunk = interp[:, c * LANES : (c + 1) * LANES]
        for i in range(groups):
            wide = None
            for h in range(groups):
                piece = turn(chunk, (h - i) * q)
                wide = piece if wide is None else jnp.where(group == h, piece, wide)
            interp_ref[c * groups + i] = wide

    def block_values(b, carry):
        rows = pl.ds(pl.multiple_of(b * q, SUB), q)
        interp = interp_ref[b]
        total = jac_ref[0, rows, :] * interp[0:1]
        for p in range(1, params):
            total = total + jac_ref[p, rows, :] * interp[p : p + 1]
        sent_ref[rows, :] = total
        return carry

    lax.fori_loop(0, tiles // q, block_values, 0)


def first_kernel(
    q,
    n_det,
    me_ref,
    gathered_ref,
    rows_ref,
    weight_ref,
    grad_ref,
    norm_ref,
    sent_ref,
    edge_ref,
    interp_ref,
):
    n_track = grad_ref.shape[0]

    def put(b, field):
        grad_ref[b] = field

    field_sums(gathered_ref, n_track, n_det, rows_ref.shape[0], put)
    norm_ref[...] = jnp.broadcast_to(full_dot(grad_ref, grad_ref), norm_ref.shape)
    edge = sum(
        weight_ref[index, KNOT_DEV : KNOT_DEV + PAD, :].astype(jnp.float32) for index in (2, 1, 0)
    )[0:SUB]
    edge_ref[...] = edge
    parts = [weight_ref[index, 0:KNOT_DEV, :] for index in range(3)]
    predict(me_ref[0], q, grad_ref, rows_ref, parts, edge[0:1], interp_ref, sent_ref)


def step_kernel(
    q,
    n_det,
    me_ref,
    gathered_ref,
    rows_ref,
    weight_ref,
    edge_ref,
    grad_ref,
    direction_ref,
    norm_ref,
    knot_ref,
    direction_out,
    norm_out,
    knot_out,
    length_out,
    sent_ref,
    grad_out,
    image_ref,
    interp_ref,
):
    n_track = grad_ref.shape[0]
    me = me_ref[0]

    def put(b, field):
        image_ref[b] = field + damping * direction_ref[b]

    field_sums(gathered_ref, n_track, n_det, rows_ref.shape[0], put)
    norm = norm_ref[0:1, 0:1]
    length = norm / full_dot(direction_ref, image_ref)
    length_out[...] = jnp.broadcast_to(length, length_out.shape)
    knot_out[...] = knot_ref[...] + length * direction_ref[me]
    for b in range(n_track):
        grad_out[b] = grad_ref[b] - length * image_ref[b]
    new_norm = full_dot(grad_out, grad_out)
    norm_out[...] = jnp.broadcast_to(new_norm, norm_out.shape)
    ratio = new_norm / norm
    for b in range(n_track):
        direction_out[b] = grad_out[b] + ratio * direction_ref[b]
    parts = [weight_ref[index, 0:KNOT_DEV, :] for index in range(3)]
    predict(me, q, direction_out, rows_ref, parts, edge_ref[0:1, :], interp_ref, sent_ref)


def last_kernel(q, me_ref, sent_ref, arrived_ref, diff_ref, send_ref):
    difference(me_ref[0], sent_ref, arrived_ref, diff_ref, q)
    diff = diff_ref[...]
    squares = jnp.sum(diff * diff, axis=0, keepdims=True)
    send_ref[...] = jnp.broadcast_to(squares[None], send_ref.shape)


def restore_kernel(q, me_ref, match_hbm, misfit_ref, diff_ref, *refs):
    steps = (len(refs) - 5) // 2
    residual_out, diff_out, residual_ref, match_ref, sem = refs[2 * steps :]
    tiles = misfit_ref.shape[0]
    copy = pltpu.make_async_copy(match_hbm, match_ref, sem)
    copy.start()
    copy.wait()
    perm = crossing_order(me_ref[0], match_ref[...])
    residual = misfit_ref[...]
    for length_ref, change_ref in zip(refs[:steps], refs[steps : 2 * steps]):
        residual = residual - length_ref[0:1, 0:1] * change_ref[...]
    residual_ref[...] = residual
    for source, target in ((residual_ref, residual_out), (diff_ref, diff_out)):
        target[...] = from_crossing(
            lambda index: source[index * q : (index + 1) * q, :], perm, q, tiles
        )


def finish_kernel(
    me_ref, squares_ref, direction_ref, norm_ref, knot_ref, residual_ref, diff_ref, knot_out, residual_out
):
    params = knot_out.shape[0]
    squares = squares_ref[0]
    for d in range(1, squares_ref.shape[0]):
        squares = squares + squares_ref[d]
    curvature = 0.5 * jnp.sum(squares, keepdims=True) + damping * full_dot(
        direction_ref, direction_ref
    )
    length = norm_ref[0:1, 0:1] / curvature
    knot = knot_ref[...] + length * direction_ref[me_ref[0]]
    knot_out[...] = knot[0:params]
    residual_out[...] = residual_ref[...] - length * diff_ref[...]


def call(kernel, outs, ins, scratch=()):
    return pl.pallas_call(
        kernel,
        out_shape=outs,
        in_specs=ins,
        out_specs=jax.tree.map(lambda _: VMEM, outs),
        scratch_shapes=list(scratch),
        compiler_params=PARAMS,
    )


def local(jac, obs, match, tile_knot, tile_frac):
    tiles, params, columns = jac.shape
    n_track = lax.axis_size("track")
    n_det = lax.axis_size("det")
    n_all = n_track * n_det
    q = tiles // n_track
    me = lax.axis_index("track").astype(jnp.int32).reshape(1)

    def crossing(values):
        return lax.all_to_all(values, "track", split_axis=0, concat_axis=0, tiled=True)

    def everywhere(values):
        return lax.all_to_all(values, ("track", "det"), split_axis=0, concat_axis=0, tiled=True)

    match_row = from_hbm(match[None])
    int_row = pltpu.VMEM((1, tiles), jnp.int32)
    sent = call(
        functools.partial(order_kernel, q),
        f32(tiles, columns),
        [SMEM, ANY, ANY],
        [int_row, pltpu.VMEM((tiles, columns), jnp.float32), pltpu.SemaphoreType.DMA((2,))],
    )(me, match_row, from_hbm(obs))
    arrived = crossing(sent)
    weight_shape = (3, KNOT_DEV + PAD, tiles)
    rows, weights = call(
        functools.partial(rows_kernel, q, math.gcd(params, 3)),
        (kept((params, tiles, columns)), pltpu.HBM(weight_shape, jnp.bfloat16)),
        [SMEM] + [ANY] * 5,
        [
            int_row,
            int_row,
            pltpu.VMEM((1, tiles), jnp.float32),
            pltpu.SemaphoreType.DMA((3 + params,)),
        ],
    )(
        me,
        match_row,
        *map(from_hbm, (tile_knot[None], tile_frac[None], sent, jnp.transpose(jac, (1, 0, 2)))),
    )

    field = f32(n_track, PAD, LANES)
    scalar = f32(SUB, LANES)
    interp = pltpu.VMEM((n_track, PAD, LANES), jnp.float32)
    adjoint_out = (f32(tiles, columns), f32(n_all, PAD, LANES))
    values = pltpu.VMEM((PAD, tiles), jnp.float32)
    misfit, payload, weights = call(
        functools.partial(first_adjoint_kernel, q),
        adjoint_out + (jax.ShapeDtypeStruct(weight_shape, jnp.bfloat16),),
        [SMEM, VMEM, VMEM, ANY, ANY],
        [values, pltpu.VMEM((tiles, columns), jnp.float32), pltpu.SemaphoreType.DMA((2,))],
    )(me, arrived, rows, from_hbm(sent), from_hbm(weights))
    gradient, slope_norm, sent, edge = call(
        functools.partial(first_kernel, q, n_det),
        (field, scalar, f32(tiles, columns), f32(SUB, tiles)),
        [SMEM] + [VMEM] * 3,
        [interp],
    )(me, everywhere(payload), rows, weights)
    direction = gradient
    knot_field = jnp.zeros((PAD, KNOT_DEV), jnp.float32)
    lengths, changes = [], []
    for iteration in range(ITERS - 1):
        change, payload = call(
            functools.partial(adjoint_kernel, q), adjoint_out, [SMEM] + [VMEM] * 4, [values]
        )(me, sent, crossing(sent), rows, weights)
        gathered = everywhere(payload)
        last = iteration == ITERS - 2
        results = call(
            functools.partial(step_kernel, q, n_det),
            (field, scalar, f32(PAD, KNOT_DEV), scalar, f32(tiles, columns))
            + (() if last else (field,)),
            [SMEM] + [VMEM] * 8,
            [interp] * (3 if last else 2),
        )(
            me, gathered, rows, weights, edge, gradient, direction, slope_norm, knot_field
        )
        direction, slope_norm, knot_field, length, sent = results[:5]
        gradient = None if last else results[5]
        lengths.append(length)
        changes.append(change)
    change, squares = call(
        functools.partial(last_kernel, q),
        (f32(tiles, columns), f32(n_all, 1, LANES)),
        [SMEM] + [VMEM] * 2,
    )(me, sent, crossing(sent))
    squares = everywhere(squares)
    residual, change = call(
        functools.partial(restore_kernel, q),
        (f32(tiles, columns), f32(tiles, columns)),
        [SMEM, ANY] + [VMEM] * (2 + 2 * len(changes)),
        [pltpu.VMEM((tiles, columns), jnp.float32), int_row, pltpu.SemaphoreType.DMA],
    )(me, match_row, misfit, change, *lengths, *changes)
    return call(
        finish_kernel,
        (f32(params, KNOT_DEV), f32(tiles, columns)),
        [SMEM] + [VMEM] * 6,
    )(me, squares, direction, slope_norm, knot_field, residual, change)


def solution(mesh):
    in_specs = (P("track", None, "det"), P("track", "det"), P("track"), P("track"), P("track"))
    out_specs = (P(None, "track"), P("track", "det"))
    return jax.shard_map(local, mesh=mesh, in_specs=in_specs, out_specs=out_specs, check_vma=False)
```

```python
import functools
import math

import jax
import jax.numpy as jnp
from jax import lax
from jax.experimental import pallas as pl
from jax.experimental.pallas import tpu as pltpu
from jax.sharding import PartitionSpec as P

KNOT_DEV = 128
ITERS = 4
LANES = 128
SUB = 8
PAD = 16
VMEM_BYTES = 6 * 2**20


damping = 1.0

SMEM = pl.BlockSpec(memory_space=pltpu.SMEM)
VMEM = pl.BlockSpec(memory_space=pltpu.VMEM)
ANY = pl.BlockSpec(memory_space=pl.ANY)
PARAMS = pltpu.CompilerParams(vmem_limit_bytes=VMEM_BYTES)
HIGHEST = lax.Precision.HIGHEST


def kept(shape, dtype=jnp.float32):
    return pltpu.VMEM(shape, dtype)


def from_hbm(x):
    return pltpu.with_memory_space_constraint(x, pltpu.HBM)


def f32(*shape):
    return jax.ShapeDtypeStruct(shape, jnp.float32)


def dot(a, b, dims):
    return lax.dot_general(
        a, b, (dims, ((), ())), precision=HIGHEST, preferred_element_type=jnp.float32
    )


def split3(x):
    first = x.astype(jnp.bfloat16)
    rest = x - first.astype(jnp.float32)
    second = rest.astype(jnp.bfloat16)
    third = (rest - second.astype(jnp.float32)).astype(jnp.bfloat16)
    return first, second, third


def bf16_dot(a, b):
    return jnp.dot(a, b, preferred_element_type=jnp.float32)


def turn(x, shift):
    shift = shift % LANES
    return x if shift == 0 else pltpu.roll(x, shift, 1)


def lane_group(shape, q):
    return lax.broadcasted_iota(jnp.int32, shape, 1) // q


def to_crossing(arrays, perm, q, store):
    tiles = arrays[0].shape[0]
    groups = LANES // q
    stacked = []
    for x in arrays:
        across = jnp.concatenate(
            [x[c * LANES : (c + 1) * LANES].T for c in range(tiles // LANES)], axis=1
        )
        stacked.extend(split3(across))
    moved = bf16_dot(jnp.concatenate(stacked, axis=0), perm)
    group = lane_group((q, LANES), q)
    for index in range(len(arrays)):
        third, second, first = (
            moved[(3 * index + part) * LANES : (3 * index + part + 1) * LANES] for part in (2, 1, 0)
        )
        whole = third + second + first
        for c in range(tiles // LANES):
            for b in range(groups):
                block = None
                for h in range(groups):
                    piece = turn(
                        whole[h * q : (h + 1) * q, c * LANES : (c + 1) * LANES], (h - b) * q
                    )
                    block = piece if block is None else jnp.where(group == h, piece, block)
                store(index, c * groups + b, block)


def from_crossing(load, perm, q, tiles):
    groups = LANES // q
    group = lane_group((q, LANES), q)
    parts = []
    for c in range(tiles // LANES):
        rows = []
        for h in range(groups):
            block = None
            for b in range(groups):
                piece = turn(load(c * groups + b), (b - h) * q)
                block = piece if block is None else jnp.where(group == b, piece, block)
            rows.append(block)
        parts.append(jnp.concatenate(rows, axis=0).T)
    stacked = jnp.concatenate(parts, axis=0)
    return sum(bf16_dot(perm, part) for part in reversed(split3(stacked)))


def crossing_order(me, match):
    tiles = match.shape[1]
    slot = lax.broadcasted_iota(jnp.int32, (1, tiles), 1)
    peer = match // tiles
    other = match - peer * tiles
    inner = jnp.where(
        peer == me,
        jnp.minimum(slot, other) + jnp.where(slot > other, tiles, 0),
        jnp.where(peer > me, slot, other),
    )
    key = (peer * (2 * tiles) + inner).astype(jnp.float32)
    key_cols = jnp.broadcast_to(key, (LANES, tiles)).T[:, :1]
    place = jnp.sum(jnp.where(key < key_cols, 1.0, 0.0), axis=1, keepdims=True)
    cols = lax.broadcasted_iota(jnp.int32, (tiles, tiles), 1).astype(jnp.float32)
    return jnp.where(place == cols, 1.0, 0.0).astype(jnp.bfloat16)


def order_kernel(q, me_ref, match_hbm, obs_hbm, obs_out, match_ref, obs_ref, sems):
    copies = [
        pltpu.make_async_copy(match_hbm, match_ref, sems.at[0]),
        pltpu.make_async_copy(obs_hbm, obs_ref, sems.at[1]),
    ]
    for copy in copies:
        copy.start()
    copies[0].wait()
    perm = crossing_order(me_ref[0], match_ref[...])
    copies[1].wait()

    def put(_, index, block):
        obs_out[index * q : (index + 1) * q, :] = block

    to_crossing([obs_ref[...]], perm, q, put)


def rows_kernel(
    q,
    together,
    me_ref,
    match_hbm,
    knot_hbm,
    frac_hbm,
    _,
    jac_hbm,
    rows_ref,
    weight_ref,
    match_ref,
    knot_ref,
    frac_ref,
    sems,
):
    params, tiles = jac_hbm.shape[:2]
    pairs = [(match_hbm, match_ref), (knot_hbm, knot_ref), (frac_hbm, frac_ref)]
    pairs += [(jac_hbm.at[p], rows_ref.at[p]) for p in range(params)]
    copies = [
        pltpu.make_async_copy(source, target, sems.at[index])
        for index, (source, target) in enumerate(pairs)
    ]
    for copy in copies:
        copy.start()
    for copy in copies[:3]:
        copy.wait()
    perm = crossing_order(me_ref[0], match_ref[...])
    row = lax.broadcasted_iota(jnp.int32, (SUB, tiles), 0)
    facts = jnp.where(row == 0, knot_ref[...].astype(jnp.float32), frac_ref[...])
    moved = sum(bf16_dot(part, perm) for part in reversed(split3(facts)))
    knot, frac = moved[0:1], moved[1:2]
    knots = lax.broadcasted_iota(jnp.int32, (KNOT_DEV, tiles), 0).astype(jnp.float32)
    main = jnp.where(knots == knot, 1.0 - frac, 0.0) + jnp.where(knots == knot + 1.0, frac, 0.0)
    first_row = lax.broadcasted_iota(jnp.int32, (PAD, tiles), 0) == 0
    edge = jnp.where(first_row, jnp.where(knot == KNOT_DEV - 1.0, frac, 0.0), 0.0)
    for index, (upper, lower) in enumerate(zip(split3(main), split3(edge))):
        weight_ref[index, 0:KNOT_DEV, :] = upper
        weight_ref[index, KNOT_DEV : KNOT_DEV + PAD, :] = lower

    for first in range(0, params, together):
        for p in range(first, first + together):
            copies[3 + p].wait()

        def put(index, block_index, block):
            rows_ref[first + index, block_index * q : (block_index + 1) * q, :] = block

        to_crossing([rows_ref[p] for p in range(first, first + together)], perm, q, put)


def weight_dot(x, parts, over_tiles):
    dims = (((1,), (1 if over_tiles else 0,)), ((), ()))
    stacked = jnp.concatenate(split3(x), axis=0)
    first, second, third = (
        lax.dot_general(
            stacked[0 : (3 - index) * PAD], part, dims, preferred_element_type=jnp.float32
        )
        for index, part in enumerate(parts)
    )
    small = third + second[PAD : 2 * PAD] + first[2 * PAD : 3 * PAD]
    return (small + (second[0:PAD] + first[PAD : 2 * PAD])) + first[0:PAD]


def row_sums(parts):
    row = lax.broadcasted_iota(jnp.int32, (SUB, LANES), 0)
    level = list(parts)
    zero = jnp.zeros((SUB, LANES), jnp.float32)
    while len(level) % SUB:
        level.append(zero)
    for distance in (1, 2, 4):
        first = (row // distance) % 2 == 0
        level = [
            jnp.where(first, a, b) + pltpu.roll(jnp.where(first, b, a), distance, 0)
            for a, b in zip(level[::2], level[1::2])
        ]
    return level[0] if len(level) == 1 else jnp.concatenate(level, axis=0)


def fold_rows(x):
    total = x[0:SUB]
    for step in range(1, x.shape[0] // SUB):
        total = total + x[step * SUB : (step + 1) * SUB]
    return total


def fold_lanes(x, q):
    shift = q
    while shift < LANES:
        x = x + pltpu.roll(x, shift, 1)
        shift *= 2
    return x


def crossing_values(me, arrived_ref, out_ref, q):
    out_ref[...] = arrived_ref[...]
    own = arrived_ref[pl.ds(pl.multiple_of(me * q, SUB), q), :]
    lane = lax.broadcasted_iota(jnp.int32, (q, LANES), 1)
    swapped = jnp.where(lane % q < q // 2, turn(own, -(q // 2)), turn(own, q // 2))
    out_ref[pl.ds(pl.multiple_of(me * q, SUB), q), :] = swapped


def difference(me, sent_ref, arrived_ref, out_ref, q):
    crossing_values(me, arrived_ref, out_ref, q)
    out_ref[...] = sent_ref[...] - out_ref[...]


def first_adjoint_kernel(
    q,
    me_ref,
    arrived_ref,
    rows_ref,
    sent_hbm,
    weight_hbm,
    diff_hbm,
    send_ref,
    weight_ref,
    values_ref,
    diff_ref,
    sent_ref,
    sems,
):
    copies = [
        pltpu.make_async_copy(sent_hbm, sent_ref, sems.at[0]),
        pltpu.make_async_copy(weight_hbm, weight_ref, sems.at[1]),
    ]
    for copy in copies:
        copy.start()
    copies[0].wait()
    difference(me_ref[0], sent_ref, arrived_ref, diff_ref, q)
    out = pltpu.make_async_copy(diff_ref, diff_hbm, sems.at[2])
    out.start()
    adjoint_values(q, diff_ref, rows_ref, values_ref)
    copies[1].wait()
    adjoint_rows(rows_ref.shape[0], values_ref, weight_ref, send_ref)
    out.wait()


def adjoint_kernel(
    q,
    me_ref,
    sent_ref,
    arrived_ref,
    rows_ref,
    weight_ref,
    diff_hbm,
    send_ref,
    values_ref,
    diff_ref,
    sem,
):
    difference(me_ref[0], sent_ref, arrived_ref, diff_ref, q)
    out = pltpu.make_async_copy(diff_ref, diff_hbm, sem)
    out.start()
    adjoint_values(q, diff_ref, rows_ref, values_ref)
    adjoint_rows(rows_ref.shape[0], values_ref, weight_ref, send_ref)
    out.wait()


def adjoint_values(q, diff_ref, jac_ref, values_ref):
    params, tiles, _ = jac_ref.shape
    groups = LANES // q
    group = lane_group((PAD, LANES), q)
    for c in range(tiles // LANES):
        values = None
        for i in range(groups):
            rows = slice((c * groups + i) * q, (c * groups + i + 1) * q)
            diff = diff_ref[rows, :]
            sums = fold_lanes(
                row_sums([fold_rows(jac_ref[p, rows, :] * diff) for p in range(params)]), q
            )
            values = sums if values is None else jnp.where(group == i, sums, values)
        values_ref[:, c * LANES : (c + 1) * LANES] = values


def adjoint_rows(params, values_ref, weight_ref, send_ref):
    spread = weight_dot(values_ref[...], [weight_ref[index] for index in range(3)], True)
    lane = lax.broadcasted_iota(jnp.int32, (PAD, LANES), 1)
    row = lax.broadcasted_iota(jnp.int32, (PAD, LANES), 0)
    spill = jnp.sum(
        jnp.where(lane == row, spread[:, KNOT_DEV : KNOT_DEV + 1], 0.0), axis=0, keepdims=True
    )
    block = jnp.where(row < params, spread[:, :KNOT_DEV], jnp.where(row == params, spill, 0.0))
    for d in range(send_ref.shape[0]):
        send_ref[d] = block


def field_sums(gathered_ref, n_track, n_det, params, store, base=0):
    lane = lax.broadcasted_iota(jnp.int32, (PAD, LANES), 1)
    row = lax.broadcasted_iota(jnp.int32, (PAD, LANES), 0)
    spill = jnp.zeros((PAD, 1), jnp.float32)
    for b in range(n_track):
        total = gathered_ref[b * n_det, base : base + PAD, :]
        for d in range(1, n_det):
            total = total + gathered_ref[b * n_det + d, base : base + PAD, :]
        field = jnp.where(row < params, total, 0.0)
        field = field + jnp.where(lane == 0, spill, 0.0)
        store(b, field)
        spill = jnp.sum(
            jnp.where((lane == row) & (row < params), total[params : params + 1], 0.0),
            axis=1,
            keepdims=True,
        )


def total_of(x):
    return jnp.sum(jnp.sum(x, axis=0), keepdims=True).reshape(1, 1)


def full_dot(a_ref, b_ref):
    total = a_ref[0] * b_ref[0]
    for b in range(1, a_ref.shape[0]):
        total = total + a_ref[b] * b_ref[b]
    return jnp.sum(total, keepdims=True)


def predict(me, q, direction_ref, jac_ref, parts, edge, interp_ref, sent_ref):
    params, tiles, _ = jac_ref.shape
    n_track = direction_ref.shape[0]
    following = direction_ref[jnp.minimum(me + 1, n_track - 1)][:, 0:1]
    following = jnp.where(me + 1 < n_track, following, 0.0)
    interp = weight_dot(direction_ref[me], parts, False) + following * edge
    groups = LANES // q
    group = lane_group((PAD, LANES), q)
    for c in range(tiles // LANES):
        chunk = interp[:, c * LANES : (c + 1) * LANES]
        for i in range(groups):
            wide = None
            for h in range(groups):
                piece = turn(chunk, (h - i) * q)
                wide = piece if wide is None else jnp.where(group == h, piece, wide)
            interp_ref[c * groups + i] = wide

    def block_values(b, carry):
        rows = pl.ds(pl.multiple_of(b * q, SUB), q)
        interp = interp_ref[b]
        total = jac_ref[0, rows, :] * interp[0:1]
        for p in range(1, params):
            total = total + jac_ref[p, rows, :] * interp[p : p + 1]
        sent_ref[rows, :] = total
        return carry

    lax.fori_loop(0, tiles // q, block_values, 0)


def first_kernel(
    q,
    n_det,
    me_ref,
    gathered_ref,
    rows_ref,
    weight_ref,
    grad_ref,
    norm_ref,
    sent_ref,
    edge_ref,
    interp_ref,
):
    n_track = grad_ref.shape[0]

    def put(b, field):
        grad_ref[b] = field

    field_sums(gathered_ref, n_track, n_det, rows_ref.shape[0], put)
    norm_ref[...] = jnp.broadcast_to(full_dot(grad_ref, grad_ref), norm_ref.shape)
    edge = sum(
        weight_ref[index, KNOT_DEV : KNOT_DEV + PAD, :].astype(jnp.float32) for index in (2, 1, 0)
    )[0:SUB]
    edge_ref[...] = edge
    parts = [weight_ref[index, 0:KNOT_DEV, :] for index in range(3)]
    predict(me_ref[0], q, grad_ref, rows_ref, parts, edge[0:1], interp_ref, sent_ref)


def step_kernel(
    q,
    n_det,
    me_ref,
    gathered_ref,
    rows_ref,
    weight_ref,
    edge_ref,
    grad_ref,
    direction_ref,
    norm_ref,
    knot_ref,
    direction_out,
    norm_out,
    knot_out,
    length_out,
    sent_ref,
    grad_out,
    image_ref,
    interp_ref,
):
    n_track = grad_ref.shape[0]
    me = me_ref[0]

    def put(b, field):
        image_ref[b] = field + damping * direction_ref[b]

    field_sums(gathered_ref, n_track, n_det, rows_ref.shape[0], put)
    norm = norm_ref[0:1, 0:1]
    length = norm / full_dot(direction_ref, image_ref)
    length_out[...] = jnp.broadcast_to(length, length_out.shape)
    knot_out[...] = knot_ref[...] + length * direction_ref[me]
    for b in range(n_track):
        grad_out[b] = grad_ref[b] - length * image_ref[b]
    new_norm = full_dot(grad_out, grad_out)
    norm_out[...] = jnp.broadcast_to(new_norm, norm_out.shape)
    ratio = new_norm / norm
    for b in range(n_track):
        direction_out[b] = grad_out[b] + ratio * direction_ref[b]
    parts = [weight_ref[index, 0:KNOT_DEV, :] for index in range(3)]
    predict(me, q, direction_out, rows_ref, parts, edge_ref[0:1, :], interp_ref, sent_ref)


def last_kernel(q, me_ref, sent_ref, arrived_ref, diff_ref, send_ref):
    difference(me_ref[0], sent_ref, arrived_ref, diff_ref, q)
    diff = diff_ref[...]
    squares = jnp.sum(diff * diff, axis=0, keepdims=True)
    send_ref[...] = jnp.broadcast_to(squares[None], send_ref.shape)


def restore_kernel(q, me_ref, match_hbm, diff_ref, *refs):
    steps = (len(refs) - 7) // 2
    residual_out, diff_out, residual_ref, match_ref, held_ref, sems = refs[2 * steps + 1 :]
    tiles = diff_ref.shape[0]
    copies = [pltpu.make_async_copy(match_hbm, match_ref, sems.at[steps + 1])]
    for index, source in enumerate(refs[steps : 2 * steps + 1]):
        copies.append(pltpu.make_async_copy(source, held_ref.at[index], sems.at[index]))
    for copy in copies:
        copy.start()
    copies[0].wait()
    perm = crossing_order(me_ref[0], match_ref[...])
    diff_out[...] = from_crossing(
        lambda index: diff_ref[index * q : (index + 1) * q, :], perm, q, tiles
    )
    for copy in copies[1:]:
        copy.wait()
    residual = held_ref[0]
    for index, length_ref in enumerate(refs[:steps]):
        residual = residual - length_ref[0:1, 0:1] * held_ref[index + 1]
    residual_ref[...] = residual
    residual_out[...] = from_crossing(
        lambda index: residual_ref[index * q : (index + 1) * q, :], perm, q, tiles
    )


def finish_kernel(
    me_ref, squares_ref, direction_ref, norm_ref, knot_ref, residual_ref, diff_ref, knot_out, residual_out
):
    params = knot_out.shape[0]
    squares = squares_ref[0]
    for d in range(1, squares_ref.shape[0]):
        squares = squares + squares_ref[d]
    curvature = 0.5 * jnp.sum(squares, keepdims=True) + damping * full_dot(
        direction_ref, direction_ref
    )
    length = norm_ref[0:1, 0:1] / curvature
    knot = knot_ref[...] + length * direction_ref[me_ref[0]]
    knot_out[...] = knot[0:params]
    residual_out[...] = residual_ref[...] - length * diff_ref[...]


def call(kernel, outs, ins, scratch=(), places=None):
    return pl.pallas_call(
        kernel,
        out_shape=outs,
        in_specs=ins,
        out_specs=places or jax.tree.map(lambda _: VMEM, outs),
        scratch_shapes=list(scratch),
        compiler_params=PARAMS,
    )


def local(jac, obs, match, tile_knot, tile_frac):
    tiles, params, columns = jac.shape
    n_track = lax.axis_size("track")
    n_det = lax.axis_size("det")
    n_all = n_track * n_det
    q = tiles // n_track
    me = lax.axis_index("track").astype(jnp.int32).reshape(1)

    def crossing(values):
        return lax.all_to_all(values, "track", split_axis=0, concat_axis=0, tiled=True)

    def everywhere(values):
        return lax.all_to_all(values, ("track", "det"), split_axis=0, concat_axis=0, tiled=True)

    match_row = from_hbm(match[None])
    int_row = pltpu.VMEM((1, tiles), jnp.int32)
    sent = call(
        functools.partial(order_kernel, q),
        f32(tiles, columns),
        [SMEM, ANY, ANY],
        [int_row, pltpu.VMEM((tiles, columns), jnp.float32), pltpu.SemaphoreType.DMA((2,))],
    )(me, match_row, from_hbm(obs))
    arrived = crossing(sent)
    weight_shape = (3, KNOT_DEV + PAD, tiles)
    rows, weights = call(
        functools.partial(rows_kernel, q, math.gcd(params, 3)),
        (kept((params, tiles, columns)), pltpu.HBM(weight_shape, jnp.bfloat16)),
        [SMEM] + [ANY] * 5,
        [
            int_row,
            int_row,
            pltpu.VMEM((1, tiles), jnp.float32),
            pltpu.SemaphoreType.DMA((3 + params,)),
        ],
    )(
        me,
        match_row,
        *map(from_hbm, (tile_knot[None], tile_frac[None], sent, jnp.transpose(jac, (1, 0, 2)))),
    )

    field = f32(n_track, PAD, LANES)
    scalar = f32(SUB, LANES)
    interp = pltpu.VMEM((n_track, PAD, LANES), jnp.float32)
    adjoint_out = (pltpu.HBM((tiles, columns), jnp.float32), f32(n_all, PAD, LANES))
    values = pltpu.VMEM((PAD, tiles), jnp.float32)
    plane = pltpu.VMEM((tiles, columns), jnp.float32)
    misfit, payload, weights = call(
        functools.partial(first_adjoint_kernel, q),
        adjoint_out + (jax.ShapeDtypeStruct(weight_shape, jnp.bfloat16),),
        [SMEM, VMEM, VMEM, ANY, ANY],
        [values, plane, plane, pltpu.SemaphoreType.DMA((3,))],
        (ANY, VMEM, VMEM),
    )(me, arrived, rows, from_hbm(sent), from_hbm(weights))
    gradient, slope_norm, sent, edge = call(
        functools.partial(first_kernel, q, n_det),
        (field, scalar, f32(tiles, columns), f32(SUB, tiles)),
        [SMEM] + [VMEM] * 3,
        [interp],
    )(me, everywhere(payload), rows, weights)
    direction = gradient
    knot_field = jnp.zeros((PAD, KNOT_DEV), jnp.float32)
    lengths, changes = [], []
    for iteration in range(ITERS - 1):
        change, payload = call(
            functools.partial(adjoint_kernel, q),
            adjoint_out,
            [SMEM] + [VMEM] * 4,
            [values, plane, pltpu.SemaphoreType.DMA],
            (ANY, VMEM),
        )(me, sent, crossing(sent), rows, weights)
        gathered = everywhere(payload)
        last = iteration == ITERS - 2
        results = call(
            functools.partial(step_kernel, q, n_det),
            (field, scalar, f32(PAD, KNOT_DEV), scalar, f32(tiles, columns))
            + (() if last else (field,)),
            [SMEM] + [VMEM] * 8,
            [interp] * (3 if last else 2),
        )(
            me, gathered, rows, weights, edge, gradient, direction, slope_norm, knot_field
        )
        direction, slope_norm, knot_field, length, sent = results[:5]
        gradient = None if last else results[5]
        lengths.append(length)
        changes.append(change)
    change, squares = call(
        functools.partial(last_kernel, q),
        (f32(tiles, columns), f32(n_all, 1, LANES)),
        [SMEM] + [VMEM] * 2,
    )(me, sent, crossing(sent))
    squares = everywhere(squares)
    residual, change = call(
        functools.partial(restore_kernel, q),
        (f32(tiles, columns), f32(tiles, columns)),
        [SMEM, ANY, VMEM] + [VMEM] * len(lengths) + [ANY] * (1 + len(changes)),
        [
            plane,
            int_row,
            pltpu.VMEM((1 + len(changes), tiles, columns), jnp.float32),
            pltpu.SemaphoreType.DMA((2 + len(changes),)),
        ],
    )(me, match_row, change, *lengths, *map(from_hbm, [misfit] + changes))
    return call(
        finish_kernel,
        (f32(params, KNOT_DEV), f32(tiles, columns)),
        [SMEM] + [VMEM] * 6,
    )(me, squares, direction, slope_norm, knot_field, residual, change)


def solution(mesh):
    in_specs = (P("track", None, "det"), P("track", "det"), P("track"), P("track"), P("track"))
    out_specs = (P(None, "track"), P("track", "det"))
    return jax.shard_map(local, mesh=mesh, in_specs=in_specs, out_specs=out_specs, check_vma=False)
```

```python
import functools
import math

import jax
import jax.numpy as jnp
from jax import lax
from jax.experimental import pallas as pl
from jax.experimental.pallas import tpu as pltpu
from jax.sharding import PartitionSpec as P

KNOT_DEV = 128
ITERS = 4
LANES = 128
SUB = 8
PAD = 16
VMEM_BYTES = 6 * 2**20


damping = 1.0

SMEM = pl.BlockSpec(memory_space=pltpu.SMEM)
VMEM = pl.BlockSpec(memory_space=pltpu.VMEM)
ANY = pl.BlockSpec(memory_space=pl.ANY)
PARAMS = pltpu.CompilerParams(vmem_limit_bytes=VMEM_BYTES)
HIGHEST = lax.Precision.HIGHEST


def kept(shape, dtype=jnp.float32):
    return pltpu.VMEM(shape, dtype)


def from_hbm(x):
    return pltpu.with_memory_space_constraint(x, pltpu.HBM)


def f32(*shape):
    return jax.ShapeDtypeStruct(shape, jnp.float32)


def dot(a, b, dims):
    return lax.dot_general(
        a, b, (dims, ((), ())), precision=HIGHEST, preferred_element_type=jnp.float32
    )


def split3(x):
    first = x.astype(jnp.bfloat16)
    rest = x - first.astype(jnp.float32)
    second = rest.astype(jnp.bfloat16)
    third = (rest - second.astype(jnp.float32)).astype(jnp.bfloat16)
    return first, second, third


def bf16_dot(a, b):
    return jnp.dot(a, b, preferred_element_type=jnp.float32)


def turn(x, shift):
    shift = shift % LANES
    return x if shift == 0 else pltpu.roll(x, shift, 1)


def lane_group(shape, q):
    return lax.broadcasted_iota(jnp.int32, shape, 1) // q


def to_crossing(arrays, perm, q, store):
    tiles = arrays[0].shape[0]
    groups = LANES // q
    stacked = []
    for x in arrays:
        across = jnp.concatenate(
            [x[c * LANES : (c + 1) * LANES].T for c in range(tiles // LANES)], axis=1
        )
        stacked.extend(split3(across))
    moved = bf16_dot(jnp.concatenate(stacked, axis=0), perm)
    group = lane_group((q, LANES), q)
    for index in range(len(arrays)):
        third, second, first = (
            moved[(3 * index + part) * LANES : (3 * index + part + 1) * LANES] for part in (2, 1, 0)
        )
        whole = third + second + first
        for c in range(tiles // LANES):
            for b in range(groups):
                block = None
                for h in range(groups):
                    piece = turn(
                        whole[h * q : (h + 1) * q, c * LANES : (c + 1) * LANES], (h - b) * q
                    )
                    block = piece if block is None else jnp.where(group == h, piece, block)
                store(index, c * groups + b, block)


def from_crossing(load, perm, q, tiles):
    groups = LANES // q
    group = lane_group((q, LANES), q)
    parts = []
    for c in range(tiles // LANES):
        rows = []
        for h in range(groups):
            block = None
            for b in range(groups):
                piece = turn(load(c * groups + b), (b - h) * q)
                block = piece if block is None else jnp.where(group == b, piece, block)
            rows.append(block)
        parts.append(jnp.concatenate(rows, axis=0).T)
    stacked = jnp.concatenate(parts, axis=0)
    return sum(bf16_dot(perm, part) for part in reversed(split3(stacked)))


def crossing_order(me, match):
    tiles = match.shape[1]
    slot = lax.broadcasted_iota(jnp.int32, (1, tiles), 1)
    peer = match // tiles
    other = match - peer * tiles
    inner = jnp.where(
        peer == me,
        jnp.minimum(slot, other) + jnp.where(slot > other, tiles, 0),
        jnp.where(peer > me, slot, other),
    )
    key = (peer * (2 * tiles) + inner).astype(jnp.float32)
    key_cols = jnp.broadcast_to(key, (LANES, tiles)).T[:, :1]
    place = jnp.sum(jnp.where(key < key_cols, 1.0, 0.0), axis=1, keepdims=True)
    cols = lax.broadcasted_iota(jnp.int32, (tiles, tiles), 1).astype(jnp.float32)
    return jnp.where(place == cols, 1.0, 0.0).astype(jnp.bfloat16)


def order_kernel(q, me_ref, match_hbm, obs_hbm, obs_out, match_ref, obs_ref, sems):
    copies = [
        pltpu.make_async_copy(match_hbm, match_ref, sems.at[0]),
        pltpu.make_async_copy(obs_hbm, obs_ref, sems.at[1]),
    ]
    for copy in copies:
        copy.start()
    copies[0].wait()
    perm = crossing_order(me_ref[0], match_ref[...])
    copies[1].wait()

    def put(_, index, block):
        obs_out[index * q : (index + 1) * q, :] = block

    to_crossing([obs_ref[...]], perm, q, put)


def rows_kernel(
    q,
    together,
    me_ref,
    match_hbm,
    knot_hbm,
    frac_hbm,
    _,
    jac_hbm,
    rows_ref,
    weight_ref,
    match_ref,
    knot_ref,
    frac_ref,
    sems,
):
    params, tiles = jac_hbm.shape[:2]
    pairs = [(match_hbm, match_ref), (knot_hbm, knot_ref), (frac_hbm, frac_ref)]
    pairs += [(jac_hbm.at[p], rows_ref.at[p]) for p in range(params)]
    copies = [
        pltpu.make_async_copy(source, target, sems.at[index])
        for index, (source, target) in enumerate(pairs)
    ]
    for copy in copies:
        copy.start()
    for copy in copies[:3]:
        copy.wait()
    perm = crossing_order(me_ref[0], match_ref[...])
    row = lax.broadcasted_iota(jnp.int32, (SUB, tiles), 0)
    facts = jnp.where(row == 0, knot_ref[...].astype(jnp.float32), frac_ref[...])
    moved = sum(bf16_dot(part, perm) for part in reversed(split3(facts)))
    knot, frac = moved[0:1], moved[1:2]
    knots = lax.broadcasted_iota(jnp.int32, (KNOT_DEV, tiles), 0).astype(jnp.float32)
    main = jnp.where(knots == knot, 1.0 - frac, 0.0) + jnp.where(knots == knot + 1.0, frac, 0.0)
    first_row = lax.broadcasted_iota(jnp.int32, (PAD, tiles), 0) == 0
    edge = jnp.where(first_row, jnp.where(knot == KNOT_DEV - 1.0, frac, 0.0), 0.0)
    for index, (upper, lower) in enumerate(zip(split3(main), split3(edge))):
        weight_ref[index, 0:KNOT_DEV, :] = upper
        weight_ref[index, KNOT_DEV : KNOT_DEV + PAD, :] = lower

    for first in range(0, params, together):
        for p in range(first, first + together):
            copies[3 + p].wait()

        def put(index, block_index, block):
            rows_ref[first + index, block_index * q : (block_index + 1) * q, :] = block

        to_crossing([rows_ref[p] for p in range(first, first + together)], perm, q, put)


def weight_dot(x, parts, over_tiles):
    dims = (((1,), (1 if over_tiles else 0,)), ((), ()))
    stacked = jnp.concatenate(split3(x), axis=0)
    first, second, third = (
        lax.dot_general(
            stacked[0 : (3 - index) * PAD], part, dims, preferred_element_type=jnp.float32
        )
        for index, part in enumerate(parts)
    )
    small = third + second[PAD : 2 * PAD] + first[2 * PAD : 3 * PAD]
    return (small + (second[0:PAD] + first[PAD : 2 * PAD])) + first[0:PAD]


def row_sums(parts):
    row = lax.broadcasted_iota(jnp.int32, (SUB, LANES), 0)
    level = list(parts)
    zero = jnp.zeros((SUB, LANES), jnp.float32)
    while len(level) % SUB:
        level.append(zero)
    for distance in (1, 2, 4):
        first = (row // distance) % 2 == 0
        level = [
            jnp.where(first, a, b) + pltpu.roll(jnp.where(first, b, a), distance, 0)
            for a, b in zip(level[::2], level[1::2])
        ]
    return level[0] if len(level) == 1 else jnp.concatenate(level, axis=0)


def fold_rows(x):
    total = x[0:SUB]
    for step in range(1, x.shape[0] // SUB):
        total = total + x[step * SUB : (step + 1) * SUB]
    return total


def fold_lanes(x, q):
    shift = q
    while shift < LANES:
        x = x + pltpu.roll(x, shift, 1)
        shift *= 2
    return x


def crossing_values(me, arrived_ref, out_ref, q):
    out_ref[...] = arrived_ref[...]
    own = arrived_ref[pl.ds(pl.multiple_of(me * q, SUB), q), :]
    lane = lax.broadcasted_iota(jnp.int32, (q, LANES), 1)
    swapped = jnp.where(lane % q < q // 2, turn(own, -(q // 2)), turn(own, q // 2))
    out_ref[pl.ds(pl.multiple_of(me * q, SUB), q), :] = swapped


def difference(me, sent_ref, arrived_ref, out_ref, q):
    crossing_values(me, arrived_ref, out_ref, q)
    out_ref[...] = sent_ref[...] - out_ref[...]


def first_adjoint_kernel(
    q,
    me_ref,
    arrived_ref,
    rows_ref,
    sent_hbm,
    weight_hbm,
    diff_ref,
    send_ref,
    weight_ref,
    values_ref,
    sent_ref,
    sems,
):
    copies = [
        pltpu.make_async_copy(sent_hbm, sent_ref, sems.at[0]),
        pltpu.make_async_copy(weight_hbm, weight_ref, sems.at[1]),
    ]
    for copy in copies:
        copy.start()
    copies[0].wait()
    difference(me_ref[0], sent_ref, arrived_ref, diff_ref, q)
    adjoint_values(q, diff_ref, rows_ref, values_ref)
    copies[1].wait()
    adjoint_rows(rows_ref.shape[0], values_ref, weight_ref, send_ref)


def adjoint_kernel(
    q, me_ref, sent_ref, arrived_ref, rows_ref, weight_ref, diff_ref, send_ref, values_ref
):
    difference(me_ref[0], sent_ref, arrived_ref, diff_ref, q)
    adjoint_values(q, diff_ref, rows_ref, values_ref)
    adjoint_rows(rows_ref.shape[0], values_ref, weight_ref, send_ref)


def adjoint_values(q, diff_ref, jac_ref, values_ref):
    params, tiles, _ = jac_ref.shape
    groups = LANES // q
    group = lane_group((PAD, LANES), q)
    for c in range(tiles // LANES):
        values = None
        for i in range(groups):
            rows = slice((c * groups + i) * q, (c * groups + i + 1) * q)
            diff = diff_ref[rows, :]
            sums = fold_lanes(
                row_sums([fold_rows(jac_ref[p, rows, :] * diff) for p in range(params)]), q
            )
            values = sums if values is None else jnp.where(group == i, sums, values)
        values_ref[:, c * LANES : (c + 1) * LANES] = values


def adjoint_rows(params, values_ref, weight_ref, send_ref):
    spread = weight_dot(values_ref[...], [weight_ref[index] for index in range(3)], True)
    lane = lax.broadcasted_iota(jnp.int32, (PAD, LANES), 1)
    row = lax.broadcasted_iota(jnp.int32, (PAD, LANES), 0)
    spill = jnp.sum(
        jnp.where(lane == row, spread[:, KNOT_DEV : KNOT_DEV + 1], 0.0), axis=0, keepdims=True
    )
    block = jnp.where(row < params, spread[:, :KNOT_DEV], jnp.where(row == params, spill, 0.0))
    for d in range(send_ref.shape[0]):
        send_ref[d] = block


def field_sums(gathered_ref, n_track, n_det, params, store, base=0):
    lane = lax.broadcasted_iota(jnp.int32, (PAD, LANES), 1)
    row = lax.broadcasted_iota(jnp.int32, (PAD, LANES), 0)
    spill = jnp.zeros((PAD, 1), jnp.float32)
    for b in range(n_track):
        total = gathered_ref[b * n_det, base : base + PAD, :]
        for d in range(1, n_det):
            total = total + gathered_ref[b * n_det + d, base : base + PAD, :]
        field = jnp.where(row < params, total, 0.0)
        field = field + jnp.where(lane == 0, spill, 0.0)
        store(b, field)
        spill = jnp.sum(
            jnp.where((lane == row) & (row < params), total[params : params + 1], 0.0),
            axis=1,
            keepdims=True,
        )


def total_of(x):
    return jnp.sum(jnp.sum(x, axis=0), keepdims=True).reshape(1, 1)


def full_dot(a_ref, b_ref):
    total = a_ref[0] * b_ref[0]
    for b in range(1, a_ref.shape[0]):
        total = total + a_ref[b] * b_ref[b]
    return jnp.sum(total, keepdims=True)


def predict(me, q, direction_ref, jac_ref, parts, edge, interp_ref, sent_ref):
    params, tiles, _ = jac_ref.shape
    n_track = direction_ref.shape[0]
    following = direction_ref[jnp.minimum(me + 1, n_track - 1)][:, 0:1]
    following = jnp.where(me + 1 < n_track, following, 0.0)
    interp = weight_dot(direction_ref[me], parts, False) + following * edge
    groups = LANES // q
    group = lane_group((PAD, LANES), q)
    for c in range(tiles // LANES):
        chunk = interp[:, c * LANES : (c + 1) * LANES]
        for i in range(groups):
            wide = None
            for h in range(groups):
                piece = turn(chunk, (h - i) * q)
                wide = piece if wide is None else jnp.where(group == h, piece, wide)
            interp_ref[c * groups + i] = wide

    def block_values(b, carry):
        rows = pl.ds(pl.multiple_of(b * q, SUB), q)
        interp = interp_ref[b]
        total = jac_ref[0, rows, :] * interp[0:1]
        for p in range(1, params):
            total = total + jac_ref[p, rows, :] * interp[p : p + 1]
        sent_ref[rows, :] = total
        return carry

    lax.fori_loop(0, tiles // q, block_values, 0)


def first_kernel(
    q,
    n_det,
    me_ref,
    gathered_ref,
    rows_ref,
    weight_ref,
    grad_ref,
    norm_ref,
    sent_ref,
    edge_ref,
    interp_ref,
):
    n_track = grad_ref.shape[0]

    def put(b, field):
        grad_ref[b] = field

    field_sums(gathered_ref, n_track, n_det, rows_ref.shape[0], put)
    norm_ref[...] = jnp.broadcast_to(full_dot(grad_ref, grad_ref), norm_ref.shape)
    edge = sum(
        weight_ref[index, KNOT_DEV : KNOT_DEV + PAD, :].astype(jnp.float32) for index in (2, 1, 0)
    )[0:SUB]
    edge_ref[...] = edge
    parts = [weight_ref[index, 0:KNOT_DEV, :] for index in range(3)]
    predict(me_ref[0], q, grad_ref, rows_ref, parts, edge[0:1], interp_ref, sent_ref)


def step_kernel(
    q,
    n_det,
    me_ref,
    gathered_ref,
    rows_ref,
    weight_ref,
    edge_ref,
    grad_ref,
    direction_ref,
    norm_ref,
    knot_ref,
    residual_ref,
    diff_ref,
    direction_out,
    norm_out,
    knot_out,
    residual_out,
    sent_ref,
    grad_out,
    image_ref,
    interp_ref,
):
    n_track = grad_ref.shape[0]
    me = me_ref[0]

    def put(b, field):
        image_ref[b] = field + damping * direction_ref[b]

    field_sums(gathered_ref, n_track, n_det, rows_ref.shape[0], put)
    norm = norm_ref[0:1, 0:1]
    length = norm / full_dot(direction_ref, image_ref)
    residual_out[...] = residual_ref[...] - length * diff_ref[...]
    knot_out[...] = knot_ref[...] + length * direction_ref[me]
    for b in range(n_track):
        grad_out[b] = grad_ref[b] - length * image_ref[b]
    new_norm = full_dot(grad_out, grad_out)
    norm_out[...] = jnp.broadcast_to(new_norm, norm_out.shape)
    ratio = new_norm / norm
    for b in range(n_track):
        direction_out[b] = grad_out[b] + ratio * direction_ref[b]
    parts = [weight_ref[index, 0:KNOT_DEV, :] for index in range(3)]
    predict(me, q, direction_out, rows_ref, parts, edge_ref[0:1, :], interp_ref, sent_ref)


def last_kernel(q, me_ref, sent_ref, arrived_ref, diff_ref, send_ref):
    difference(me_ref[0], sent_ref, arrived_ref, diff_ref, q)
    diff = diff_ref[...]
    squares = jnp.sum(diff * diff, axis=0, keepdims=True)
    send_ref[...] = jnp.broadcast_to(squares[None], send_ref.shape)


def restore_kernel(
    q, me_ref, match_hbm, residual_ref, diff_ref, residual_out, diff_out, match_ref, sem
):
    tiles = residual_ref.shape[0]
    copy = pltpu.make_async_copy(match_hbm, match_ref, sem)
    copy.start()
    copy.wait()
    perm = crossing_order(me_ref[0], match_ref[...])
    for source, target in ((residual_ref, residual_out), (diff_ref, diff_out)):
        target[...] = from_crossing(
            lambda index: source[index * q : (index + 1) * q, :], perm, q, tiles
        )


def finish_kernel(
    me_ref, squares_ref, direction_ref, norm_ref, knot_ref, residual_ref, diff_ref, knot_out, residual_out
):
    params = knot_out.shape[0]
    squares = squares_ref[0]
    for d in range(1, squares_ref.shape[0]):
        squares = squares + squares_ref[d]
    curvature = 0.5 * jnp.sum(squares, keepdims=True) + damping * full_dot(
        direction_ref, direction_ref
    )
    length = norm_ref[0:1, 0:1] / curvature
    knot = knot_ref[...] + length * direction_ref[me_ref[0]]
    knot_out[...] = knot[0:params]
    residual_out[...] = residual_ref[...] - length * diff_ref[...]


def call(kernel, outs, ins, scratch=()):
    return pl.pallas_call(
        kernel,
        out_shape=outs,
        in_specs=ins,
        out_specs=jax.tree.map(lambda _: VMEM, outs),
        scratch_shapes=list(scratch),
        compiler_params=PARAMS,
    )


def local(jac, obs, match, tile_knot, tile_frac):
    tiles, params, columns = jac.shape
    n_track = lax.axis_size("track")
    n_det = lax.axis_size("det")
    n_all = n_track * n_det
    q = tiles // n_track
    me = lax.axis_index("track").astype(jnp.int32).reshape(1)

    def crossing(values):
        return lax.all_to_all(values, "track", split_axis=0, concat_axis=0, tiled=True)

    def everywhere(values):
        return lax.all_to_all(values, ("track", "det"), split_axis=0, concat_axis=0, tiled=True)

    match_row = from_hbm(match[None])
    int_row = pltpu.VMEM((1, tiles), jnp.int32)
    sent = call(
        functools.partial(order_kernel, q),
        f32(tiles, columns),
        [SMEM, ANY, ANY],
        [int_row, pltpu.VMEM((tiles, columns), jnp.float32), pltpu.SemaphoreType.DMA((2,))],
    )(me, match_row, from_hbm(obs))
    arrived = crossing(sent)
    weight_shape = (3, KNOT_DEV + PAD, tiles)
    rows, weights = call(
        functools.partial(rows_kernel, q, math.gcd(params, 3)),
        (kept((params, tiles, columns)), pltpu.HBM(weight_shape, jnp.bfloat16)),
        [SMEM] + [ANY] * 5,
        [
            int_row,
            int_row,
            pltpu.VMEM((1, tiles), jnp.float32),
            pltpu.SemaphoreType.DMA((3 + params,)),
        ],
    )(
        me,
        match_row,
        *map(from_hbm, (tile_knot[None], tile_frac[None], sent, jnp.transpose(jac, (1, 0, 2)))),
    )

    field = f32(n_track, PAD, LANES)
    scalar = f32(SUB, LANES)
    interp = pltpu.VMEM((n_track, PAD, LANES), jnp.float32)
    adjoint_out = (f32(tiles, columns), f32(n_all, PAD, LANES))
    values = pltpu.VMEM((PAD, tiles), jnp.float32)
    residual, payload, weights = call(
        functools.partial(first_adjoint_kernel, q),
        adjoint_out + (jax.ShapeDtypeStruct(weight_shape, jnp.bfloat16),),
        [SMEM, VMEM, VMEM, ANY, ANY],
        [values, pltpu.VMEM((tiles, columns), jnp.float32), pltpu.SemaphoreType.DMA((2,))],
    )(me, arrived, rows, from_hbm(sent), from_hbm(weights))
    gradient, slope_norm, sent, edge = call(
        functools.partial(first_kernel, q, n_det),
        (field, scalar, f32(tiles, columns), f32(SUB, tiles)),
        [SMEM] + [VMEM] * 3,
        [interp],
    )(me, everywhere(payload), rows, weights)
    direction = gradient
    knot_field = jnp.zeros((PAD, KNOT_DEV), jnp.float32)
    for iteration in range(ITERS - 1):
        change, payload = call(
            functools.partial(adjoint_kernel, q), adjoint_out, [SMEM] + [VMEM] * 4, [values]
        )(me, sent, crossing(sent), rows, weights)
        gathered = everywhere(payload)
        last = iteration == ITERS - 2
        results = call(
            functools.partial(step_kernel, q, n_det),
            (field, scalar, f32(PAD, KNOT_DEV), f32(tiles, columns), f32(tiles, columns))
            + (() if last else (field,)),
            [SMEM] + [VMEM] * 10,
            [interp] * (3 if last else 2),
        )(
            me,
            gathered,
            rows,
            weights,
            edge,
            gradient,
            direction,
            slope_norm,
            knot_field,
            residual,
            change,
        )
        direction, slope_norm, knot_field, residual, sent = results[:5]
        gradient = None if last else results[5]
    change, squares = call(
        functools.partial(last_kernel, q),
        (f32(tiles, columns), f32(n_all, 1, LANES)),
        [SMEM] + [VMEM] * 2,
    )(me, sent, crossing(sent))
    squares = everywhere(squares)
    residual, change = call(
        functools.partial(restore_kernel, q),
        (f32(tiles, columns), f32(tiles, columns)),
        [SMEM, ANY, VMEM, VMEM],
        [int_row, pltpu.SemaphoreType.DMA],
    )(me, match_row, residual, change)
    return call(
        finish_kernel,
        (f32(params, KNOT_DEV), f32(tiles, columns)),
        [SMEM] + [VMEM] * 6,
    )(me, squares, direction, slope_norm, knot_field, residual, change)


def solution(mesh):
    in_specs = (P("track", None, "det"), P("track", "det"), P("track"), P("track"), P("track"))
    out_specs = (P(None, "track"), P("track", "det"))
    return jax.shard_map(local, mesh=mesh, in_specs=in_specs, out_specs=out_specs, check_vma=False)
```

```python
import functools
import math

import jax
import jax.numpy as jnp
from jax import lax
from jax.experimental import pallas as pl
from jax.experimental.pallas import tpu as pltpu
from jax.sharding import PartitionSpec as P

KNOT_DEV = 128
ITERS = 4
LANES = 128
SUB = 8
PAD = 16
VMEM_BYTES = 6 * 2**20


damping = 1.0

SMEM = pl.BlockSpec(memory_space=pltpu.SMEM)
VMEM = pl.BlockSpec(memory_space=pltpu.VMEM)
ANY = pl.BlockSpec(memory_space=pl.ANY)
PARAMS = pltpu.CompilerParams(vmem_limit_bytes=VMEM_BYTES)
HIGHEST = lax.Precision.HIGHEST


def kept(shape, dtype=jnp.float32):
    return pltpu.VMEM(shape, dtype)


def from_hbm(x):
    return pltpu.with_memory_space_constraint(x, pltpu.HBM)


def f32(*shape):
    return jax.ShapeDtypeStruct(shape, jnp.float32)


def dot(a, b, dims):
    return lax.dot_general(
        a, b, (dims, ((), ())), precision=HIGHEST, preferred_element_type=jnp.float32
    )


def split3(x):
    first = x.astype(jnp.bfloat16)
    rest = x - first.astype(jnp.float32)
    second = rest.astype(jnp.bfloat16)
    third = (rest - second.astype(jnp.float32)).astype(jnp.bfloat16)
    return first, second, third


def bf16_dot(a, b):
    return jnp.dot(a, b, preferred_element_type=jnp.float32)


def turn(x, shift):
    shift = shift % LANES
    return x if shift == 0 else pltpu.roll(x, shift, 1)


def lane_group(shape, q):
    return lax.broadcasted_iota(jnp.int32, shape, 1) // q


def to_crossing(arrays, perm, q, store):
    tiles = arrays[0].shape[0]
    groups = LANES // q
    stacked = []
    for x in arrays:
        across = jnp.concatenate(
            [x[c * LANES : (c + 1) * LANES].T for c in range(tiles // LANES)], axis=1
        )
        stacked.extend(split3(across))
    moved = bf16_dot(jnp.concatenate(stacked, axis=0), perm)
    group = lane_group((q, LANES), q)
    for index in range(len(arrays)):
        third, second, first = (
            moved[(3 * index + part) * LANES : (3 * index + part + 1) * LANES] for part in (2, 1, 0)
        )
        whole = third + second + first
        for c in range(tiles // LANES):
            for b in range(groups):
                block = None
                for h in range(groups):
                    piece = turn(
                        whole[h * q : (h + 1) * q, c * LANES : (c + 1) * LANES], (h - b) * q
                    )
                    block = piece if block is None else jnp.where(group == h, piece, block)
                store(index, c * groups + b, block)


def from_crossing(load, perm, q, tiles):
    groups = LANES // q
    group = lane_group((q, LANES), q)
    parts = []
    for c in range(tiles // LANES):
        rows = []
        for h in range(groups):
            block = None
            for b in range(groups):
                piece = turn(load(c * groups + b), (b - h) * q)
                block = piece if block is None else jnp.where(group == b, piece, block)
            rows.append(block)
        parts.append(jnp.concatenate(rows, axis=0).T)
    stacked = jnp.concatenate(parts, axis=0)
    return sum(bf16_dot(perm, part) for part in reversed(split3(stacked)))


def crossing_order(me, match):
    tiles = match.shape[1]
    slot = lax.broadcasted_iota(jnp.int32, (1, tiles), 1)
    peer = match // tiles
    other = match - peer * tiles
    inner = jnp.where(
        peer == me,
        jnp.minimum(slot, other) + jnp.where(slot > other, tiles, 0),
        jnp.where(peer > me, slot, other),
    )
    key = (peer * (2 * tiles) + inner).astype(jnp.float32)
    key_cols = jnp.broadcast_to(key, (LANES, tiles)).T[:, :1]
    place = jnp.sum(jnp.where(key < key_cols, 1.0, 0.0), axis=1, keepdims=True)
    cols = lax.broadcasted_iota(jnp.int32, (tiles, tiles), 1).astype(jnp.float32)
    return jnp.where(place == cols, 1.0, 0.0).astype(jnp.bfloat16)


def order_kernel(q, me_ref, match_hbm, obs_hbm, obs_out, match_ref, obs_ref, sems):
    copies = [
        pltpu.make_async_copy(match_hbm, match_ref, sems.at[0]),
        pltpu.make_async_copy(obs_hbm, obs_ref, sems.at[1]),
    ]
    for copy in copies:
        copy.start()
    copies[0].wait()
    perm = crossing_order(me_ref[0], match_ref[...])
    copies[1].wait()

    def put(_, index, block):
        obs_out[index * q : (index + 1) * q, :] = block

    to_crossing([obs_ref[...]], perm, q, put)


def rows_kernel(
    q,
    together,
    me_ref,
    match_hbm,
    knot_hbm,
    frac_hbm,
    sent_hbm,
    jac_hbm,
    rows_ref,
    weight_ref,
    values_ref,
    match_ref,
    knot_ref,
    frac_ref,
    sent_ref,
    sems,
):
    params, tiles = jac_hbm.shape[:2]
    pairs = [(match_hbm, match_ref), (knot_hbm, knot_ref), (frac_hbm, frac_ref)]
    pairs += [(jac_hbm.at[p], rows_ref.at[p]) for p in range(params)]
    pairs += [(sent_hbm, sent_ref)]
    copies = [
        pltpu.make_async_copy(source, target, sems.at[index])
        for index, (source, target) in enumerate(pairs)
    ]
    for copy in copies:
        copy.start()
    for copy in copies[:3]:
        copy.wait()
    perm = crossing_order(me_ref[0], match_ref[...])
    row = lax.broadcasted_iota(jnp.int32, (SUB, tiles), 0)
    facts = jnp.where(row == 0, knot_ref[...].astype(jnp.float32), frac_ref[...])
    moved = sum(bf16_dot(part, perm) for part in reversed(split3(facts)))
    knot, frac = moved[0:1], moved[1:2]
    knots = lax.broadcasted_iota(jnp.int32, (KNOT_DEV, tiles), 0).astype(jnp.float32)
    main = jnp.where(knots == knot, 1.0 - frac, 0.0) + jnp.where(knots == knot + 1.0, frac, 0.0)
    first_row = lax.broadcasted_iota(jnp.int32, (PAD, tiles), 0) == 0
    edge = jnp.where(first_row, jnp.where(knot == KNOT_DEV - 1.0, frac, 0.0), 0.0)
    for index, (upper, lower) in enumerate(zip(split3(main), split3(edge))):
        weight_ref[index, 0:KNOT_DEV, :] = upper
        weight_ref[index, KNOT_DEV : KNOT_DEV + PAD, :] = lower

    for first in range(0, params, together):
        for p in range(first, first + together):
            copies[3 + p].wait()

        def put(index, block_index, block):
            rows_ref[first + index, block_index * q : (block_index + 1) * q, :] = block

        to_crossing([rows_ref[p] for p in range(first, first + together)], perm, q, put)
    copies[3 + params].wait()
    adjoint_values(q, sent_ref, rows_ref, values_ref)


def weight_dot(x, parts, over_tiles):
    dims = (((1,), (1 if over_tiles else 0,)), ((), ()))
    stacked = jnp.concatenate(split3(x), axis=0)
    first, second, third = (
        lax.dot_general(
            stacked[0 : (3 - index) * PAD], part, dims, preferred_element_type=jnp.float32
        )
        for index, part in enumerate(parts)
    )
    small = third + second[PAD : 2 * PAD] + first[2 * PAD : 3 * PAD]
    return (small + (second[0:PAD] + first[PAD : 2 * PAD])) + first[0:PAD]


def row_sums(parts):
    row = lax.broadcasted_iota(jnp.int32, (SUB, LANES), 0)
    level = list(parts)
    zero = jnp.zeros((SUB, LANES), jnp.float32)
    while len(level) % SUB:
        level.append(zero)
    for distance in (1, 2, 4):
        first = (row // distance) % 2 == 0
        level = [
            jnp.where(first, a, b) + pltpu.roll(jnp.where(first, b, a), distance, 0)
            for a, b in zip(level[::2], level[1::2])
        ]
    return level[0] if len(level) == 1 else jnp.concatenate(level, axis=0)


def fold_rows(x):
    total = x[0:SUB]
    for step in range(1, x.shape[0] // SUB):
        total = total + x[step * SUB : (step + 1) * SUB]
    return total


def fold_lanes(x, q):
    shift = q
    while shift < LANES:
        x = x + pltpu.roll(x, shift, 1)
        shift *= 2
    return x


def crossing_values(me, arrived_ref, out_ref, q):
    out_ref[...] = arrived_ref[...]
    own = arrived_ref[pl.ds(pl.multiple_of(me * q, SUB), q), :]
    lane = lax.broadcasted_iota(jnp.int32, (q, LANES), 1)
    swapped = jnp.where(lane % q < q // 2, turn(own, -(q // 2)), turn(own, q // 2))
    out_ref[pl.ds(pl.multiple_of(me * q, SUB), q), :] = swapped


def difference(me, sent_ref, arrived_ref, out_ref, q):
    crossing_values(me, arrived_ref, out_ref, q)
    out_ref[...] = sent_ref[...] - out_ref[...]


def first_adjoint_kernel(
    q,
    me_ref,
    arrived_ref,
    rows_ref,
    own_hbm,
    sent_hbm,
    weight_hbm,
    diff_ref,
    send_ref,
    weight_ref,
    values_ref,
    own_ref,
    sent_ref,
    sems,
):
    copies = [
        pltpu.make_async_copy(own_hbm, own_ref, sems.at[0]),
        pltpu.make_async_copy(weight_hbm, weight_ref, sems.at[1]),
        pltpu.make_async_copy(sent_hbm, sent_ref, sems.at[2]),
    ]
    for copy in copies:
        copy.start()
    crossing_values(me_ref[0], arrived_ref, diff_ref, q)
    adjoint_values(q, diff_ref, rows_ref, values_ref)
    copies[0].wait()
    values_ref[...] = own_ref[...] - values_ref[...]
    copies[1].wait()
    adjoint_rows(rows_ref.shape[0], values_ref, weight_ref, send_ref)
    copies[2].wait()
    diff_ref[...] = sent_ref[...] - diff_ref[...]


def adjoint_kernel(
    q, me_ref, sent_ref, arrived_ref, rows_ref, weight_ref, diff_ref, send_ref, values_ref
):
    difference(me_ref[0], sent_ref, arrived_ref, diff_ref, q)
    adjoint_values(q, diff_ref, rows_ref, values_ref)
    adjoint_rows(rows_ref.shape[0], values_ref, weight_ref, send_ref)


def adjoint_values(q, diff_ref, jac_ref, values_ref):
    params, tiles, _ = jac_ref.shape
    groups = LANES // q
    group = lane_group((PAD, LANES), q)
    for c in range(tiles // LANES):
        values = None
        for i in range(groups):
            rows = slice((c * groups + i) * q, (c * groups + i + 1) * q)
            diff = diff_ref[rows, :]
            sums = fold_lanes(
                row_sums([fold_rows(jac_ref[p, rows, :] * diff) for p in range(params)]), q
            )
            values = sums if values is None else jnp.where(group == i, sums, values)
        values_ref[:, c * LANES : (c + 1) * LANES] = values


def adjoint_rows(params, values_ref, weight_ref, send_ref):
    spread = weight_dot(values_ref[...], [weight_ref[index] for index in range(3)], True)
    lane = lax.broadcasted_iota(jnp.int32, (PAD, LANES), 1)
    row = lax.broadcasted_iota(jnp.int32, (PAD, LANES), 0)
    spill = jnp.sum(
        jnp.where(lane == row, spread[:, KNOT_DEV : KNOT_DEV + 1], 0.0), axis=0, keepdims=True
    )
    block = jnp.where(row < params, spread[:, :KNOT_DEV], jnp.where(row == params, spill, 0.0))
    for d in range(send_ref.shape[0]):
        send_ref[d] = block


def field_sums(gathered_ref, n_track, n_det, params, store, base=0):
    lane = lax.broadcasted_iota(jnp.int32, (PAD, LANES), 1)
    row = lax.broadcasted_iota(jnp.int32, (PAD, LANES), 0)
    spill = jnp.zeros((PAD, 1), jnp.float32)
    for b in range(n_track):
        total = gathered_ref[b * n_det, base : base + PAD, :]
        for d in range(1, n_det):
            total = total + gathered_ref[b * n_det + d, base : base + PAD, :]
        field = jnp.where(row < params, total, 0.0)
        field = field + jnp.where(lane == 0, spill, 0.0)
        store(b, field)
        spill = jnp.sum(
            jnp.where((lane == row) & (row < params), total[params : params + 1], 0.0),
            axis=1,
            keepdims=True,
        )


def total_of(x):
    return jnp.sum(jnp.sum(x, axis=0), keepdims=True).reshape(1, 1)


def full_dot(a_ref, b_ref):
    total = a_ref[0] * b_ref[0]
    for b in range(1, a_ref.shape[0]):
        total = total + a_ref[b] * b_ref[b]
    return jnp.sum(total, keepdims=True)


def predict(me, q, direction_ref, jac_ref, parts, edge, interp_ref, sent_ref):
    params, tiles, _ = jac_ref.shape
    n_track = direction_ref.shape[0]
    following = direction_ref[jnp.minimum(me + 1, n_track - 1)][:, 0:1]
    following = jnp.where(me + 1 < n_track, following, 0.0)
    interp = weight_dot(direction_ref[me], parts, False) + following * edge
    groups = LANES // q
    group = lane_group((PAD, LANES), q)
    for c in range(tiles // LANES):
        chunk = interp[:, c * LANES : (c + 1) * LANES]
        for i in range(groups):
            wide = None
            for h in range(groups):
                piece = turn(chunk, (h - i) * q)
                wide = piece if wide is None else jnp.where(group == h, piece, wide)
            interp_ref[c * groups + i] = wide

    def block_values(b, carry):
        rows = pl.ds(pl.multiple_of(b * q, SUB), q)
        interp = interp_ref[b]
        total = jac_ref[0, rows, :] * interp[0:1]
        for p in range(1, params):
            total = total + jac_ref[p, rows, :] * interp[p : p + 1]
        sent_ref[rows, :] = total
        return carry

    lax.fori_loop(0, tiles // q, block_values, 0)


def first_kernel(
    q,
    n_det,
    me_ref,
    gathered_ref,
    rows_ref,
    weight_ref,
    grad_ref,
    norm_ref,
    sent_ref,
    edge_ref,
    interp_ref,
):
    n_track = grad_ref.shape[0]

    def put(b, field):
        grad_ref[b] = field

    field_sums(gathered_ref, n_track, n_det, rows_ref.shape[0], put)
    norm_ref[...] = jnp.broadcast_to(full_dot(grad_ref, grad_ref), norm_ref.shape)
    edge = sum(
        weight_ref[index, KNOT_DEV : KNOT_DEV + PAD, :].astype(jnp.float32) for index in (2, 1, 0)
    )[0:SUB]
    edge_ref[...] = edge
    parts = [weight_ref[index, 0:KNOT_DEV, :] for index in range(3)]
    predict(me_ref[0], q, grad_ref, rows_ref, parts, edge[0:1], interp_ref, sent_ref)


def step_kernel(
    q,
    n_det,
    me_ref,
    gathered_ref,
    rows_ref,
    weight_ref,
    edge_ref,
    grad_ref,
    direction_ref,
    norm_ref,
    knot_ref,
    residual_ref,
    diff_ref,
    direction_out,
    norm_out,
    knot_out,
    residual_out,
    sent_ref,
    grad_out,
    image_ref,
    interp_ref,
):
    n_track = grad_ref.shape[0]
    me = me_ref[0]

    def put(b, field):
        image_ref[b] = field + damping * direction_ref[b]

    field_sums(gathered_ref, n_track, n_det, rows_ref.shape[0], put)
    norm = norm_ref[0:1, 0:1]
    length = norm / full_dot(direction_ref, image_ref)
    residual_out[...] = residual_ref[...] - length * diff_ref[...]
    knot_out[...] = knot_ref[...] + length * direction_ref[me]
    for b in range(n_track):
        grad_out[b] = grad_ref[b] - length * image_ref[b]
    new_norm = full_dot(grad_out, grad_out)
    norm_out[...] = jnp.broadcast_to(new_norm, norm_out.shape)
    ratio = new_norm / norm
    for b in range(n_track):
        direction_out[b] = grad_out[b] + ratio * direction_ref[b]
    parts = [weight_ref[index, 0:KNOT_DEV, :] for index in range(3)]
    predict(me, q, direction_out, rows_ref, parts, edge_ref[0:1, :], interp_ref, sent_ref)


def last_kernel(q, me_ref, sent_ref, arrived_ref, diff_ref, send_ref):
    difference(me_ref[0], sent_ref, arrived_ref, diff_ref, q)
    diff = diff_ref[...]
    squares = jnp.sum(diff * diff, axis=0, keepdims=True)
    send_ref[...] = jnp.broadcast_to(squares[None], send_ref.shape)


def restore_kernel(
    q, me_ref, match_hbm, residual_ref, diff_ref, residual_out, diff_out, match_ref, sem
):
    tiles = residual_ref.shape[0]
    copy = pltpu.make_async_copy(match_hbm, match_ref, sem)
    copy.start()
    copy.wait()
    perm = crossing_order(me_ref[0], match_ref[...])
    for source, target in ((residual_ref, residual_out), (diff_ref, diff_out)):
        target[...] = from_crossing(
            lambda index: source[index * q : (index + 1) * q, :], perm, q, tiles
        )


def finish_kernel(
    me_ref, squares_ref, direction_ref, norm_ref, knot_ref, residual_ref, diff_ref, knot_out, residual_out
):
    params = knot_out.shape[0]
    squares = squares_ref[0]
    for d in range(1, squares_ref.shape[0]):
        squares = squares + squares_ref[d]
    curvature = 0.5 * jnp.sum(squares, keepdims=True) + damping * full_dot(
        direction_ref, direction_ref
    )
    length = norm_ref[0:1, 0:1] / curvature
    knot = knot_ref[...] + length * direction_ref[me_ref[0]]
    knot_out[...] = knot[0:params]
    residual_out[...] = residual_ref[...] - length * diff_ref[...]


def call(kernel, outs, ins, scratch=()):
    return pl.pallas_call(
        kernel,
        out_shape=outs,
        in_specs=ins,
        out_specs=jax.tree.map(lambda _: VMEM, outs),
        scratch_shapes=list(scratch),
        compiler_params=PARAMS,
    )


def local(jac, obs, match, tile_knot, tile_frac):
    tiles, params, columns = jac.shape
    n_track = lax.axis_size("track")
    n_det = lax.axis_size("det")
    n_all = n_track * n_det
    q = tiles // n_track
    me = lax.axis_index("track").astype(jnp.int32).reshape(1)

    def crossing(values):
        return lax.all_to_all(values, "track", split_axis=0, concat_axis=0, tiled=True)

    def everywhere(values):
        return lax.all_to_all(values, ("track", "det"), split_axis=0, concat_axis=0, tiled=True)

    match_row = from_hbm(match[None])
    int_row = pltpu.VMEM((1, tiles), jnp.int32)
    sent = call(
        functools.partial(order_kernel, q),
        f32(tiles, columns),
        [SMEM, ANY, ANY],
        [int_row, pltpu.VMEM((tiles, columns), jnp.float32), pltpu.SemaphoreType.DMA((2,))],
    )(me, match_row, from_hbm(obs))
    arrived = crossing(sent)
    weight_shape = (3, KNOT_DEV + PAD, tiles)
    rows, weights, own = call(
        functools.partial(rows_kernel, q, math.gcd(params, 3)),
        (
            kept((params, tiles, columns)),
            pltpu.HBM(weight_shape, jnp.bfloat16),
            pltpu.HBM((PAD, tiles), jnp.float32),
        ),
        [SMEM] + [ANY] * 5,
        [
            int_row,
            int_row,
            pltpu.VMEM((1, tiles), jnp.float32),
            pltpu.VMEM((tiles, columns), jnp.float32),
            pltpu.SemaphoreType.DMA((4 + params,)),
        ],
    )(
        me,
        match_row,
        *map(from_hbm, (tile_knot[None], tile_frac[None], sent, jnp.transpose(jac, (1, 0, 2)))),
    )

    field = f32(n_track, PAD, LANES)
    scalar = f32(SUB, LANES)
    interp = pltpu.VMEM((n_track, PAD, LANES), jnp.float32)
    adjoint_out = (f32(tiles, columns), f32(n_all, PAD, LANES))
    values = pltpu.VMEM((PAD, tiles), jnp.float32)
    residual, payload, weights = call(
        functools.partial(first_adjoint_kernel, q),
        adjoint_out + (jax.ShapeDtypeStruct(weight_shape, jnp.bfloat16),),
        [SMEM, VMEM, VMEM, ANY, ANY, ANY],
        [values, values, pltpu.VMEM((tiles, columns), jnp.float32), pltpu.SemaphoreType.DMA((3,))],
    )(me, arrived, rows, *map(from_hbm, (own, sent, weights)))
    gradient, slope_norm, sent, edge = call(
        functools.partial(first_kernel, q, n_det),
        (field, scalar, f32(tiles, columns), f32(SUB, tiles)),
        [SMEM] + [VMEM] * 3,
        [interp],
    )(me, everywhere(payload), rows, weights)
    direction = gradient
    knot_field = jnp.zeros((PAD, KNOT_DEV), jnp.float32)
    for iteration in range(ITERS - 1):
        change, payload = call(
            functools.partial(adjoint_kernel, q), adjoint_out, [SMEM] + [VMEM] * 4, [values]
        )(me, sent, crossing(sent), rows, weights)
        gathered = everywhere(payload)
        last = iteration == ITERS - 2
        results = call(
            functools.partial(step_kernel, q, n_det),
            (field, scalar, f32(PAD, KNOT_DEV), f32(tiles, columns), f32(tiles, columns))
            + (() if last else (field,)),
            [SMEM] + [VMEM] * 10,
            [interp] * (3 if last else 2),
        )(
            me,
            gathered,
            rows,
            weights,
            edge,
            gradient,
            direction,
            slope_norm,
            knot_field,
            residual,
            change,
        )
        direction, slope_norm, knot_field, residual, sent = results[:5]
        gradient = None if last else results[5]
    change, squares = call(
        functools.partial(last_kernel, q),
        (f32(tiles, columns), f32(n_all, 1, LANES)),
        [SMEM] + [VMEM] * 2,
    )(me, sent, crossing(sent))
    squares = everywhere(squares)
    residual, change = call(
        functools.partial(restore_kernel, q),
        (f32(tiles, columns), f32(tiles, columns)),
        [SMEM, ANY, VMEM, VMEM],
        [int_row, pltpu.SemaphoreType.DMA],
    )(me, match_row, residual, change)
    return call(
        finish_kernel,
        (f32(params, KNOT_DEV), f32(tiles, columns)),
        [SMEM] + [VMEM] * 6,
    )(me, squares, direction, slope_norm, knot_field, residual, change)


def solution(mesh):
    in_specs = (P("track", None, "det"), P("track", "det"), P("track"), P("track"), P("track"))
    out_specs = (P(None, "track"), P("track", "det"))
    return jax.shard_map(local, mesh=mesh, in_specs=in_specs, out_specs=out_specs, check_vma=False)
```
